32 devices in a mesh: dp: 4 (over z), fsdp: 8 (over y, x, core).
Axes of the slice: x: 2, y: 2, z: 4, core: 2. Of those that a mesh axis runs over, the one named last changes fastest.
Arguments:
- tokens: bfloat16 [4096, 2048], P(('dp', 'fsdp')), may hold values from -6 to 6
- out_grad: bfloat16 [4096, 2048], P(('dp', 'fsdp')), may hold values from -6 to 6
- seq_lengths: int32 [4, 3], P('dp'), may hold values from 1 to 896, as said below
- query_weight: float32 [2048, 2048], P(('dp', 'fsdp')), may hold values from -0.125 to 0.125
- query_first: float32 [2048, 2048], P(('dp', 'fsdp')), may hold values from -384 to 384
- query_second: float32 [2048, 2048], P(('dp', 'fsdp')), may hold values from 2048 to 32768
- key_weight: float32 [2048, 256], P(('dp', 'fsdp')), may hold values from -0.125 to 0.125
- key_first: float32 [2048, 256], P(('dp', 'fsdp')), may hold values from -1024 to 1024
- key_second: float32 [2048, 256], P(('dp', 'fsdp')), may hold values from 18432 to 294912
- value_weight: float32 [2048, 256], P(('dp', 'fsdp')), may hold values from -0.125 to 0.125
- value_first: float32 [2048, 256], P(('dp', 'fsdp')), may hold values from -1024 to 1024
- value_second: float32 [2048, 256], P(('dp', 'fsdp')), may hold values from 18432 to 294912
- output_weight: float32 [2048, 2048], P(('dp', 'fsdp')), may hold values from -1.5 to 1.5
- output_first: float32 [2048, 2048], P(('dp', 'fsdp')), may hold values from -32 to 32
- output_second: float32 [2048, 2048], P(('dp', 'fsdp')), may hold values from 18 to 292
- gate_weight: float32 [2048, 5632], P(('dp', 'fsdp')), may hold values from -0.125 to 0.125
- gate_first: float32 [2048, 5632], P(('dp', 'fsdp')), may hold values from -224 to 224
- gate_second: float32 [2048, 5632], P(('dp', 'fsdp')), may hold values from 737.28 to 11796.48
- up_weight: float32 [2048, 5632], P(('dp', 'fsdp')), may hold values from -0.125 to 0.125
- up_first: float32 [2048, 5632], P(('dp', 'fsdp')), may hold values from -224 to 224
- up_second: float32 [2048, 5632], P(('dp', 'fsdp')), may hold values from 737.28 to 11796.48
- down_weight: float32 [5632, 2048], P(('dp', 'fsdp')), may hold values from -0.078125 to 0.078125
- down_first: float32 [5632, 2048], P(('dp', 'fsdp')), may hold values from -224 to 224
- down_second: float32 [5632, 2048], P(('dp', 'fsdp')), may hold values from 737.28 to 11796.48
- norm_gains: float32 [2, 2048], P(None, ('dp', 'fsdp')), may hold values from 0.5 to 1.5
- gains_first: float32 [2, 2048], P(None, ('dp', 'fsdp')), may hold values from -512 to 512
- gains_second: float32 [2, 2048], P(None, ('dp', 'fsdp')), may hold values from 4608 to 73728
Outputs:
- result: bfloat16 [4096, 2048], P(('dp', 'fsdp'))
- grad_tokens: float32 [4096, 2048], P(('dp', 'fsdp'))
- query_weight_next: float32 [2048, 2048], P(('dp', 'fsdp'))
- query_first_next: float32 [2048, 2048], P(('dp', 'fsdp'))
- query_second_next: float32 [2048, 2048], P(('dp', 'fsdp'))
- key_weight_next: float32 [2048, 256], P(('dp', 'fsdp'))
- key_first_next: float32 [2048, 256], P(('dp', 'fsdp'))
- key_second_next: float32 [2048, 256], P(('dp', 'fsdp'))
- value_weight_next: float32 [2048, 256], P(('dp', 'fsdp'))
- value_first_next: float32 [2048, 256], P(('dp', 'fsdp'))
- value_second_next: float32 [2048, 256], P(('dp', 'fsdp'))
- output_weight_next: float32 [2048, 2048], P(('dp', 'fsdp'))
- output_first_next: float32 [2048, 2048], P(('dp', 'fsdp'))
- output_second_next: float32 [2048, 2048], P(('dp', 'fsdp'))
- gate_weight_next: float32 [2048, 5632], P(('dp', 'fsdp'))
- gate_first_next: float32 [2048, 5632], P(('dp', 'fsdp'))
- gate_second_next: float32 [2048, 5632], P(('dp', 'fsdp'))
- up_weight_next: float32 [2048, 5632], P(('dp', 'fsdp'))
- up_first_next: float32 [2048, 5632], P(('dp', 'fsdp'))
- up_second_next: float32 [2048, 5632], P(('dp', 'fsdp'))
- down_weight_next: float32 [5632, 2048], P(('dp', 'fsdp'))
- down_first_next: float32 [5632, 2048], P(('dp', 'fsdp'))
- down_second_next: float32 [5632, 2048], P(('dp', 'fsdp'))
- norm_gains_next: float32 [2, 2048], P(None, ('dp', 'fsdp'))
- gains_first_next: float32 [2, 2048], P(None, ('dp', 'fsdp'))
- gains_second_next: float32 [2, 2048], P(None, ('dp', 'fsdp'))
The draws below stay inside these ranges and needn't reach their ends.
Inputs may be any that keep to these rules, and one draw needn't show every extreme that they name: `seq_lengths`: row b holds, in token order, the lengths of the 3 sequences of batch b; each row sums to 1024; the middle sequence has 896 tokens and the other two together 128.
All inputs are finite; a program needn't handle non-finite values.
Results may differ from the reference program's by a relative error of at most 0.014.
Values may be sent and summed in bfloat16 or wider, within the bound.
No kernel may reach another device: no remote copies, remote signals or barrier semaphores. Data moves between devices by JAX's collectives and lax.ppermute only.
A program may use at most 288 MiB of HBM per device.

```python
import math
import jax
import jax.numpy as jnp
from jax import lax

D = 2048
HEADS = 32
KV_HEADS = 4
HEAD_DIM = 64
FF = 5632
TOK_DEV = 128
STEP = 3
GROUP_TOK = 1024
LONGEST = 896
TOKENS = 4096
N_DP = 4


def draw_seq_lengths(key, part):
    first = jax.random.randint(key, (N_DP, 1), 1, TOK_DEV, dtype=jnp.int32)
    last = TOK_DEV - first
    middle = jnp.zeros((N_DP, 1), jnp.int32) + (GROUP_TOK - TOK_DEV)
    return jnp.concatenate([first, middle, last], 1)


def shard_levels(key, shape, split, low, top_value):
    factor_of, own = 1.0, jax.random.fold_in(key, 6)
    for dim, blocks in split:
        heights = jnp.exp(jax.random.uniform(jax.random.fold_in(own, dim), (blocks,), jnp.float32, low / len(split), top_value / len(split)))
        factor_of = factor_of * jnp.repeat(heights, shape[dim] // blocks).reshape([-1 if axis == dim else 1 for axis in range(len(shape))])
    return factor_of


def gaussian(rng, dims, deviation, reach, shards=(), held_as=jnp.bfloat16):
    loudness = shard_levels(rng, dims, shards, -0.22, 0.18) if shards else 1.0
    array = jax.random.normal(rng, dims, jnp.float32) * deviation * loudness
    return jnp.minimum(jnp.maximum(array, -reach), reach).astype(held_as)


def setup_inputs(seed: int = 0) -> dict:
    seeds = jax.random.split(jax.random.key(seed), 28)
    return {
        "tokens": gaussian(seeds[0], (TOKENS, D), 1.0, 6.0, ((0, 32),)),
        "out_grad": gaussian(seeds[1], (TOKENS, D), 1.0, 6.0, ((0, 32),)),
        "seq_lengths": draw_seq_lengths(jax.random.fold_in(seeds[27], 71), 0),
        "query_weight": gaussian(seeds[3], (D, HEADS * HEAD_DIM), D ** -0.5, 0.125, ((0, 32),), jnp.float32),
        "query_first": gaussian(seeds[4], (D, HEADS * HEAD_DIM), (TOKENS ** 0.5), 384.0, ((0, 32),), jnp.float32),
        "query_second": jnp.clip(jnp.exp(math.log(32768.0) - 2.7725887 * jax.random.uniform(seeds[5], (D, HEADS * HEAD_DIM), jnp.float32) ** shard_levels(seeds[5], (D, HEADS * HEAD_DIM), ((0, 32),), -0.2, 0.2)), 2048.0, 32768.0),
        "key_weight": gaussian(seeds[6], (D, KV_HEADS * HEAD_DIM), D ** -0.5, 0.125, ((0, 32),), jnp.float32),
        "key_first": gaussian(seeds[7], (D, KV_HEADS * HEAD_DIM), (3 * TOKENS ** 0.5), 1024.0, ((0, 32),), jnp.float32),
        "key_second": jnp.clip(jnp.exp(math.log(294912.0) - 2.7725887 * jax.random.uniform(seeds[8], (D, KV_HEADS * HEAD_DIM), jnp.float32) ** shard_levels(seeds[8], (D, KV_HEADS * HEAD_DIM), ((0, 32),), -0.2, 0.2)), 18432.0, 294912.0),
        "value_weight": gaussian(seeds[9], (D, KV_HEADS * HEAD_DIM), D ** -0.5, 0.125, ((0, 32),), jnp.float32),
        "value_first": gaussian(seeds[10], (D, KV_HEADS * HEAD_DIM), (3 * TOKENS ** 0.5), 1024.0, ((0, 32),), jnp.float32),
        "value_second": jnp.clip(jnp.exp(math.log(294912.0) - 2.7725887 * jax.random.uniform(seeds[11], (D, KV_HEADS * HEAD_DIM), jnp.float32) ** shard_levels(seeds[11], (D, KV_HEADS * HEAD_DIM), ((0, 32),), -0.2, 0.2)), 18432.0, 294912.0),
        "output_weight": gaussian(seeds[12], (HEADS * HEAD_DIM, D), (HEADS * HEAD_DIM * 8 // LONGEST) ** -0.5, 1.5, ((0, 32),), jnp.float32),
        "output_first": gaussian(seeds[13], (HEADS * HEAD_DIM, D), ((8 * TOKENS // LONGEST) ** 0.5), 32.0, ((0, 32),), jnp.float32),
        "output_second": jnp.clip(jnp.exp(math.log(292.0) - 2.786382 * jax.random.uniform(seeds[14], (HEADS * HEAD_DIM, D), jnp.float32) ** shard_levels(seeds[14], (HEADS * HEAD_DIM, D), ((0, 32),), -0.2, 0.2)), 18.0, 292.0),
        "gate_weight": gaussian(seeds[15], (D, FF), D ** -0.5, 0.125, ((0, 32),), jnp.float32),
        "gate_first": gaussian(seeds[16], (D, FF), (0.6 * TOKENS ** 0.5), 224.0, ((0, 32),), jnp.float32),
        "gate_second": jnp.clip(jnp.exp(math.log(11796.48) - 2.7725887 * jax.random.uniform(seeds[17], (D, FF), jnp.float32) ** shard_levels(seeds[17], (D, FF), ((0, 32),), -0.2, 0.2)), 737.28, 11796.48),
        "up_weight": gaussian(seeds[18], (D, FF), D ** -0.5, 0.125, ((0, 32),), jnp.float32),
        "up_first": gaussian(seeds[19], (D, FF), (0.6 * TOKENS ** 0.5), 224.0, ((0, 32),), jnp.float32),
        "up_second": jnp.clip(jnp.exp(math.log(11796.48) - 2.7725887 * jax.random.uniform(seeds[20], (D, FF), jnp.float32) ** shard_levels(seeds[20], (D, FF), ((0, 32),), -0.2, 0.2)), 737.28, 11796.48),
        "down_weight": gaussian(seeds[21], (FF, D), FF ** -0.5, 0.078125, ((0, 32),), jnp.float32),
        "down_first": gaussian(seeds[22], (FF, D), (0.6 * TOKENS ** 0.5), 224.0, ((0, 32),), jnp.float32),
        "down_second": jnp.clip(jnp.exp(math.log(11796.48) - 2.7725887 * jax.random.uniform(seeds[23], (FF, D), jnp.float32) ** shard_levels(seeds[23], (FF, D), ((0, 32),), -0.2, 0.2)), 737.28, 11796.48),
        "norm_gains": jnp.clip(1.0 + 0.1 * jax.random.normal(seeds[24], (2, D), jnp.float32), 0.5, 1.5),
        "gains_first": gaussian(seeds[25], (2, D), (1.5 * TOKENS ** 0.5), 512.0, ((1, 32),), jnp.float32),
        "gains_second": jnp.clip(jnp.exp(math.log(73728.0) - 2.7725887 * jax.random.uniform(seeds[26], (2, D), jnp.float32) ** shard_levels(seeds[26], (2, D), ((1, 32),), -0.2, 0.2)), 4608.0, 73728.0),
    }


@jax.custom_vjp
def low(v):
    return lax.optimization_barrier(v.astype(jnp.bfloat16)).astype(jnp.float32)

@jax.custom_vjp
def low_back(v):
    return v

def low_keep(v):
    return (low(v), None)

def low_pass(kept, grad):
    return (grad,)

def back_keep(v):
    return (v, None)

def back_low(kept, grad):
    return (low(grad),)
low.defvjp(low_keep, low_pass)
low_back.defvjp(back_keep, back_low)
NORM_EPS = 1e-05
ROPE_BASE = 10000.0
BETA = 0.5
ADAM_EPS = 1e-08
DECAY = 0.1
RATES = (0.02, 0.02, 0.02, 0.1, 0.02, 0.02, 0.02, 0.2)
MASKED = -1e+30

def matmul(left, right):
    return jnp.dot(left, right, precision=lax.Precision.HIGHEST, preferred_element_type=jnp.float32)

def rms_norm(values, gain):
    return values * lax.rsqrt(lax.optimization_barrier(jnp.mean(values * values, -1, keepdims=True)) + NORM_EPS) * gain

def rope_tables(places, head_size):
    half = head_size // 2
    freqs = jnp.exp(jnp.arange(half, dtype=jnp.float32) * (-2.0 * math.log(ROPE_BASE) / head_size))
    angles = places.astype(jnp.float32)[:, None] * freqs[None, :]
    cosine = jnp.cos(angles)
    sine = jnp.sin(angles)
    return (jnp.concatenate([cosine, cosine], 1), jnp.concatenate([sine, sine], 1))

def rotate(values, cosine, sine):
    half = values.shape[-1] // 2
    turned = jnp.concatenate([-values[..., half:], values[..., :half]], -1)
    return values * cosine[:, None, :] + turned * sine[:, None, :]

def segment_info(lengths_row, places):
    ends = jnp.cumsum(lengths_row, dtype=jnp.int32)
    starts = ends - lengths_row
    segments = lax.optimization_barrier(jnp.sum((places[:, None] >= ends[None, :]).astype(jnp.int32), 1, dtype=jnp.int32))
    which_seq = segments[:, None] == jnp.arange(lengths_row.shape[0], dtype=jnp.int32)[None, :]
    first_place = lax.optimization_barrier(jnp.sum(jnp.where(which_seq, starts[None, :], 0), 1, dtype=jnp.int32))
    return (segments, places - first_place)

def group_layer(group_items, rounded):
    group_tokens, segments, places = group_items
    w_query, w_key, w_value, w_output, w_gate, w_up, w_down, gains = rounded
    length = group_tokens.shape[0]
    cosine, sine = rope_tables(places, HEAD_DIM)
    normed = low(rms_norm(group_tokens, gains[0]))
    queries = low_back(matmul(normed, w_query)).reshape(length, HEADS, HEAD_DIM)
    queries = low(rotate(queries, cosine, sine))
    keys_rot = low_back(matmul(normed, w_key)).reshape(length, KV_HEADS, HEAD_DIM)
    keys_rot = low(rotate(keys_rot, cosine, sine))
    values = low(low_back(matmul(normed, w_value))).reshape(length, KV_HEADS, HEAD_DIM)
    shared = HEADS // KV_HEADS
    keys_all = jnp.repeat(keys_rot, shared, axis=1)
    values_all = jnp.repeat(values, shared, axis=1)
    position = jnp.arange(length, dtype=jnp.int32)
    allowed = (segments[:, None] == segments[None, :]) & (position[None, :] <= position[:, None])
    score_scale = HEAD_DIM ** (-0.5)

    def one_head(head_items):
        query_head, key_head, value_head = head_items
        scores = low_back(matmul(query_head, key_head.T)) * score_scale
        scores = jnp.where(allowed, scores, MASKED)
        soft_weights = jax.nn.softmax(scores, axis=-1)
        mixture = matmul(low(soft_weights), value_head)
        return low(low_back(mixture))
    mixtures = lax.map(jax.checkpoint(one_head), (jnp.swapaxes(queries, 0, 1), jnp.swapaxes(keys_all, 0, 1), jnp.swapaxes(values_all, 0, 1)))
    attended = jnp.swapaxes(mixtures, 0, 1).reshape(length, HEADS * HEAD_DIM)
    resid_sum = group_tokens + low_back(matmul(attended, w_output))
    normed_two = low(rms_norm(resid_sum, gains[1]))
    gate_value = low_back(matmul(normed_two, w_gate))
    up_value = low_back(matmul(normed_two, w_up))
    hidden = low(jax.nn.silu(gate_value) * up_value)
    return resid_sum + low_back(matmul(hidden, w_down))

def adam_step(master, first_moment, second_moment, gradient, rate):
    first_new = BETA * first_moment + (1.0 - BETA) * gradient
    second_new = BETA * second_moment + (1.0 - BETA) * gradient * gradient
    correction = 1.0 - BETA ** STEP
    master_new = master - rate * (first_new / correction / (jnp.sqrt(second_new / correction) + ADAM_EPS) + DECAY * master)
    return (master_new, first_new, second_new)

def reference(tokens, out_grad, seq_lengths, query_weight, query_first, query_second, key_weight, key_first, key_second, value_weight, value_first, value_second, output_weight, output_first, output_second, gate_weight, gate_first, gate_second, up_weight, up_first, up_second, down_weight, down_first, down_second, norm_gains, gains_first, gains_second):
    tokens_f = tokens.astype(jnp.float32)
    places_all = jnp.arange(GROUP_TOK, dtype=jnp.int32)
    segments_all, positions_all = jax.vmap(segment_info, (0, None))(seq_lengths, places_all)
    masters = (query_weight, key_weight, value_weight, output_weight, gate_weight, up_weight, down_weight, norm_gains)
    firsts = (query_first, key_first, value_first, output_first, gate_first, up_first, down_first, gains_first)
    seconds = (query_second, key_second, value_second, output_second, gate_second, up_second, down_second, gains_second)

    def forward(tokens_in, weights):
        rounded = tuple((low(weight) for weight in weights))

        def one_group(group_items):
            return group_layer(group_items, rounded)
        outputs = lax.map(jax.checkpoint(one_group), (tokens_in.reshape(N_DP, GROUP_TOK, D), segments_all, positions_all))
        return outputs.reshape(N_DP * GROUP_TOK, D)
    result, pullback = jax.vjp(forward, tokens_f, masters)
    grad_tokens, grad_masters = pullback(out_grad.astype(jnp.float32))
    updated = [adam_step(masters[number], firsts[number], seconds[number], grad_masters[number], RATES[number]) for number in range(8)]
    return (result.astype(jnp.bfloat16), grad_tokens, updated[0][0], updated[0][1], updated[0][2], updated[1][0], updated[1][1], updated[1][2], updated[2][0], updated[2][1], updated[2][2], updated[3][0], updated[3][1], updated[3][2], updated[4][0], updated[4][1], updated[4][2], updated[5][0], updated[5][1], updated[5][2], updated[6][0], updated[6][1], updated[6][2], updated[7][0], updated[7][1], updated[7][2])
```

```python
import functools
import math

import jax
import jax.numpy as jnp
from jax import lax
from jax.experimental import pallas as pl
from jax.experimental.pallas import tpu as pltpu
from jax.sharding import PartitionSpec as P

HEADS = 32
KV_HEADS = 4
HEAD_DIM = 64
STEP = 3

NORM_EPS = 1e-05
ROPE_BASE = 10000.0
BETA = 0.5
ADAM_EPS = 1e-08
DECAY = 0.1
MASKED = -1e30
PAIR = 2 * HEAD_DIM
BF16 = jnp.bfloat16
F32 = jnp.float32


def matmul(left, right):
    return jnp.dot(left, right, preferred_element_type=F32)


def matmul_tn(left, right):
    return lax.dot_general(left, right, (((0,), (0,)), ((), ())), preferred_element_type=F32)


def matmul_nt(left, right):
    return lax.dot_general(left, right, (((1,), (1,)), ((), ())), preferred_element_type=F32)


def rms_scale(values):
    return lax.rsqrt(jnp.mean(values * values, -1, keepdims=True) + NORM_EPS)


def adam_step(master, first_moment, second_moment, gradient, rate):
    first_new = BETA * first_moment + (1.0 - BETA) * gradient
    second_new = BETA * second_moment + (1.0 - BETA) * gradient * gradient
    correction = 1.0 - BETA**STEP
    master_new = master - rate * (
        first_new / correction / (jnp.sqrt(second_new / correction) + ADAM_EPS) + DECAY * master
    )
    return (master_new, first_new, second_new)


def core_swap(value):
    members = lax.axis_size("fsdp")
    return lax.ppermute(value, "fsdp", [(i, i ^ 1) for i in range(members)])


def chip_send(value, step):
    members = lax.axis_size("fsdp")
    return lax.ppermute(value, "fsdp", [(i, i ^ (2 * step)) for i in range(members)])


def plane_gather(own):
    chips = lax.axis_size("fsdp") // 2
    mine = jnp.stack([own] + [chip_send(own, step) for step in range(1, chips)])
    partner = core_swap(mine)
    return jnp.stack([mine, partner], 1).reshape((2 * chips,) + own.shape)


def plane_scatter(parts):
    members = parts.shape[0]
    chips = members // 2
    parts = parts.reshape((chips, 2) + parts.shape[1:])
    sums = parts[:, 0] + core_swap(parts[:, 1].astype(BF16)).astype(F32)
    total = sums[0]
    low = sums.astype(BF16)
    for step in range(1, chips):
        total = total + chip_send(low[step], step).astype(F32)
    return total


def plane_exchange(blocks):
    members = blocks.shape[0]
    chips = members // 2
    blocks = blocks.reshape((chips, 2) + blocks.shape[1:])
    mine, other = blocks[:, 0], core_swap(blocks[:, 1])
    pairs = jnp.stack([mine, other], 1)
    got = jnp.stack([pairs[0]] + [chip_send(pairs[step], step) for step in range(1, chips)])
    return got.reshape((members,) + blocks.shape[2:])


def by_offset(blocks, index):
    count = blocks.shape[0]
    return jnp.stack(
        [lax.dynamic_index_in_dim(blocks, j ^ index, 0, keepdims=False) for j in range(count)]
    )


def lane_ids(shape):
    return lax.broadcasted_iota(jnp.int32, shape, len(shape) - 1)


def turn(values, cosine, sine):
    low_half = lane_ids(values.shape) % HEAD_DIM < HEAD_DIM // 2
    shifted = jnp.where(
        low_half,
        pltpu.roll(values, PAIR - HEAD_DIM // 2, 1),
        pltpu.roll(values, HEAD_DIM // 2, 1),
    )
    return values * cosine + shifted * sine


def attend_kernel(
    members, pairs, index_ref, start_ref, cos_ref, sin_ref, qkv_ref, q_ref, kv_ref, o_ref
):
    length = qkv_ref.shape[0]
    rows = length // members
    index = index_ref[0]
    even = lane_ids((rows, PAIR)) < HEAD_DIM
    for j in range(members):
        there = pl.ds(pl.multiple_of((j ^ index) * rows, rows), rows)
        here = pl.ds(j * rows, rows)
        cosine = cos_ref[here, :]
        sine = sin_ref[here, :]
        for pair in range(pairs):
            lanes = pl.ds(pair * PAIR, PAIR)
            turned = turn(qkv_ref[there, lanes], cosine, sine)
            q_ref[here, lanes] = (turned.astype(BF16).astype(F32) * HEAD_DIM**-0.5).astype(BF16)
        both = qkv_ref[there, pl.ds(pairs * PAIR, PAIR)]
        both = jnp.where(even, turn(both, cosine, sine), both)
        kv_ref[here, :] = both.astype(BF16)
    block = min(2 * rows, 256)
    for first in range(0, length, block):
        reach = first + block
        both = kv_ref[:reach, :].astype(F32)
        left = lane_ids(both.shape) < HEAD_DIM
        keys_even = jnp.where(left, both, 0.0)
        values_odd = jnp.where(left, 0.0, both)
        keys = (keys_even.astype(BF16), pltpu.roll(keys_even, HEAD_DIM, 1).astype(BF16))
        values = (pltpu.roll(values_odd, HEAD_DIM, 1).astype(BF16), values_odd.astype(BF16))
        query_at = first + lax.broadcasted_iota(jnp.int32, (block, reach), 0)
        key_at = lax.broadcasted_iota(jnp.int32, (block, reach), 1)
        allowed = (key_at <= query_at) & (key_at >= start_ref[first:reach, :])
        for pair in range(pairs):
            lanes = pl.ds(pair * PAIR, PAIR)
            query = q_ref[first:reach, lanes]
            mixed = jnp.zeros((block, PAIR), F32)
            for side in range(2):
                scores = jnp.where(allowed, matmul_nt(query, keys[side]), MASKED)
                raised = jnp.exp(scores - jnp.max(scores, -1, keepdims=True))
                weights = raised * (1.0 / jnp.sum(raised, -1, keepdims=True))
                mixed = mixed + matmul(weights.astype(BF16), values[side])
            mixed = mixed.astype(BF16)
            for part in range(block // rows):
                j = first // rows + part
                there = pl.ds(pl.multiple_of((j ^ index) * rows, rows), rows)
                o_ref[there, lanes] = mixed[part * rows : (part + 1) * rows, :]


def attend(qkv, index, start, cosine, sine):
    length, width = qkv.shape
    pairs = width // PAIR - 1
    vmem = pl.BlockSpec(memory_space=pltpu.VMEM)
    return pl.pallas_call(
        functools.partial(attend_kernel, lax.axis_size("fsdp"), pairs),
        out_shape=(
            jax.ShapeDtypeStruct((length, pairs * PAIR), BF16),
            jax.ShapeDtypeStruct((length, PAIR), BF16),
            jax.ShapeDtypeStruct((length, pairs * PAIR), BF16),
        ),
        in_specs=[pl.BlockSpec(memory_space=pltpu.SMEM)] + [vmem] * 4,
        out_specs=(vmem,) * 3,
        compiler_params=pltpu.CompilerParams(vmem_limit_bytes=48 * 2**20),
        cost_estimate=pl.CostEstimate(
            flops=8 * length * length * pairs * PAIR // 3,
            bytes_accessed=length * pairs * PAIR * 12,
            transcendentals=length * length * pairs,
        ),
        name="attend",
    )(index, start, cosine, sine, qkv)


def attend_back_kernel(
    members,
    pairs,
    index_ref,
    start_ref,
    cos_ref,
    sin_ref,
    q_ref,
    kv_ref,
    do_ref,
    out_ref,
    dk_ref,
    dv_ref,
):
    length = q_ref.shape[0]
    rows = length // members
    index = index_ref[0]
    block = min(2 * rows, 256)
    dk_ref[...] = jnp.zeros_like(dk_ref)
    dv_ref[...] = jnp.zeros_like(dv_ref)
    for first in range(0, length, block):
        reach = first + block
        both = kv_ref[:reach, :].astype(F32)
        left = lane_ids(both.shape) < HEAD_DIM
        keys_even = jnp.where(left, both, 0.0)
        values_odd = jnp.where(left, 0.0, both)
        keys = (keys_even.astype(BF16), pltpu.roll(keys_even, HEAD_DIM, 1).astype(BF16))
        values = (pltpu.roll(values_odd, HEAD_DIM, 1).astype(BF16), values_odd.astype(BF16))
        key_at = lax.broadcasted_iota(jnp.int32, (reach, block), 0)
        query_at = first + lax.broadcasted_iota(jnp.int32, (reach, block), 1)
        allowed = (key_at <= query_at) & (key_at >= start_ref[:, first:reach])
        half = lane_ids((block, PAIR)) < HEAD_DIM
        for pair in range(pairs):
            lanes = pl.ds(pair * PAIR, PAIR)
            query = q_ref[first:reach, lanes]
            grad = jnp.concatenate(
                [
                    do_ref[
                        pl.ds(pl.multiple_of(((first // rows + part) ^ index) * rows, rows), rows),
                        lanes,
                    ]
                    for part in range(block // rows)
                ],
                0,
            )
            dq = jnp.zeros((block, PAIR), F32)
            for side in range(2):
                keep = half if side == 0 else ~half
                query_side = jnp.where(keep, query.astype(F32), 0.0).astype(BF16)
                grad_side = jnp.where(keep, grad.astype(F32), 0.0).astype(BF16)
                scores = jnp.where(allowed, matmul_nt(keys[side], query), MASKED)
                raised = jnp.exp(scores - jnp.max(scores, 0, keepdims=True))
                weights = raised * (1.0 / jnp.sum(raised, 0, keepdims=True))
                dp = matmul_nt(values[side], grad)
                centre = jnp.sum(weights * dp, 0, keepdims=True)
                ds = (weights * (dp - centre)).astype(BF16)
                dv_ref[:reach, :] += matmul(weights.astype(BF16), grad_side)
                dk_ref[:reach, :] += matmul(ds, query_side)
                dq = dq + matmul_tn(ds, keys[side])
            dq = dq * HEAD_DIM**-0.5
            for part in range(block // rows):
                j = first // rows + part
                piece = dq[part * rows : (part + 1) * rows, :]
                here = pl.ds(j * rows, rows)
                there = pl.ds(pl.multiple_of((j ^ index) * rows, rows), rows)
                out_ref[there, lanes] = turn(piece, cos_ref[here, :], -sin_ref[here, :]).astype(BF16)
    left = lane_ids((rows, PAIR)) < HEAD_DIM
    for j in range(members):
        here = pl.ds(j * rows, rows)
        there = pl.ds(pl.multiple_of((j ^ index) * rows, rows), rows)
        dk = dk_ref[here, :]
        dv = dv_ref[here, :]
        dk = turn(dk + pltpu.roll(dk, HEAD_DIM, 1), cos_ref[here, :], -sin_ref[here, :])
        dv = dv + pltpu.roll(dv, HEAD_DIM, 1)
        out_ref[there, pl.ds(pairs * PAIR, PAIR)] = jnp.where(left, dk, dv).astype(BF16)


def attend_back(queries, keys_values, grad, index, start, cosine, sine):
    length, width = queries.shape
    pairs = width // PAIR
    vmem = pl.BlockSpec(memory_space=pltpu.VMEM)
    return pl.pallas_call(
        functools.partial(attend_back_kernel, lax.axis_size("fsdp"), pairs),
        out_shape=jax.ShapeDtypeStruct((length, width + PAIR), BF16),
        in_specs=[pl.BlockSpec(memory_space=pltpu.SMEM)] + [vmem] * 6,
        out_specs=vmem,
        scratch_shapes=[pltpu.VMEM((length, PAIR), F32), pltpu.VMEM((length, PAIR), F32)],
        compiler_params=pltpu.CompilerParams(vmem_limit_bytes=48 * 2**20),
        cost_estimate=pl.CostEstimate(
            flops=20 * length * length * pairs * PAIR // 3,
            bytes_accessed=length * pairs * PAIR * 12,
            transcendentals=length * length * pairs,
        ),
        name="attend_back",
    )(index, start, cosine, sine, queries, keys_values, grad)


def segment_starts(lengths_row, length):
    count = lengths_row.shape[0]
    ahead = jnp.arange(count)[:, None] < jnp.arange(count)[None, :]
    starts = jnp.sum(jnp.where(ahead, lengths_row[:, None], 0), 0, dtype=jnp.int32)
    ends = starts + lengths_row
    places = jnp.arange(length, dtype=jnp.int32)
    within = (places[:, None] >= starts[None, :]) & (places[:, None] < ends[None, :])
    return jnp.sum(jnp.where(within, starts[None, :], 0), 1, dtype=jnp.int32)


def rope_tables(positions):
    half = HEAD_DIM // 2
    freqs = jnp.exp(jnp.arange(half, dtype=F32) * (-2.0 * math.log(ROPE_BASE) / HEAD_DIM))
    angles = positions.astype(F32)[:, None] * freqs[None, :]
    cosine = jnp.cos(angles)
    sine = jnp.sin(angles)
    return (
        jnp.concatenate([cosine] * 4, 1),
        jnp.concatenate([-sine, sine, -sine, sine], 1),
    )


def local(
    tokens,
    out_grad,
    seq_lengths,
    query_weight,
    query_first,
    query_second,
    key_weight,
    key_first,
    key_second,
    value_weight,
    value_first,
    value_second,
    output_weight,
    output_first,
    output_second,
    gate_weight,
    gate_first,
    gate_second,
    up_weight,
    up_first,
    up_second,
    down_weight,
    down_first,
    down_second,
    norm_gains,
    gains_first,
    gains_second,
):
    both = ("dp", "fsdp")
    planes = lax.axis_size("dp")
    members = lax.axis_size("fsdp")
    index = lax.axis_index("fsdp")
    index_ref = index.astype(jnp.int32)[None]
    count, width = tokens.shape
    length = count * members
    slice_rows = query_weight.shape[0]
    own_q = query_weight.shape[1] // members
    own_ff = gate_weight.shape[1] // members
    ff_piece = own_ff // planes
    sharing = members // KV_HEADS

    tokens_all = plane_gather(tokens).reshape(length, width)
    out_grad_all = plane_gather(out_grad).reshape(length, width)
    gains = lax.all_gather(norm_gains.astype(BF16), both, axis=1, tiled=True).astype(F32)

    start = segment_starts(seq_lengths[0], length)
    cosine, sine = rope_tables(jnp.arange(length, dtype=jnp.int32) - start)

    def head_columns(weight):
        return weight.reshape(slice_rows, -1, HEAD_DIM * HEADS // members)

    q_cols = query_weight.astype(BF16).reshape(slice_rows, members, own_q)
    k_cols = jnp.repeat(key_weight.astype(BF16).reshape(slice_rows, KV_HEADS, HEAD_DIM), sharing, 1)
    v_cols = jnp.repeat(value_weight.astype(BF16).reshape(slice_rows, KV_HEADS, HEAD_DIM), sharing, 1)
    qkv_cols = jnp.transpose(jnp.concatenate([q_cols, k_cols, v_cols], 2), (1, 0, 2))
    qkv_got = by_offset(plane_exchange(by_offset(qkv_cols, index)), index)
    w_qkv = lax.all_gather(qkv_got.reshape(members * slice_rows, -1), "dp", axis=0, tiled=True)

    hop = members // planes
    out_rows = lax.all_gather(output_weight.astype(BF16), "dp", axis=0, tiled=False)
    own_plane = index // hop

    def out_route(turn_no):
        return [
            (i, ((turn_no + i) % planes) * hop + i // planes) for i in range(members)
        ]

    w_output = jnp.zeros((planes, slice_rows, width), BF16)
    for turn_no in range(planes):
        sent = lax.dynamic_index_in_dim(out_rows, (turn_no + index) % planes, 0, keepdims=False)
        got = lax.ppermute(sent, "fsdp", out_route(turn_no))
        place = (own_plane + planes - turn_no) % planes
        w_output = lax.dynamic_update_index_in_dim(w_output, got, place, 0)
    w_output = w_output.reshape(planes * slice_rows, width)

    def ff_columns(weight):
        cols = weight.astype(BF16).reshape(slice_rows, planes, members, ff_piece)
        cols = jnp.transpose(cols, (2, 0, 1, 3)).reshape(members, slice_rows, own_ff)
        got = by_offset(plane_exchange(by_offset(cols, index)), index)
        return lax.all_gather(got.reshape(members * slice_rows, own_ff), "dp", axis=0, tiled=True)

    w_gate = ff_columns(gate_weight)
    w_up = ff_columns(up_weight)
    w_down = lax.all_gather(down_weight.astype(BF16), "dp", axis=0, tiled=True)

    tokens_f = tokens_all.astype(F32)
    scale_one_all = rms_scale(tokens_f)
    normed = (tokens_f * scale_one_all * gains[0]).astype(BF16)
    qkv = matmul(normed, w_qkv)
    queries, keys_values, attended = attend(qkv, index_ref, start[:, None], cosine, sine)
    own_tokens = tokens.astype(F32)
    mixed = matmul(attended, w_output)
    resid = own_tokens + plane_scatter(mixed.reshape(members, count, width))
    scale_two = rms_scale(resid)
    normed_two = plane_gather((resid * scale_two * gains[1]).astype(BF16)).reshape(length, width)
    gate_value = matmul(normed_two, w_gate)
    up_value = matmul(normed_two, w_up)
    sigmoid_gate = jax.nn.sigmoid(gate_value)
    hidden = (gate_value * sigmoid_gate * up_value).astype(BF16)

    grad_hidden = matmul_nt(out_grad_all, w_down)
    grad_gate = (
        grad_hidden * up_value * sigmoid_gate * (1.0 + gate_value * (1.0 - sigmoid_gate))
    ).astype(BF16)
    grad_up = (grad_hidden * gate_value * sigmoid_gate).astype(BF16)
    grad_normed_two = matmul_nt(grad_gate, w_gate) + matmul_nt(grad_up, w_up)
    grad_normed_two = plane_scatter(grad_normed_two.reshape(members, count, width))
    weighted_two = grad_normed_two * gains[1]
    grad_gain_two = jnp.sum(grad_normed_two * resid * scale_two, 0)
    grad_resid = (
        out_grad.astype(F32)
        + scale_two * weighted_two
        - resid
        * (scale_two * scale_two * scale_two)
        * jnp.mean(weighted_two * resid, -1, keepdims=True)
    )
    grad_attn_out = plane_gather(grad_resid.astype(BF16)).reshape(length, width)

    def ff_gradient(gradient):
        part = lax.psum_scatter(gradient.astype(BF16), "dp", scatter_dimension=0, tiled=True)
        blocks = by_offset(part.reshape(members, slice_rows, own_ff), index)
        got = by_offset(plane_exchange(blocks), index)
        got = got.reshape(members, slice_rows, planes, ff_piece)
        return jnp.transpose(got, (1, 2, 0, 3)).reshape(slice_rows, members * own_ff).astype(F32)

    grad_gate_weight = ff_gradient(matmul_tn(normed_two, grad_gate))
    grad_up_weight = ff_gradient(matmul_tn(normed_two, grad_up))
    grad_down_weight = lax.psum_scatter(
        matmul_tn(hidden, out_grad_all).astype(BF16), "dp", scatter_dimension=0, tiled=True
    ).astype(F32)
    result = resid + plane_scatter(matmul(hidden, w_down).reshape(members, count, width))

    grad_mixed = matmul_nt(grad_attn_out, w_output).astype(BF16)
    grad_qkv = attend_back(
        queries, keys_values, grad_mixed, index_ref, start[None, :], cosine, sine
    )
    grad_normed = plane_scatter(matmul_nt(grad_qkv, w_qkv).reshape(members, count, width))
    scale_one = rms_scale(own_tokens)
    weighted_one = grad_normed * gains[0]
    grad_gain_one = jnp.sum(grad_normed * own_tokens * scale_one, 0)
    grad_tokens = (
        grad_resid
        + scale_one * weighted_one
        - own_tokens
        * (scale_one * scale_one * scale_one)
        * jnp.mean(weighted_one * own_tokens, -1, keepdims=True)
    )

    grad_output = matmul_tn(attended, grad_attn_out).astype(BF16)
    grad_output = grad_output.reshape(planes, slice_rows, width)
    out_parts = jnp.zeros((planes, slice_rows, width), BF16)
    for turn_no in range(planes):
        place = (own_plane + planes - turn_no) % planes
        sent = lax.dynamic_index_in_dim(grad_output, place, 0, keepdims=False)
        got = lax.ppermute(sent, "fsdp", [(b, a) for a, b in out_route(turn_no)])
        out_parts = lax.dynamic_update_index_in_dim(out_parts, got, (turn_no + index) % planes, 0)
    grad_output_weight = lax.psum_scatter(
        out_parts.reshape(planes * slice_rows, width), "dp", scatter_dimension=0, tiled=True
    ).astype(F32)

    grad_w_qkv = lax.psum_scatter(
        matmul_tn(normed, grad_qkv).astype(BF16), "dp", scatter_dimension=0, tiled=True
    )
    blocks = by_offset(grad_w_qkv.reshape(members, slice_rows, -1), index)
    got = by_offset(plane_exchange(blocks), index).astype(F32)
    got = jnp.transpose(got, (1, 0, 2))
    grad_query_weight = got[:, :, :own_q].reshape(slice_rows, -1)
    grad_kv = got[:, :, own_q:].reshape(slice_rows, KV_HEADS, sharing, PAIR).sum(2)
    grad_key_weight = grad_kv[:, :, :HEAD_DIM].reshape(slice_rows, -1)
    grad_value_weight = grad_kv[:, :, HEAD_DIM:].reshape(slice_rows, -1)
    gain_grads = lax.psum_scatter(
        jnp.stack([grad_gain_one, grad_gain_two]), both, scatter_dimension=1, tiled=True
    )

    updated = (
        adam_step(query_weight, query_first, query_second, grad_query_weight, 0.02)
        + adam_step(key_weight, key_first, key_second, grad_key_weight, 0.02)
        + adam_step(value_weight, value_first, value_second, grad_value_weight, 0.02)
        + adam_step(output_weight, output_first, output_second, grad_output_weight, 0.1)
        + adam_step(gate_weight, gate_first, gate_second, grad_gate_weight, 0.02)
        + adam_step(up_weight, up_first, up_second, grad_up_weight, 0.02)
        + adam_step(down_weight, down_first, down_second, grad_down_weight, 0.02)
        + adam_step(norm_gains, gains_first, gains_second, gain_grads, 0.2)
    )
    return (result.astype(BF16), grad_tokens) + updated


def solution(mesh):
    rows = P(("dp", "fsdp"), None)
    columns = P(None, ("dp", "fsdp"))
    in_specs = (rows, rows, P("dp", None)) + (rows,) * 21 + (columns,) * 3
    out_specs = (rows, rows) + (rows,) * 21 + (columns,) * 3
    return jax.shard_map(local, mesh=mesh, in_specs=in_specs, out_specs=out_specs, check_vma=False)
```

```python
import functools
import math

import jax
import jax.numpy as jnp
from jax import lax
from jax.experimental import pallas as pl
from jax.experimental.pallas import tpu as pltpu
from jax.sharding import PartitionSpec as P

HEADS = 32
KV_HEADS = 4
HEAD_DIM = 64
STEP = 3

NORM_EPS = 1e-05
ROPE_BASE = 10000.0
BETA = 0.5
ADAM_EPS = 1e-08
DECAY = 0.1
MASKED = -1e30
PAIR = 2 * HEAD_DIM
BF16 = jnp.bfloat16
F32 = jnp.float32


def matmul(left, right):
    return jnp.dot(left, right, preferred_element_type=F32)


def matmul_tn(left, right):
    return lax.dot_general(left, right, (((0,), (0,)), ((), ())), preferred_element_type=F32)


def matmul_nt(left, right):
    return lax.dot_general(left, right, (((1,), (1,)), ((), ())), preferred_element_type=F32)


def rms_scale(values):
    return lax.rsqrt(jnp.mean(values * values, -1, keepdims=True) + NORM_EPS)


def adam_step(master, first_moment, second_moment, gradient, rate):
    first_new = BETA * first_moment + (1.0 - BETA) * gradient
    second_new = BETA * second_moment + (1.0 - BETA) * gradient * gradient
    correction = 1.0 - BETA**STEP
    master_new = master - rate * (
        first_new / correction / (jnp.sqrt(second_new / correction) + ADAM_EPS) + DECAY * master
    )
    return (master_new, first_new, second_new)


def core_swap(value):
    members = lax.axis_size("fsdp")
    return lax.ppermute(value, "fsdp", [(i, i ^ 1) for i in range(members)])


def chip_send(value, step):
    members = lax.axis_size("fsdp")
    return lax.ppermute(value, "fsdp", [(i, i ^ (2 * step)) for i in range(members)])


def plane_send(value, step):
    planes = lax.axis_size("dp")
    return lax.ppermute(value, "dp", [(i, i ^ step) for i in range(planes)])


def gather(own, send, count):
    return [own] + [send(own, step) for step in range(1, count)]


def gather_line(own, send, count):
    got = {0: own}
    bit = count // 2
    while bit:
        for step in sorted(got):
            got[step + bit] = send(got[step], bit)
        bit //= 2
    return [got[step] for step in range(count)]


def gather_cores(own, send, count):
    blocks = []
    for block in send(own, count):
        blocks += [block, core_swap(block)]
    return blocks


def scatter_cores(mine, other, send):
    total = None
    for step in list(range(1, len(mine))) + [0]:
        part = mine[step] + core_swap(other[step]).astype(F32)
        if step:
            part = send(part.astype(BF16), step).astype(F32)
        total = part if total is None else total + part
    return total


def scatter_sum(parts, send):
    total = parts[0].astype(F32)
    for step in range(1, len(parts)):
        total = total + send(parts[step], step).astype(F32)
    return total


def exchange(mine, other, send):
    got = core_swap(other)
    pairs = [jnp.stack([mine[step], got[step]]) for step in range(mine.shape[0])]
    return pairs[:1] + [send(pairs[step], step) for step in range(1, len(pairs))]


def by_offset(blocks, index):
    count = blocks.shape[0]
    return jnp.stack(
        [lax.dynamic_index_in_dim(blocks, j ^ index, 0, keepdims=False) for j in range(count)]
    )


def lane_ids(shape):
    return lax.broadcasted_iota(jnp.int32, shape, len(shape) - 1)


def turn(values, cosine, sine):
    low_half = lane_ids(values.shape) % HEAD_DIM < HEAD_DIM // 2
    shifted = jnp.where(
        low_half,
        pltpu.roll(values, PAIR - HEAD_DIM // 2, 1),
        pltpu.roll(values, HEAD_DIM // 2, 1),
    )
    return values * cosine + shifted * sine


VMEM = pl.BlockSpec(memory_space=pltpu.VMEM)
SMEM = pl.BlockSpec(memory_space=pltpu.SMEM)
ANY = pl.BlockSpec(memory_space=pl.ANY)


def params(mib=56):
    return pltpu.CompilerParams(vmem_limit_bytes=mib * 2**20)


def shape_of(shape, dtype=BF16):
    return jax.ShapeDtypeStruct(shape, dtype)


def cost(flops, moved, exps=0):
    return pl.CostEstimate(flops=int(flops), bytes_accessed=int(moved), transcendentals=int(exps))


def pack_kernel(planes, chips, piece, place, gate, up, query, key, value, gu_mine, gu_other, qkv_mine, qkv_other):
    plane, chip, core = place[0], place[1], place[2]
    own_q = query.shape[1] // (2 * chips)
    sharing = 2 * chips // KV_HEADS

    def put(mine, other, core_to, index, block):
        @pl.when(core == core_to)
        def _():
            mine[index] = block

        @pl.when(core != core_to)
        def _():
            other[index] = block

    for to in range(2 * chips):
        head = slice(to // sharing * HEAD_DIM, (to // sharing + 1) * HEAD_DIM)
        block = jnp.concatenate(
            [query[:, to * own_q : (to + 1) * own_q], key[:, head], value[:, head]], 1
        )
        put(qkv_mine, qkv_other, to % 2, (to // 2) ^ chip, block.astype(BF16))
    for side, weight in enumerate((gate, up)):
        for to in range(2 * planes):
            starts = [((to // 2 * chips + c) * 2 + to % 2) * piece for c in range(chips)]
            block = jnp.concatenate([weight[:, s : s + piece] for s in starts], 1).astype(BF16)
            put(
                gu_mine.at[:, side],
                gu_other.at[:, side],
                to % 2,
                (to // 2) ^ plane,
                block,
            )


def pack(place, planes, chips, gate, up, query, key, value):
    rows, hidden = gate.shape
    gu = shape_of((planes, 2, rows, hidden // (2 * planes)))
    qkv = shape_of((chips, rows, query.shape[1] // (2 * chips) + PAIR))
    return pl.pallas_call(
        functools.partial(pack_kernel, planes, chips, hidden // (2 * planes * chips)),
        out_shape=(gu, gu, qkv, qkv),
        in_specs=[SMEM] + [VMEM] * 5,
        out_specs=(VMEM,) * 4,
        compiler_params=params(),
        cost_estimate=cost(0, rows * hidden * 12),
        name="pack",
    )(place, gate, up, query, key, value)


def gather_rows_kernel(members, place, *refs):
    blocks, out = refs[:-1], refs[-1]
    first, core = place[0], place[1]
    rows = blocks[0].shape[-2]
    for step, block in enumerate(blocks):
        for side in range(2):
            at = ((first ^ step) * 2 + (core ^ side)) * rows
            if len(block.shape) == 3:
                out[pl.ds(pl.multiple_of(at, 16), rows), :] = block[side]
            else:
                for part in range(2):
                    out[part, pl.ds(pl.multiple_of(at, 16), rows), :] = block[side, part]


def gather_rows(first, core, pairs):
    lead, (rows, width) = pairs[0].shape[1:-2], pairs[0].shape[-2:]
    return pl.pallas_call(
        functools.partial(gather_rows_kernel, 2 * len(pairs)),
        out_shape=shape_of(lead + (2 * len(pairs) * rows, width)),
        in_specs=[SMEM] + [VMEM] * len(pairs),
        out_specs=VMEM,
        compiler_params=params(),
        cost_estimate=cost(0, pairs[0].size * len(pairs) * 4),
        name="gather_rows",
    )(jnp.stack([first, core]), *pairs)


def spread_rows_kernel(place, whole, mine, other):
    first, core = place[0], place[1]
    count = mine.shape[0]
    rows = mine.shape[-2]
    for step in range(count):
        for side, out in enumerate((mine, other)):
            at = pl.ds(pl.multiple_of(((first ^ step) * 2 + (core ^ side)) * rows, 16), rows)
            if len(whole.shape) == 2:
                out[step] = whole[at, :].astype(BF16)
            else:
                for part in range(2):
                    out[step, part] = whole[part, at, :].astype(BF16)


def spread_rows(first, core, whole, count):
    rows = whole.shape[-2] // (2 * count)
    out = shape_of((count,) + whole.shape[:-2] + (rows, whole.shape[-1]))
    return pl.pallas_call(
        spread_rows_kernel,
        out_shape=(out, out),
        in_specs=[SMEM, VMEM],
        out_specs=(VMEM, VMEM),
        compiler_params=params(),
        cost_estimate=cost(0, whole.size * 6),
        name="spread_rows",
    )(jnp.stack([first, core]), whole)


def attend_kernel(members, pairs, planes, place, start_ref, cos_ref, sin_ref, gain_ref, *refs):
    tokens, refs = refs[:members], refs[members:]
    weights, refs = refs[:planes], refs[planes:]
    normed_ref, q_ref, kv_ref, o_ref = refs
    plane, index = place[0], place[1]
    rows = tokens[0].shape[0]
    length = rows * members
    even = lane_ids((rows, PAIR)) < HEAD_DIM
    depth = weights[0].shape[0]
    for j in range(members):
        values = tokens[j][...].astype(F32)
        normed = values * rms_scale(values) * gain_ref[...]
        normed_ref[j * rows : (j + 1) * rows, :] = normed.astype(BF16)
    block = min(2 * rows, 256)
    per = block // rows
    for first in range(0, length, block):
        qkv = None
        for step in range(planes):
            columns = pl.ds(pl.multiple_of((plane ^ step) * depth, 128), depth)
            term = matmul(normed_ref[first : first + block, columns], weights[step][...])
            qkv = term if qkv is None else qkv + term
        for part in range(per):
            j = first // rows + part
            here = pl.ds(pl.multiple_of((j ^ index) * rows, rows), rows)
            cosine = cos_ref[here, :]
            sine = sin_ref[here, :]
            piece = qkv[part * rows : (part + 1) * rows, :]
            for pair in range(pairs):
                lanes = slice(pair * PAIR, (pair + 1) * PAIR)
                turned = turn(piece[:, lanes], cosine, sine).astype(BF16).astype(F32)
                q_ref[here, lanes] = (turned * HEAD_DIM**-0.5).astype(BF16)
            both = piece[:, pairs * PAIR :]
            kv_ref[here, :] = jnp.where(even, turn(both, cosine, sine), both).astype(BF16)
    for first in range(0, length, block):
        reach = first + block
        both = kv_ref[:reach, :].astype(F32)
        left = lane_ids(both.shape) < HEAD_DIM
        keys_even = jnp.where(left, both, 0.0)
        values_odd = jnp.where(left, 0.0, both)
        keys = (keys_even.astype(BF16), pltpu.roll(keys_even, HEAD_DIM, 1).astype(BF16))
        values = (pltpu.roll(values_odd, HEAD_DIM, 1).astype(BF16), values_odd.astype(BF16))
        query_at = first + lax.broadcasted_iota(jnp.int32, (block, reach), 0)
        key_at = lax.broadcasted_iota(jnp.int32, (block, reach), 1)
        allowed = (key_at <= query_at) & (key_at >= start_ref[first:reach, :])
        for pair in range(pairs):
            lanes = slice(pair * PAIR, (pair + 1) * PAIR)
            query = q_ref[first:reach, lanes]
            mixed = jnp.zeros((block, PAIR), F32)
            for side in range(2):
                scores = jnp.where(allowed, matmul_nt(query, keys[side]), MASKED)
                raised = jnp.exp(scores - jnp.max(scores, -1, keepdims=True))
                probs = raised * (1.0 / jnp.sum(raised, -1, keepdims=True))
                mixed = mixed + matmul(probs.astype(BF16), values[side])
            mixed = mixed.astype(BF16)
            for part in range(per):
                j = first // rows + part
                there = pl.ds(pl.multiple_of((j ^ index) * rows, rows), rows)
                o_ref[there, lanes] = mixed[part * rows : (part + 1) * rows, :]


def attend(place, tokens, weights, gain, start, cosine, sine):
    members, planes = len(tokens), len(weights)
    rows, width = tokens[0].shape
    length = members * rows
    pairs = weights[0].shape[1] // PAIR - 1
    return pl.pallas_call(
        functools.partial(attend_kernel, members, pairs, planes),
        out_shape=(
            shape_of((length, width)),
            shape_of((length, pairs * PAIR)),
            shape_of((length, PAIR)),
            shape_of((length, pairs * PAIR)),
        ),
        in_specs=[SMEM] + [VMEM] * (4 + members + planes),
        out_specs=(VMEM,) * 4,
        compiler_params=params(),
        cost_estimate=cost(
            2 * length * width * (pairs + 1) * PAIR + 3 * length * length * pairs * PAIR,
            length * width * 4,
            length * length * pairs,
        ),
        name="attend",
    )(place, start, cosine, sine, gain, *tokens, *weights)


def attend_back_kernel(members, pairs, place, start_ref, cos_ref, sin_ref, q_ref, kv_ref, w_ref, *refs):
    grads, refs = refs[:members], refs[members:]
    out_ref, do_ref, dk_ref, dv_ref = refs
    length = q_ref.shape[0]
    rows = length // members
    index = place[1]
    block = min(2 * rows, 256)
    per = block // rows
    for j in range(0, members, 2):
        grad = jnp.concatenate([grads[j][...], grads[j + 1][...]], 0)
        do_ref[j * rows : (j + 2) * rows, :] = matmul_nt(grad, w_ref[...]).astype(BF16)
    dk_ref[...] = jnp.zeros_like(dk_ref)
    dv_ref[...] = jnp.zeros_like(dv_ref)
    for first in range(0, length, block):
        reach = first + block
        both = kv_ref[:reach, :].astype(F32)
        left = lane_ids(both.shape) < HEAD_DIM
        keys_even = jnp.where(left, both, 0.0)
        values_odd = jnp.where(left, 0.0, both)
        keys = (keys_even.astype(BF16), pltpu.roll(keys_even, HEAD_DIM, 1).astype(BF16))
        values = (pltpu.roll(values_odd, HEAD_DIM, 1).astype(BF16), values_odd.astype(BF16))
        key_at = lax.broadcasted_iota(jnp.int32, (reach, block), 0)
        query_at = first + lax.broadcasted_iota(jnp.int32, (reach, block), 1)
        allowed = (key_at <= query_at) & (key_at >= start_ref[:, first:reach])
        half = lane_ids((block, PAIR)) < HEAD_DIM
        theres = [
            pl.ds(pl.multiple_of(((first // rows + part) ^ index) * rows, rows), rows)
            for part in range(per)
        ]
        for pair in range(pairs):
            lanes = slice(pair * PAIR, (pair + 1) * PAIR)
            query = q_ref[first:reach, lanes]
            grad = jnp.concatenate([do_ref[there, lanes] for there in theres], 0)
            dq = jnp.zeros((block, PAIR), F32)
            for side in range(2):
                keep = half if side == 0 else ~half
                query_side = jnp.where(keep, query.astype(F32), 0.0).astype(BF16)
                grad_side = jnp.where(keep, grad.astype(F32), 0.0).astype(BF16)
                scores = jnp.where(allowed, matmul_nt(keys[side], query), MASKED)
                raised = jnp.exp(scores - jnp.max(scores, 0, keepdims=True))
                probs = raised * (1.0 / jnp.sum(raised, 0, keepdims=True))
                dp = matmul_nt(values[side], grad)
                centre = jnp.sum(probs * dp, 0, keepdims=True)
                ds = (probs * (dp - centre)).astype(BF16)
                dv_ref[:reach, :] += matmul(probs.astype(BF16), grad_side)
                dk_ref[:reach, :] += matmul(ds, query_side)
                dq = dq + matmul_tn(ds, keys[side])
            dq = dq * HEAD_DIM**-0.5
            for part in range(per):
                piece = dq[part * rows : (part + 1) * rows, :]
                here = slice(first + part * rows, first + (part + 1) * rows)
                out_ref[theres[part], lanes] = turn(
                    piece, cos_ref[here, :], -sin_ref[here, :]
                ).astype(BF16)
    left = lane_ids((rows, PAIR)) < HEAD_DIM
    for j in range(members):
        here = slice(j * rows, (j + 1) * rows)
        there = pl.ds(pl.multiple_of((j ^ index) * rows, rows), rows)
        dk = dk_ref[here, :]
        dv = dv_ref[here, :]
        dk = turn(dk + pltpu.roll(dk, HEAD_DIM, 1), cos_ref[here, :], -sin_ref[here, :])
        dv = dv + pltpu.roll(dv, HEAD_DIM, 1)
        out_ref[there, pairs * PAIR :] = jnp.where(left, dk, dv).astype(BF16)


def attend_back(place, queries, keys_values, w_output, grads, start, cosine, sine):
    length, width = queries.shape
    pairs = width // PAIR
    members = len(grads)
    model = grads[0].shape[1]
    return pl.pallas_call(
        functools.partial(attend_back_kernel, members, pairs),
        out_shape=shape_of((length, width + PAIR)),
        in_specs=[SMEM] + [VMEM] * (6 + members),
        out_specs=VMEM,
        scratch_shapes=[
            pltpu.VMEM((length, width), BF16),
            pltpu.VMEM((length, PAIR), F32),
            pltpu.VMEM((length, PAIR), F32),
        ],
        compiler_params=params(),
        cost_estimate=cost(
            2 * length * width * model + 7 * length * length * width,
            length * model * 2,
            length * length * pairs,
        ),
        name="attend_back",
    )(place, start, cosine, sine, queries, keys_values, w_output, *grads)


def project_kernel(count, left_ref, weight_ref, *outs):
    rows = left_ref.shape[0] // (2 * count)
    for step in range(count):
        whole = matmul(left_ref[2 * step * rows : 2 * (step + 1) * rows, :], weight_ref[...])
        outs[step][...] = whole[:rows, :]
        outs[count + step][...] = whole[rows:, :].astype(BF16)


def project(left, weight, count):
    rows, width = left.shape[0] // (2 * count), weight.shape[1]
    outs = pl.pallas_call(
        functools.partial(project_kernel, count),
        out_shape=(shape_of((rows, width), F32),) * count + (shape_of((rows, width)),) * count,
        in_specs=[VMEM, VMEM],
        out_specs=(VMEM,) * (2 * count),
        compiler_params=params(),
        cost_estimate=cost(2 * left.size * width, left.shape[0] * width * 3),
        name="project",
    )(left, weight)
    return outs[:count], outs[count:]


def project_back_kernel(planes, count, place, left_ref, *refs):
    weights, outs = refs[:planes], refs[planes:]
    rows = left_ref.shape[0] // (2 * count)
    depth = weights[0].shape[0]
    for step in range(count):
        left = left_ref[2 * step * rows : 2 * (step + 1) * rows, :]
        for far in range(planes):
            columns = pl.ds(pl.multiple_of((place[0] ^ far) * depth, 128), depth)
            whole = matmul_nt(left, weights[far][...])
            outs[step][:, columns] = whole[:rows, :]
            outs[count + step][:, columns] = whole[rows:, :].astype(BF16)


def project_back(place, left, weights, count):
    rows, planes = left.shape[0] // (2 * count), len(weights)
    width = weights[0].shape[0] * planes
    outs = pl.pallas_call(
        functools.partial(project_back_kernel, planes, count),
        out_shape=(shape_of((rows, width), F32),) * count + (shape_of((rows, width)),) * count,
        in_specs=[SMEM] + [VMEM] * (1 + planes),
        out_specs=(VMEM,) * (2 * count),
        compiler_params=params(),
        cost_estimate=cost(2 * left.size * width, left.shape[0] * width * 3),
        name="project_back",
    )(place, left, *weights)
    return outs[:count], outs[count:]


def qkv_grad_kernel(place, normed_ref, grad_ref, *outs):
    depth = outs[0].shape[0]
    for far, out in enumerate(outs):
        columns = pl.ds(pl.multiple_of((place[0] ^ far) * depth, 128), depth)
        out[...] = matmul_tn(normed_ref[:, columns], grad_ref[...]).astype(BF16)


def qkv_grad(place, normed, grad, planes):
    depth, width = normed.shape[1] // planes, grad.shape[1]
    return pl.pallas_call(
        qkv_grad_kernel,
        out_shape=(shape_of((depth, width)),) * planes,
        in_specs=[SMEM, VMEM, VMEM],
        out_specs=(VMEM,) * planes,
        compiler_params=params(),
        cost_estimate=cost(2 * normed.size * width, normed.size * 2),
        name="qkv_grad",
    )(place, normed, grad)


def rows_grad_kernel(count, left_ref, *refs):
    grads, out = refs[:-1], refs[-1]
    left = left_ref[...]
    width = out.shape[1]
    block = 512
    for first in range(0, width, block):
        columns = slice(first, first + block)
        right = jnp.concatenate([grad[:, columns] for grad in grads], 0)
        out[:, columns] = matmul_tn(left, right).astype(BF16)


def rows_grad(left, grads):
    return pl.pallas_call(
        functools.partial(rows_grad_kernel, len(grads)),
        out_shape=shape_of((left.shape[1], grads[0].shape[1])),
        in_specs=[VMEM] * (1 + len(grads)),
        out_specs=VMEM,
        compiler_params=params(),
        cost_estimate=cost(2 * left.size * grads[0].shape[1], left.size * 2),
        name="rows_grad",
    )(left, *grads)


def weight_copies(planes, chips, gu_ref, gu, sem):
    rows = gu.shape[1] // (planes * chips)
    return [
        pltpu.make_async_copy(
            gu_ref.at[chip, side, pl.ds(plane * rows, rows), :],
            gu.at[side, pl.ds((plane * chips + chip) * rows, rows), :],
            sem.at[side],
        )
        for side in range(2)
        for chip in range(chips)
        for plane in range(planes)
    ]


def feed_kernel(planes, chips, x_mine, x_other, g_mine, g_other, gu_ref, down_ref, *refs):
    (hidden_ref, gate_ref, up_ref, out_mine, out_other, dx_mine, dx_other, gu, down, sem) = refs
    rows = x_mine.shape[0]
    copies = weight_copies(planes, chips, gu_ref, gu, sem)
    down_copy = pltpu.make_async_copy(down_ref, down, sem.at[2])
    half = len(copies) // 2
    for copy in copies:
        copy.start()
    down_copy.start()
    x = jnp.concatenate([x_mine[...], x_other[...]], 0)
    grad = jnp.concatenate([g_mine[...], g_other[...]], 0)
    for copy in copies[:half]:
        copy.wait()
    gate = matmul(x, gu[0])
    for copy in copies[half:]:
        copy.wait()
    up = matmul(x, gu[1])
    down_copy.wait()
    dhidden = matmul_nt(grad, down[...])
    sigmoid = 1.0 / (1.0 + jnp.exp(-gate))
    hidden = (gate * sigmoid * up).astype(BF16)
    dgate = (dhidden * up * sigmoid * (1.0 + gate * (1.0 - sigmoid))).astype(BF16)
    dup = (dhidden * gate * sigmoid).astype(BF16)
    hidden_ref[...] = hidden
    gate_ref[...] = dgate
    up_ref[...] = dup
    block = 512
    for first in range(0, x.shape[1], block):
        columns = slice(first, first + block)
        dx = matmul_nt(dgate, gu[0, columns, :]) + matmul_nt(dup, gu[1, columns, :])
        dx_mine[:, columns] = dx[:rows, :]
        dx_other[:, columns] = dx[rows:, :].astype(BF16)
    for first in range(0, x.shape[1], block):
        columns = slice(first, first + block)
        out = matmul(hidden, down[:, columns])
        out_mine[:, columns] = out[:rows, :]
        out_other[:, columns] = out[rows:, :].astype(BF16)


def feed(planes, chips, x, grad, w_gate_up, w_down):
    rows, width = x[0].shape
    units = w_down.shape[0]
    part = shape_of((2 * rows, units))
    return pl.pallas_call(
        functools.partial(feed_kernel, planes, chips),
        out_shape=(part,) * 3 + (shape_of((rows, width), F32), shape_of((rows, width))) * 2,
        in_specs=[VMEM] * 4 + [ANY] * 2,
        out_specs=(VMEM,) * 7,
        scratch_shapes=[
            pltpu.VMEM((2, width, units), BF16),
            pltpu.VMEM((units, width), BF16),
            pltpu.SemaphoreType.DMA((3,)),
        ],
        compiler_params=params(),
        cost_estimate=cost(24 * rows * width * units, 6 * width * units, 2 * rows * units),
        name="feed",
    )(*x, *grad, w_gate_up, w_down)


def feed_grad_kernel(planes, chips, count, *refs):
    x, refs = refs[:count], refs[count:]
    gates, refs = refs[: count // 2], refs[count // 2 :]
    ups, refs = refs[: count // 2], refs[count // 2 :]
    out, held, sem = refs
    width = held.shape[1]
    block = 256
    rows = width // (planes * chips)
    copies = []
    dgate = jnp.concatenate([gate[...] for gate in gates], 0)
    dup = jnp.concatenate([up[...] for up in ups], 0)
    for first in range(0, width, block):
        columns = slice(first, first + block)
        left = jnp.concatenate([part[:, columns] for part in x], 0)
        held[0, columns, :] = matmul_tn(left, dgate).astype(BF16)
        held[1, columns, :] = matmul_tn(left, dup).astype(BF16)
        for at in range(first // rows, (first + block) // rows):
            for side in range(2):
                copy = pltpu.make_async_copy(
                    held.at[side, pl.ds(at * rows, rows), :],
                    out.at[at % chips, side, pl.ds(at // chips * rows, rows), :],
                    sem,
                )
                copy.start()
                copies.append(copy)
    for copy in copies:
        copy.wait()


def feed_grad(planes, chips, x, gates, ups):
    width, units = x[0].shape[1], gates[0].shape[1]
    tokens = x[0].shape[0] * len(x)
    return pl.pallas_call(
        functools.partial(feed_grad_kernel, planes, chips, len(x)),
        out_shape=shape_of((chips, 2, width // chips, units)),
        in_specs=[VMEM] * (len(x) + len(gates) + len(ups)),
        out_specs=ANY,
        scratch_shapes=[pltpu.VMEM((2, width, units), BF16), pltpu.SemaphoreType.DMA],
        compiler_params=params(),
        cost_estimate=cost(4 * tokens * width * units, 4 * width * units),
        name="feed_grad",
    )(*x, *gates, *ups)


def feed_adam_kernel(planes, chips, piece, place, *refs):
    blocks, refs = refs[:planes], refs[planes:]
    ins, outs = refs[:6], refs[6:12]
    held = refs[12]
    plane, core = place[0], place[2]
    for step in range(planes):
        for side in range(2):
            held[plane ^ step, core ^ side] = blocks[step][side].astype(F32)
    for part in range(2):
        w, m, u = ins[3 * part : 3 * part + 3]
        new = outs[3 * part : 3 * part + 3]
        for to in range(2 * planes):
            grad_block = held[to // 2, to % 2, part]
            for c in range(chips):
                at = ((to // 2 * chips + c) * 2 + to % 2) * piece
                columns = slice(at, at + piece)
                grad = grad_block[:, c * piece : (c + 1) * piece]
                updated = adam_step(w[:, columns], m[:, columns], u[:, columns], grad, 0.02)
                for out, value in zip(new, updated):
                    out[:, columns] = value


def feed_adam(place, planes, chips, blocks, arrays):
    rows, hidden = arrays[0].shape
    piece = hidden // (2 * planes * chips)
    tile = min(rows, 16)
    whole = pl.BlockSpec((tile, hidden), lambda i: (i, 0))
    block = pl.BlockSpec((2, 2, tile, piece * chips), lambda i: (0, 0, i, 0))
    return pl.pallas_call(
        functools.partial(feed_adam_kernel, planes, chips, piece),
        grid=(rows // tile,),
        out_shape=(shape_of((rows, hidden), F32),) * 6,
        in_specs=[SMEM] + [block] * planes + [whole] * 6,
        out_specs=(whole,) * 6,
        scratch_shapes=[pltpu.VMEM((planes, 2, 2, tile, piece * chips), F32)],
        compiler_params=params(),
        cost_estimate=cost(40 * rows * hidden, 52 * rows * hidden),
        name="feed_adam",
    )(place, *blocks, *arrays)


def segment_starts(lengths_row, length):
    count = lengths_row.shape[0]
    ahead = jnp.arange(count)[:, None] < jnp.arange(count)[None, :]
    starts = jnp.sum(jnp.where(ahead, lengths_row[:, None], 0), 0, dtype=jnp.int32)
    ends = starts + lengths_row
    places = jnp.arange(length, dtype=jnp.int32)
    within = (places[:, None] >= starts[None, :]) & (places[:, None] < ends[None, :])
    return jnp.sum(jnp.where(within, starts[None, :], 0), 1, dtype=jnp.int32)


def rope_tables(positions):
    half = HEAD_DIM // 2
    freqs = jnp.exp(jnp.arange(half, dtype=F32) * (-2.0 * math.log(ROPE_BASE) / HEAD_DIM))
    angles = positions.astype(F32)[:, None] * freqs[None, :]
    cosine = jnp.cos(angles)
    sine = jnp.sin(angles)
    return (
        jnp.concatenate([cosine] * 4, 1),
        jnp.concatenate([-sine, sine, -sine, sine], 1),
    )


def local(
    tokens,
    out_grad,
    seq_lengths,
    query_weight,
    query_first,
    query_second,
    key_weight,
    key_first,
    key_second,
    value_weight,
    value_first,
    value_second,
    output_weight,
    output_first,
    output_second,
    gate_weight,
    gate_first,
    gate_second,
    up_weight,
    up_first,
    up_second,
    down_weight,
    down_first,
    down_second,
    norm_gains,
    gains_first,
    gains_second,
):
    planes = lax.axis_size("dp")
    members = lax.axis_size("fsdp")
    chips = members // 2
    plane = lax.axis_index("dp")
    index = lax.axis_index("fsdp")
    chip = index // 2
    core = index % 2
    place = jnp.stack([plane, chip, core]).astype(jnp.int32)
    spot = jnp.stack([plane, index]).astype(jnp.int32)
    count, width = tokens.shape
    length = count * members
    slice_rows = query_weight.shape[0]
    own_q = query_weight.shape[1] // members
    sharing = members // KV_HEADS
    same_core = [list(range(c, members, 2)) for c in range(2)]

    def chip_all(own, size):
        return gather(own, chip_send, size)

    def plane_all(own, size):
        return gather_line(own, plane_send, size)

    gu_mine, gu_other, qkv_mine, qkv_other = pack(
        place, planes, chips, gate_weight, up_weight, query_weight, key_weight, value_weight
    )
    tokens_all = gather_cores(tokens, chip_all, chips)
    qkv_rows = gather_rows(chip, core, exchange(qkv_mine, qkv_other, chip_send))
    gate_up_rows = gather_rows(plane, core, exchange(gu_mine, gu_other, plane_send))
    w_down = lax.all_gather(
        down_weight.astype(BF16), "fsdp", axis=0, tiled=True, axis_index_groups=same_core
    )
    gate_up_rows, w_down = lax.optimization_barrier((gate_up_rows, w_down))
    w_gate_up = lax.all_gather(
        gate_up_rows, "fsdp", axis=0, tiled=False, axis_index_groups=same_core
    )
    w_qkv = plane_all(qkv_rows, planes)

    gains = norm_gains.astype(BF16).astype(F32)
    gains = by_offset(jnp.stack(gather(gains, plane_send, planes)), plane)
    gains = jnp.stack(gather_cores(gains, chip_all, chips))
    gains = jnp.transpose(by_offset(gains, index), (2, 1, 0, 3)).reshape(2, width)

    start = segment_starts(seq_lengths[0], length)
    cosine, sine = rope_tables(jnp.arange(length, dtype=jnp.int32) - start)

    hop = members // planes
    out_rows = jnp.stack(plane_all(output_weight.astype(BF16), planes))
    own_plane = index // hop

    def out_route(turn_no):
        return [(i, ((turn_no + i) % planes) * hop + i // planes) for i in range(members)]

    w_output = jnp.zeros((planes, slice_rows, width), BF16)
    for turn_no in range(planes):
        sent = lax.dynamic_index_in_dim(
            out_rows, ((turn_no + index) % planes) ^ plane, 0, keepdims=False
        )
        got = lax.ppermute(sent, "fsdp", out_route(turn_no))
        spare = (own_plane + planes - turn_no) % planes
        w_output = lax.dynamic_update_index_in_dim(w_output, got, spare, 0)
    w_output = w_output.reshape(planes * slice_rows, width)
    out_grad_all = gather_cores(out_grad, plane_all, planes)

    normed, queries, keys_values, attended = attend(
        spot, tokens_all, w_qkv, gains[:1], start[:, None], cosine, sine
    )
    own_tokens = tokens.astype(F32)
    resid = own_tokens + scatter_cores(*project(attended, w_output, chips), chip_send)
    scale_two = rms_scale(resid)
    own_normed_two = (resid * scale_two * gains[1]).astype(BF16)

    normed_two = gather_cores(own_normed_two, plane_all, planes)
    fed = [
        feed(
            planes,
            chips,
            normed_two[2 * step : 2 * step + 2],
            out_grad_all[2 * step : 2 * step + 2],
            w_gate_up,
            w_down,
        )
        for step in range(planes)
    ]
    hidden, grad_gate, grad_up, out_mine, out_other, dx_mine, dx_other = zip(*fed)
    grad_normed_two = scatter_cores(dx_mine, dx_other, plane_send)
    weighted_two = grad_normed_two * gains[1]
    grad_gain_two = jnp.sum(grad_normed_two * resid * scale_two, 0)
    grad_resid = (
        out_grad.astype(F32)
        + scale_two * weighted_two
        - resid
        * (scale_two * scale_two * scale_two)
        * jnp.mean(weighted_two * resid, -1, keepdims=True)
    )
    grad_attn_out = gather_cores(grad_resid.astype(BF16), chip_all, chips)

    grad_gate_up = feed_grad(planes, chips, normed_two, grad_gate, grad_up)
    grad_gate_up = lax.psum_scatter(
        grad_gate_up, "fsdp", scatter_dimension=0, tiled=False, axis_index_groups=same_core
    )
    grad_down = rows_grad(jnp.concatenate(hidden), out_grad_all)
    grad_down, grad_gate_up = lax.optimization_barrier((grad_down, grad_gate_up))
    grad_down_weight = lax.psum_scatter(
        grad_down, "fsdp", scatter_dimension=0, tiled=True, axis_index_groups=same_core
    ).astype(F32)
    grad_gate_up = exchange(*spread_rows(plane, core, grad_gate_up, planes), plane_send)

    grad_qkv = attend_back(
        spot, queries, keys_values, w_output, grad_attn_out, start[None, :], cosine, sine
    )
    grad_normed = scatter_cores(*project_back(spot, grad_qkv, w_qkv, chips), chip_send)
    scale_one = rms_scale(own_tokens)
    weighted_one = grad_normed * gains[0]
    grad_gain_one = jnp.sum(grad_normed * own_tokens * scale_one, 0)
    grad_tokens = (
        grad_resid
        + scale_one * weighted_one
        - own_tokens
        * (scale_one * scale_one * scale_one)
        * jnp.mean(weighted_one * own_tokens, -1, keepdims=True)
    )
    out_mine, _ = lax.optimization_barrier((out_mine, grad_attn_out[0]))
    result = resid + scatter_cores(out_mine, out_other, plane_send)

    grad_output = rows_grad(attended, grad_attn_out).reshape(planes, slice_rows, width)
    out_parts = jnp.zeros((planes, slice_rows, width), BF16)
    for turn_no in range(planes):
        spare = (own_plane + planes - turn_no) % planes
        sent = lax.dynamic_index_in_dim(grad_output, spare, 0, keepdims=False)
        got = lax.ppermute(sent, "fsdp", [(b, a) for a, b in out_route(turn_no)])
        out_parts = lax.dynamic_update_index_in_dim(
            out_parts, got, ((turn_no + index) % planes) ^ plane, 0
        )
    grad_output_weight = scatter_sum([out_parts[step] for step in range(planes)], plane_send)

    grad_w_qkv = scatter_sum(qkv_grad(spot, normed, grad_qkv, planes), plane_send)
    got = exchange(*spread_rows(chip, core, grad_w_qkv, chips), chip_send)
    got = by_offset(jnp.concatenate(got), index).astype(F32)
    got = jnp.transpose(got, (1, 0, 2))
    grad_query_weight = got[:, :, :own_q].reshape(slice_rows, -1)
    grad_kv = got[:, :, own_q:].reshape(slice_rows, KV_HEADS, sharing, PAIR).sum(2)
    grad_key_weight = grad_kv[:, :, :HEAD_DIM].reshape(slice_rows, -1)
    grad_value_weight = grad_kv[:, :, HEAD_DIM:].reshape(slice_rows, -1)

    gain_grads = jnp.stack([grad_gain_one, grad_gain_two]).reshape(2, planes, members, -1)
    gain_grads = by_offset(jnp.transpose(gain_grads, (2, 1, 0, 3)), index)
    gain_grads = gain_grads.reshape((chips, 2) + gain_grads.shape[1:])
    gain_grads = gain_grads[:, 0] + core_swap(gain_grads[:, 1])
    gain_grads = gain_grads[0] + sum(chip_send(gain_grads[s], s) for s in range(1, chips))
    gain_grads = by_offset(gain_grads, plane)
    gain_grads = gain_grads[0] + sum(plane_send(gain_grads[s], s) for s in range(1, planes))

    updated = (
        adam_step(query_weight, query_first, query_second, grad_query_weight, 0.02)
        + adam_step(key_weight, key_first, key_second, grad_key_weight, 0.02)
        + adam_step(value_weight, value_first, value_second, grad_value_weight, 0.02)
        + adam_step(output_weight, output_first, output_second, grad_output_weight, 0.1)
        + tuple(
            feed_adam(
                place,
                planes,
                chips,
                grad_gate_up,
                (gate_weight, gate_first, gate_second, up_weight, up_first, up_second),
            )
        )
        + adam_step(down_weight, down_first, down_second, grad_down_weight, 0.02)
        + adam_step(norm_gains, gains_first, gains_second, gain_grads, 0.2)
    )
    return (result.astype(BF16), grad_tokens) + updated


def solution(mesh):
    rows = P(("dp", "fsdp"), None)
    columns = P(None, ("dp", "fsdp"))
    in_specs = (rows, rows, P("dp", None)) + (rows,) * 21 + (columns,) * 3
    out_specs = (rows, rows) + (rows,) * 21 + (columns,) * 3
    return jax.shard_map(local, mesh=mesh, in_specs=in_specs, out_specs=out_specs, check_vma=False)
```

```python
import functools
import math

import jax
import jax.numpy as jnp
from jax import lax
from jax.experimental import pallas as pl
from jax.experimental.pallas import tpu as pltpu
from jax.sharding import PartitionSpec as P

HEADS = 32
KV_HEADS = 4
HEAD_DIM = 64
STEP = 3

NORM_EPS = 1e-05
ROPE_BASE = 10000.0
BETA = 0.5
ADAM_EPS = 1e-08
DECAY = 0.1
MASKED = -1e30
PAIR = 2 * HEAD_DIM
BF16 = jnp.bfloat16
F32 = jnp.float32


def matmul(left, right):
    return jnp.dot(left, right, preferred_element_type=F32)


def matmul_tn(left, right):
    return lax.dot_general(left, right, (((0,), (0,)), ((), ())), preferred_element_type=F32)


def matmul_nt(left, right):
    return lax.dot_general(left, right, (((1,), (1,)), ((), ())), preferred_element_type=F32)


def rms_scale(values):
    return lax.rsqrt(jnp.mean(values * values, -1, keepdims=True) + NORM_EPS)


def adam_step(master, first_moment, second_moment, gradient, rate):
    first_new = BETA * first_moment + (1.0 - BETA) * gradient
    second_new = BETA * second_moment + (1.0 - BETA) * gradient * gradient
    correction = 1.0 - BETA**STEP
    master_new = master - rate * (
        first_new / correction / (jnp.sqrt(second_new / correction) + ADAM_EPS) + DECAY * master
    )
    return (master_new, first_new, second_new)


def core_swap(value):
    members = lax.axis_size("fsdp")
    return lax.ppermute(value, "fsdp", [(i, i ^ 1) for i in range(members)])


def chip_send(value, step):
    members = lax.axis_size("fsdp")
    return lax.ppermute(value, "fsdp", [(i, i ^ (2 * step)) for i in range(members)])


def plane_send(value, step):
    planes = lax.axis_size("dp")
    return lax.ppermute(value, "dp", [(i, i ^ step) for i in range(planes)])


def gather(own, send, count):
    return [own] + [send(own, step) for step in range(1, count)]


def ones(step):
    return step.bit_count()


def gather_stage(got, send, count, stage):
    more = {j: send(got[j & (j - 1)], j & -j) for j in range(count) if ones(j) == stage}
    return {**got, **more}


def scatter_stage(parts, send, stage):
    parts = dict(parts)
    for j in sorted(parts, reverse=True):
        if ones(j) == stage:
            got = send(parts.pop(j).astype(BF16), j & -j)
            parts[j & (j - 1)] = parts[j & (j - 1)].astype(F32) + got.astype(F32)
    return parts


def gather_terms(parts, send):
    return [parts[0]] + [send(parts[step], step) for step in range(1, len(parts))]


def scatter_sum(parts, send):
    return sum(part.astype(F32) for part in gather_terms(parts, send))


def together(*values):
    return lax.optimization_barrier(values)


def swap_pairs(mine, other):
    got = core_swap(other)
    return [jnp.stack([mine[step], got[step]]) for step in range(mine.shape[0])]


def exchange(pairs, send):
    return pairs[:1] + [send(pairs[step], step) for step in range(1, len(pairs))]


def by_offset(blocks, index):
    count = blocks.shape[0]
    return jnp.stack(
        [lax.dynamic_index_in_dim(blocks, j ^ index, 0, keepdims=False) for j in range(count)]
    )


def lane_ids(shape):
    return lax.broadcasted_iota(jnp.int32, shape, len(shape) - 1)


def turn(values, cosine, sine):
    low_half = lane_ids(values.shape) % HEAD_DIM < HEAD_DIM // 2
    shifted = jnp.where(
        low_half,
        pltpu.roll(values, PAIR - HEAD_DIM // 2, 1),
        pltpu.roll(values, HEAD_DIM // 2, 1),
    )
    return values * cosine + shifted * sine


VMEM = pl.BlockSpec(memory_space=pltpu.VMEM)
SMEM = pl.BlockSpec(memory_space=pltpu.SMEM)
ANY = pl.BlockSpec(memory_space=pl.ANY)


def params(mib=56):
    return pltpu.CompilerParams(vmem_limit_bytes=mib * 2**20)


def shape_of(shape, dtype=BF16):
    return jax.ShapeDtypeStruct(shape, dtype)


def cost(flops, moved, exps=0):
    return pl.CostEstimate(flops=int(flops), bytes_accessed=int(moved), transcendentals=int(exps))


def whole_lanes(width):
    return -(-width // 128) * 128


def head_order(planes, members):
    chips = members // 2
    if HEADS == planes * members and planes == chips:
        return [
            [f // 2 * members + 2 * ((f // 2) ^ step) + f % 2 for step in range(chips)]
            for f in range(members)
        ]
    share = HEADS // members
    return [list(range(f * share, (f + 1) * share)) for f in range(members)]


def pack_kernel(planes, chips, piece, place, gains, gate, up, query, key, value, *outs):
    gu_mine, gu_other, qkv_mine, qkv_other = outs
    plane, chip, core = place[0], place[1], place[2]
    sharing = 2 * chips // KV_HEADS
    heads = head_order(planes, 2 * chips)

    def put(mine, other, core_to, index, block):
        @pl.when(core == core_to)
        def _():
            mine[index] = block

        @pl.when(core != core_to)
        def _():
            other[index] = block

    def rounded(block, row):
        return (block.astype(BF16).astype(F32) * gains[:, row : row + 1]).astype(BF16)

    for to in range(2 * chips):
        head = slice(to // sharing * HEAD_DIM, (to // sharing + 1) * HEAD_DIM)
        columns = [query[:, h * HEAD_DIM : (h + 1) * HEAD_DIM] for h in heads[to]]
        block = jnp.concatenate(columns + [key[:, head], value[:, head]], 1)
        put(qkv_mine, qkv_other, to % 2, (to // 2) ^ chip, rounded(block, 0))
    for side, weight in enumerate((gate, up)):
        for to in range(2 * planes):
            starts = [((to // 2 * chips + c) * 2 + to % 2) * piece for c in range(chips)]
            columns = [weight[:, s : s + piece] for s in starts]
            spare = gu_mine.shape[-1] - chips * piece
            if spare:
                columns.append(jnp.zeros((weight.shape[0], spare), F32))
            block = rounded(jnp.concatenate(columns, 1), 1)
            put(gu_mine.at[:, side], gu_other.at[:, side], to % 2, (to // 2) ^ plane, block)


def whole_lanes(width):
    return -(-width // 128) * 128


def pack(place, planes, chips, gains, gate, up, query, key, value):
    rows, hidden = gate.shape
    gu = shape_of((planes, 2, rows, whole_lanes(hidden // (2 * planes))))
    qkv = shape_of((chips, rows, query.shape[1] // (2 * chips) + PAIR))
    return pl.pallas_call(
        functools.partial(pack_kernel, planes, chips, hidden // (2 * planes * chips)),
        out_shape=(gu, gu, qkv, qkv),
        in_specs=[SMEM] + [VMEM] * 6,
        out_specs=(VMEM,) * 4,
        compiler_params=params(),
        cost_estimate=cost(0, rows * hidden * 12),
        name="pack",
    )(place, gains, gate, up, query, key, value)


def gather_rows_kernel(members, place, *refs):
    blocks, out = refs[:-1], refs[-1]
    first, core = place[0], place[1]
    rows = blocks[0].shape[-2]
    for step, block in enumerate(blocks):
        for side in range(2):
            at = ((first ^ step) * 2 + (core ^ side)) * rows
            if len(block.shape) == 3:
                out[pl.ds(pl.multiple_of(at, 16), rows), :] = block[side]
            else:
                for part in range(2):
                    out[part, pl.ds(pl.multiple_of(at, 16), rows), :] = block[side, part]


def gather_rows(first, core, pairs):
    lead, (rows, width) = pairs[0].shape[1:-2], pairs[0].shape[-2:]
    return pl.pallas_call(
        functools.partial(gather_rows_kernel, 2 * len(pairs)),
        out_shape=shape_of(lead + (2 * len(pairs) * rows, width)),
        in_specs=[SMEM] + [VMEM] * len(pairs),
        out_specs=VMEM,
        compiler_params=params(),
        cost_estimate=cost(0, pairs[0].size * len(pairs) * 4),
        name="gather_rows",
    )(jnp.stack([first, core]), *pairs)


def spread_rows_kernel(place, *refs):
    terms, (mine, other) = refs[:-2], refs[-2:]
    first, core = place[0], place[1]
    count = mine.shape[0]
    rows = mine.shape[-2]
    for step in range(count):
        for side, out in enumerate((mine, other)):
            at = pl.ds(pl.multiple_of(((first ^ step) * 2 + (core ^ side)) * rows, 16), rows)
            if len(mine.shape) == 3:
                out[step] = sum(t[at, :].astype(F32) for t in terms).astype(BF16)
            else:
                for part in range(2):
                    out[step, part] = sum(t[part, at, :].astype(F32) for t in terms).astype(BF16)


def spread_rows(first, core, terms, count):
    whole = terms[0]
    rows = whole.shape[-2] // (2 * count)
    out = shape_of((count,) + whole.shape[:-2] + (rows, whole.shape[-1]))
    return pl.pallas_call(
        spread_rows_kernel,
        out_shape=(out, out),
        in_specs=[SMEM] + [VMEM] * len(terms),
        out_specs=(VMEM, VMEM),
        compiler_params=params(),
        cost_estimate=cost(0, whole.size * 6),
        name="spread_rows",
    )(jnp.stack([first, core]), *terms)


def attend_kernel(members, pairs, planes, place, start_ref, cos_ref, sin_ref, *refs):
    tokens, refs = refs[:2], refs[2:]
    weights, refs = refs[:planes], refs[planes:]
    normed_ref, q_ref, kv_ref, o_ref = refs
    plane, index = place[0], place[1]
    rows = tokens[0].shape[1]
    length = rows * members
    even = lane_ids((rows, PAIR)) < HEAD_DIM
    depth = weights[0].shape[0]
    for j in range(members):
        values = tokens[j % 2][j // 2].astype(F32)
        normed_ref[j * rows : (j + 1) * rows, :] = (values * rms_scale(values)).astype(BF16)
    block = min(2 * rows, 256)
    per = block // rows
    for first in range(0, length, block):
        qkv = None
        for step in range(planes):
            columns = pl.ds(pl.multiple_of((plane ^ step) * depth, 128), depth)
            term = matmul(normed_ref[first : first + block, columns], weights[step][...])
            qkv = term if qkv is None else qkv + term
        for part in range(per):
            j = first // rows + part
            here = pl.ds(pl.multiple_of((j ^ index) * rows, rows), rows)
            cosine = cos_ref[here, :]
            sine = sin_ref[here, :]
            piece = qkv[part * rows : (part + 1) * rows, :]
            for pair in range(pairs):
                lanes = slice(pair * PAIR, (pair + 1) * PAIR)
                turned = turn(piece[:, lanes], cosine, sine).astype(BF16).astype(F32)
                q_ref[here, lanes] = (turned * HEAD_DIM**-0.5).astype(BF16)
            both = piece[:, pairs * PAIR :]
            kv_ref[here, :] = jnp.where(even, turn(both, cosine, sine), both).astype(BF16)
    for first in range(0, length, block):
        reach = first + block
        both = kv_ref[:reach, :].astype(F32)
        left = lane_ids(both.shape) < HEAD_DIM
        keys_even = jnp.where(left, both, 0.0)
        values_odd = jnp.where(left, 0.0, both)
        keys = (keys_even.astype(BF16), pltpu.roll(keys_even, HEAD_DIM, 1).astype(BF16))
        values = (pltpu.roll(values_odd, HEAD_DIM, 1).astype(BF16), values_odd.astype(BF16))
        query_at = first + lax.broadcasted_iota(jnp.int32, (block, reach), 0)
        key_at = lax.broadcasted_iota(jnp.int32, (block, reach), 1)
        allowed = (key_at <= query_at) & (key_at >= start_ref[first:reach, :])
        for pair in range(pairs):
            lanes = slice(pair * PAIR, (pair + 1) * PAIR)
            query = q_ref[first:reach, lanes]
            mixed = jnp.zeros((block, PAIR), F32)
            for side in range(2):
                scores = jnp.where(allowed, matmul_nt(query, keys[side]), MASKED)
                raised = jnp.exp(scores - jnp.max(scores, -1, keepdims=True))
                probs = raised * (1.0 / jnp.sum(raised, -1, keepdims=True))
                mixed = mixed + matmul(probs.astype(BF16), values[side])
            mixed = mixed.astype(BF16)
            for part in range(per):
                j = first // rows + part
                there = pl.ds(pl.multiple_of((j ^ index) * rows, rows), rows)
                o_ref[there, lanes] = mixed[part * rows : (part + 1) * rows, :]


def attend(place, mine, other, weights, start, cosine, sine):
    members, planes = 2 * mine.shape[0], len(weights)
    rows, width = mine.shape[1:]
    length = members * rows
    pairs = weights[0].shape[1] // PAIR - 1
    return pl.pallas_call(
        functools.partial(attend_kernel, members, pairs, planes),
        out_shape=(
            shape_of((length, width)),
            shape_of((length, pairs * PAIR)),
            shape_of((length, PAIR)),
            shape_of((length, pairs * PAIR)),
        ),
        in_specs=[SMEM] + [VMEM] * (5 + planes),
        out_specs=(VMEM,) * 4,
        compiler_params=params(),
        cost_estimate=cost(
            2 * length * width * (pairs + 1) * PAIR + 3 * length * length * pairs * PAIR,
            length * width * 4,
            length * length * pairs,
        ),
        name="attend",
    )(place, start, cosine, sine, mine, other, *weights)


def attend_back_kernel(members, pairs, place, start_ref, cos_ref, sin_ref, q_ref, kv_ref, w_ref, *refs):
    grads, refs = refs[:members], refs[members:]
    out_ref, do_ref, dk_ref, dv_ref = refs
    length = q_ref.shape[0]
    rows = length // members
    index = place[1]
    block = min(2 * rows, 256)
    per = block // rows
    for j in range(0, members, 2):
        grad = jnp.concatenate([grads[j][...], grads[j + 1][...]], 0)
        do_ref[j * rows : (j + 2) * rows, :] = matmul_nt(grad, w_ref[...]).astype(BF16)
    dk_ref[...] = jnp.zeros_like(dk_ref)
    dv_ref[...] = jnp.zeros_like(dv_ref)
    for first in range(0, length, block):
        reach = first + block
        both = kv_ref[:reach, :].astype(F32)
        left = lane_ids(both.shape) < HEAD_DIM
        keys_even = jnp.where(left, both, 0.0)
        values_odd = jnp.where(left, 0.0, both)
        keys = (keys_even.astype(BF16), pltpu.roll(keys_even, HEAD_DIM, 1).astype(BF16))
        values = (pltpu.roll(values_odd, HEAD_DIM, 1).astype(BF16), values_odd.astype(BF16))
        key_at = lax.broadcasted_iota(jnp.int32, (reach, block), 0)
        query_at = first + lax.broadcasted_iota(jnp.int32, (reach, block), 1)
        allowed = (key_at <= query_at) & (key_at >= start_ref[:, first:reach])
        half = lane_ids((block, PAIR)) < HEAD_DIM
        theres = [
            pl.ds(pl.multiple_of(((first // rows + part) ^ index) * rows, rows), rows)
            for part in range(per)
        ]
        for pair in range(pairs):
            lanes = slice(pair * PAIR, (pair + 1) * PAIR)
            query = q_ref[first:reach, lanes]
            grad = jnp.concatenate([do_ref[there, lanes] for there in theres], 0)
            dq = jnp.zeros((block, PAIR), F32)
            for side in range(2):
                keep = half if side == 0 else ~half
                query_side = jnp.where(keep, query.astype(F32), 0.0).astype(BF16)
                grad_side = jnp.where(keep, grad.astype(F32), 0.0).astype(BF16)
                scores = jnp.where(allowed, matmul_nt(keys[side], query), MASKED)
                raised = jnp.exp(scores - jnp.max(scores, 0, keepdims=True))
                probs = raised * (1.0 / jnp.sum(raised, 0, keepdims=True))
                dp = matmul_nt(values[side], grad)
                centre = jnp.sum(probs * dp, 0, keepdims=True)
                ds = (probs * (dp - centre)).astype(BF16)
                dv_ref[:reach, :] += matmul(probs.astype(BF16), grad_side)
                dk_ref[:reach, :] += matmul(ds, query_side)
                dq = dq + matmul_tn(ds, keys[side])
            dq = dq * HEAD_DIM**-0.5
            for part in range(per):
                piece = dq[part * rows : (part + 1) * rows, :]
                here = slice(first + part * rows, first + (part + 1) * rows)
                out_ref[theres[part], lanes] = turn(
                    piece, cos_ref[here, :], -sin_ref[here, :]
                ).astype(BF16)
    left = lane_ids((rows, PAIR)) < HEAD_DIM
    for j in range(members):
        here = slice(j * rows, (j + 1) * rows)
        there = pl.ds(pl.multiple_of((j ^ index) * rows, rows), rows)
        dk = dk_ref[here, :]
        dv = dv_ref[here, :]
        dk = turn(dk + pltpu.roll(dk, HEAD_DIM, 1), cos_ref[here, :], -sin_ref[here, :])
        dv = dv + pltpu.roll(dv, HEAD_DIM, 1)
        out_ref[there, pairs * PAIR :] = jnp.where(left, dk, dv).astype(BF16)


def attend_back(place, queries, keys_values, w_output, grads, start, cosine, sine):
    length, width = queries.shape
    pairs = width // PAIR
    members = len(grads)
    model = grads[0].shape[1]
    return pl.pallas_call(
        functools.partial(attend_back_kernel, members, pairs),
        out_shape=shape_of((length, width + PAIR)),
        in_specs=[SMEM] + [VMEM] * (6 + members),
        out_specs=VMEM,
        scratch_shapes=[
            pltpu.VMEM((length, width), BF16),
            pltpu.VMEM((length, PAIR), F32),
            pltpu.VMEM((length, PAIR), F32),
        ],
        compiler_params=params(),
        cost_estimate=cost(
            2 * length * width * model + 7 * length * length * width,
            length * model * 2,
            length * length * pairs,
        ),
        name="attend_back",
    )(place, start, cosine, sine, queries, keys_values, w_output, *grads)


def project_kernel(count, left_ref, weight_ref, *outs):
    rows = left_ref.shape[0] // (2 * count)
    for step in range(count):
        whole = matmul(left_ref[2 * step * rows : 2 * (step + 1) * rows, :], weight_ref[...])
        outs[step][...] = whole[:rows, :]
        outs[count + step][...] = whole[rows:, :].astype(BF16)


def project(left, weight, count):
    rows, width = left.shape[0] // (2 * count), weight.shape[1]
    outs = pl.pallas_call(
        functools.partial(project_kernel, count),
        out_shape=(shape_of((rows, width), F32),) * count + (shape_of((rows, width)),) * count,
        in_specs=[VMEM, VMEM],
        out_specs=(VMEM,) * (2 * count),
        compiler_params=params(),
        cost_estimate=cost(2 * left.size * width, left.shape[0] * width * 3),
        name="project",
    )(left, weight)
    return outs[:count], outs[count:]


def project_back_kernel(planes, count, place, left_ref, *refs):
    weights, outs = refs[:planes], refs[planes:]
    rows = left_ref.shape[0] // (2 * count)
    depth = weights[0].shape[0]
    for step in range(count):
        left = left_ref[2 * step * rows : 2 * (step + 1) * rows, :]
        for far in range(planes):
            columns = pl.ds(pl.multiple_of((place[0] ^ far) * depth, 128), depth)
            whole = matmul_nt(left, weights[far][...])
            outs[step][:, columns] = whole[:rows, :]
            outs[count + step][:, columns] = whole[rows:, :].astype(BF16)


def project_back(place, left, weights, count):
    rows, planes = left.shape[0] // (2 * count), len(weights)
    width = weights[0].shape[0] * planes
    outs = pl.pallas_call(
        functools.partial(project_back_kernel, planes, count),
        out_shape=(shape_of((rows, width), F32),) * count + (shape_of((rows, width)),) * count,
        in_specs=[SMEM] + [VMEM] * (1 + planes),
        out_specs=(VMEM,) * (2 * count),
        compiler_params=params(),
        cost_estimate=cost(2 * left.size * width, left.shape[0] * width * 3),
        name="project_back",
    )(place, left, *weights)
    return outs[:count], outs[count:]


def qkv_grad_kernel(place, normed_ref, grad_ref, *outs):
    depth = outs[0].shape[0]
    for far, out in enumerate(outs):
        columns = pl.ds(pl.multiple_of((place[0] ^ far) * depth, 128), depth)
        out[...] = matmul_tn(normed_ref[:, columns], grad_ref[...]).astype(BF16)


def qkv_grad(place, normed, grad, planes):
    depth, width = normed.shape[1] // planes, grad.shape[1]
    return pl.pallas_call(
        qkv_grad_kernel,
        out_shape=(shape_of((depth, width)),) * planes,
        in_specs=[SMEM, VMEM, VMEM],
        out_specs=(VMEM,) * planes,
        compiler_params=params(),
        cost_estimate=cost(2 * normed.size * width, normed.size * 2),
        name="qkv_grad",
    )(place, normed, grad)


def rows_grad_kernel(count, left_ref, *refs):
    grads, out = refs[:-1], refs[-1]
    left = left_ref[...]
    width = out.shape[1]
    block = 512
    for first in range(0, width, block):
        columns = slice(first, first + block)
        right = jnp.concatenate([grad[:, columns] for grad in grads], 0)
        out[:, columns] = matmul_tn(left, right).astype(BF16)


def rows_grad(left, grads):
    return pl.pallas_call(
        functools.partial(rows_grad_kernel, len(grads)),
        out_shape=shape_of((left.shape[1], grads[0].shape[1])),
        in_specs=[VMEM] * (1 + len(grads)),
        out_specs=VMEM,
        compiler_params=params(),
        cost_estimate=cost(2 * left.size * grads[0].shape[1], left.size * 2),
        name="rows_grad",
    )(left, *grads)


def weight_copies(place, planes, sides, gu, sem):
    chips = len(sides)
    rows = gu.shape[1] // (planes * chips)
    copies = []
    for side in range(2):
        for step, pair in enumerate(sides):
            for plane in range(planes):
                to = (plane * chips + (place[1] ^ step)) * rows
                copies.append(
                    pltpu.make_async_copy(
                        pair[side].at[pl.ds(plane * rows, rows), :],
                        gu.at[side, pl.ds(pl.multiple_of(to, 16), rows), :],
                        sem.at[side],
                    )
                )
    return copies


def feed_kernel(planes, layout, count, place, *refs):
    x, refs = refs[:count], refs[count:]
    grads, refs = refs[:count], refs[count:]
    blocks, refs = refs[: len(layout)], refs[len(layout) :]
    chips = 1 + max(step for step, _ in layout)
    sides = [[None, None] for _ in range(chips)]
    for (step, side), ref in zip(layout, blocks):
        for part in (0, 1) if side is None else (side,):
            sides[step][part] = ref.at[part] if side is None else ref
    down_ref, hidden_ref, gate_ref, up_ref = refs[:4]
    outs, refs = refs[4 : 4 + count], refs[4 + count :]
    dxs, refs = refs[:count], refs[count:]
    gu, down, sem = refs
    rows = x[0].shape[0]
    units = down.shape[0]
    copies = weight_copies(place, planes, sides, gu, sem)
    down_copy = pltpu.make_async_copy(down_ref, down, sem.at[2])
    half = len(copies) // 2
    for copy in copies:
        copy.start()
    down_copy.start()
    x = jnp.concatenate([part[...] for part in x], 0)
    grad = jnp.concatenate([part[...] for part in grads], 0)
    for copy in copies[:half]:
        copy.wait()
    gate = matmul(x, gu[0, :, :units])
    for copy in copies[half:]:
        copy.wait()
    up = matmul(x, gu[1, :, :units])
    down_copy.wait()
    dhidden = matmul_nt(grad, down[...])
    sigmoid = 1.0 / (1.0 + jnp.exp(-gate))
    hidden = (gate * sigmoid * up).astype(BF16)
    dgate = (dhidden * up * sigmoid * (1.0 + gate * (1.0 - sigmoid))).astype(BF16)
    dup = (dhidden * gate * sigmoid).astype(BF16)
    hidden_ref[...] = hidden
    gate_ref[...] = dgate
    up_ref[...] = dup
    block = 512
    for first in range(0, x.shape[1], block):
        columns = slice(first, first + block)
        dx = matmul_nt(dgate, gu[0, columns, :units]) + matmul_nt(dup, gu[1, columns, :units])
        for j in range(count):
            dxs[j][:, columns] = dx[j * rows : (j + 1) * rows, :].astype(dxs[j].dtype)
    for first in range(0, x.shape[1], block):
        columns = slice(first, first + block)
        out = matmul(hidden, down[:, columns])
        for j in range(count):
            outs[j][:, columns] = out[j * rows : (j + 1) * rows, :].astype(outs[j].dtype)


def feed(place, planes, x, grad, w_gate_up, w_down):
    layout, blocks = zip(*w_gate_up)
    rows, width = x[0].shape
    units = w_down.shape[0]
    count = len(x)
    part = shape_of((count * rows, units))
    terms = (shape_of((rows, width), F32), shape_of((rows, width))) * (count // 2)
    got = pl.pallas_call(
        functools.partial(feed_kernel, planes, layout, count),
        out_shape=(part,) * 3 + terms * 2,
        in_specs=[SMEM] + [VMEM] * (2 * count) + [ANY] * (len(blocks) + 1),
        out_specs=(VMEM,) * (3 + 2 * count),
        scratch_shapes=[
            pltpu.VMEM((2, width, blocks[0].shape[-1]), BF16),
            pltpu.VMEM((units, width), BF16),
            pltpu.SemaphoreType.DMA((3,)),
        ],
        compiler_params=params(),
        cost_estimate=cost(12 * count * rows * width * units, 6 * width * units, rows * units),
        name="feed",
    )(place, *x, *grad, *blocks, w_down)
    return got[:3], got[3 : 3 + count], got[3 + count :]


def feed_grad_kernel(planes, chips, count, place, *refs):
    x, refs = refs[:count], refs[count:]
    gates, refs = refs[: count // 2], refs[count // 2 :]
    ups, refs = refs[: count // 2], refs[count // 2 :]
    outs, (held, sem) = refs[:-2], refs[-2:]
    width = held.shape[1]
    units = gates[0].shape[1]
    block = 256
    rows = width // (planes * chips)
    copies = []
    dgate = jnp.concatenate([gate[...] for gate in gates], 0)
    dup = jnp.concatenate([up[...] for up in ups], 0)
    if held.shape[2] > units:
        held[:, :, units:] = jnp.zeros((2, width, held.shape[2] - units), BF16)
    for plane in range(planes):
        for first in range(plane * chips * rows, (plane + 1) * chips * rows, block):
            columns = slice(first, first + block)
            left = jnp.concatenate([part[:, columns] for part in x], 0)
            held[0, columns, :units] = matmul_tn(left, dgate).astype(BF16)
            held[1, columns, :units] = matmul_tn(left, dup).astype(BF16)
        for step in range(chips):
            at = (plane * chips + (place[1] ^ step)) * rows
            for side in range(2):
                to = outs[0].at[side] if step == 0 else outs[2 * step - 1 + side]
                copy = pltpu.make_async_copy(
                    held.at[side, pl.ds(pl.multiple_of(at, 16), rows), :],
                    to.at[pl.ds(plane * rows, rows), :],
                    sem,
                )
                copy.start()
                copies.append(copy)
    for copy in copies:
        copy.wait()


def feed_grad(place, planes, chips, x, gates, ups, lanes):
    width, units = x[0].shape[1], gates[0].shape[1]
    tokens = x[0].shape[0] * len(x)
    own = shape_of((2, width // chips, lanes))
    part = shape_of((width // chips, lanes))
    outs = (own,) + (part,) * (2 * chips - 2)
    return pl.pallas_call(
        functools.partial(feed_grad_kernel, planes, chips, len(x)),
        out_shape=outs,
        in_specs=[SMEM] + [VMEM] * (len(x) + len(gates) + len(ups)),
        out_specs=(ANY,) * len(outs),
        scratch_shapes=[pltpu.VMEM((2, width, lanes), BF16), pltpu.SemaphoreType.DMA],
        compiler_params=params(),
        cost_estimate=cost(4 * tokens * width * units, 4 * width * units),
        name="feed_grad",
    )(place, *x, *gates, *ups)


def feed_adam_kernel(planes, chips, piece, place, gains, *refs):
    blocks, refs = refs[:planes], refs[planes:]
    ins, outs = refs[:6], refs[6:12]
    gain_grad, held = refs[12], refs[13]
    plane, core = place[0], place[2]
    for step in range(planes):
        for side in range(2):
            held[plane ^ step, core ^ side] = blocks[step][side].astype(F32)
    gain = gains[:, 1:2]
    total = jnp.zeros(gain.shape, F32)
    for part in range(2):
        w, m, u = ins[3 * part : 3 * part + 3]
        grad = jnp.concatenate(
            [
                held[far, c, part, :, at * piece : (at + 1) * piece]
                for far in range(planes)
                for at in range(chips)
                for c in range(2)
            ],
            1,
        )
        weight = w[...]
        total = total + jnp.sum(weight.astype(BF16).astype(F32) * grad, -1, keepdims=True)
        updated = adam_step(weight, m[...], u[...], grad * gain, 0.02)
        for out, value in zip(outs[3 * part : 3 * part + 3], updated):
            out[...] = value
    gain_grad[...] = jnp.broadcast_to(total, gain_grad.shape)


def feed_adam(place, planes, chips, gains, blocks, arrays):
    rows, hidden = arrays[0].shape
    piece = hidden // (2 * planes * chips)
    tile = min(rows, 16)
    whole = pl.BlockSpec((tile, hidden), lambda i: (i, 0))
    lanes = blocks[0].shape[-1]
    block = pl.BlockSpec((2, 2, tile, lanes), lambda i: (0, 0, i, 0))
    two = pl.BlockSpec((tile, 2), lambda i: (i, 0))
    *new, gain_grad = pl.pallas_call(
        functools.partial(feed_adam_kernel, planes, chips, piece),
        grid=(rows // tile,),
        out_shape=(shape_of((rows, hidden), F32),) * 6 + (shape_of((rows, 128), F32),),
        in_specs=[SMEM, two] + [block] * planes + [whole] * 6,
        out_specs=(whole,) * 6 + (pl.BlockSpec((tile, 128), lambda i: (i, 0)),),
        scratch_shapes=[pltpu.VMEM((planes, 2, 2, tile, lanes), F32)],
        compiler_params=params(),
        cost_estimate=cost(40 * rows * hidden, 52 * rows * hidden),
        name="feed_adam",
    )(place, gains, *blocks, *arrays)
    return tuple(new), gain_grad[:, 0]


def segment_starts(lengths_row, length):
    count = lengths_row.shape[0]
    ahead = jnp.arange(count)[:, None] < jnp.arange(count)[None, :]
    starts = jnp.sum(jnp.where(ahead, lengths_row[:, None], 0), 0, dtype=jnp.int32)
    ends = starts + lengths_row
    places = jnp.arange(length, dtype=jnp.int32)
    within = (places[:, None] >= starts[None, :]) & (places[:, None] < ends[None, :])
    return jnp.sum(jnp.where(within, starts[None, :], 0), 1, dtype=jnp.int32)


def rope_tables(positions):
    half = HEAD_DIM // 2
    freqs = jnp.exp(jnp.arange(half, dtype=F32) * (-2.0 * math.log(ROPE_BASE) / HEAD_DIM))
    angles = positions.astype(F32)[:, None] * freqs[None, :]
    cosine = jnp.cos(angles)
    sine = jnp.sin(angles)
    return (
        jnp.concatenate([cosine] * 4, 1),
        jnp.concatenate([-sine, sine, -sine, sine], 1),
    )


def local(
    tokens,
    out_grad,
    seq_lengths,
    query_weight,
    query_first,
    query_second,
    key_weight,
    key_first,
    key_second,
    value_weight,
    value_first,
    value_second,
    output_weight,
    output_first,
    output_second,
    gate_weight,
    gate_first,
    gate_second,
    up_weight,
    up_first,
    up_second,
    down_weight,
    down_first,
    down_second,
    norm_gains,
    gains_first,
    gains_second,
):
    planes = lax.axis_size("dp")
    members = lax.axis_size("fsdp")
    chips = members // 2
    plane = lax.axis_index("dp")
    index = lax.axis_index("fsdp")
    chip = index // 2
    core = index % 2
    place = jnp.stack([plane, chip, core]).astype(jnp.int32)
    spot = jnp.stack([plane, index]).astype(jnp.int32)
    count, width = tokens.shape
    length = count * members
    slice_rows = query_weight.shape[0]
    own_q = query_weight.shape[1] // members
    sharing = members // KV_HEADS
    same_core = [list(range(c, members, 2)) for c in range(2)]

    stages = planes.bit_length() - 1
    chip_stages = chips.bit_length() - 1
    everyone = range(planes)
    heads = head_order(planes, members)
    head_rows = HEADS == planes * members and planes == chips

    def both_cores(blocks):
        return [b for block in blocks for b in (block, core_swap(block))]

    def over_cores(terms):
        return terms[0] + core_swap(terms[1]).astype(F32)

    gains = norm_gains.astype(BF16).astype(F32)
    gain_columns = gains.T
    gu_mine, gu_other, qkv_mine, qkv_other = pack(
        place,
        planes,
        chips,
        gain_columns,
        gate_weight,
        up_weight,
        query_weight,
        key_weight,
        value_weight,
    )
    w_down = lax.all_gather(
        down_weight.astype(BF16), "fsdp", axis=0, tiled=True, axis_index_groups=same_core
    )
    gu_mine, gu_other, qkv_mine, qkv_other, output_rows = together(
        gu_mine, gu_other, qkv_mine, qkv_other, output_weight
    )

    qkv_pairs = swap_pairs(qkv_mine, qkv_other)
    gu_pairs = swap_pairs(gu_mine, gu_other)
    out_rows = gather_stage({0: output_rows.astype(BF16)}, plane_send, planes, 1)
    qkv_pairs, gu_pairs, out_rows = together(qkv_pairs, gu_pairs, out_rows)

    qkv_got = exchange(qkv_pairs, chip_send)
    gu_near = plane_send(gu_pairs[1], 1)
    for stage in range(2, stages + 1):
        out_rows = gather_stage(out_rows, plane_send, planes, stage)
    out_rows = jnp.stack([out_rows[far] for far in everyone])
    qkv_got, gu_pairs, gu_near, tokens, out_rows = together(
        qkv_got, gu_pairs, gu_near, tokens, out_rows
    )

    gu_got = [gu_pairs[0], gu_near] + [
        plane_send(gu_pairs[step], step) for step in range(2, planes)
    ]
    out_got = []
    token_blocks = [tokens]
    for step in range(chips):
        if head_rows:
            rows = lax.dynamic_index_in_dim(out_rows, (chip ^ step) ^ plane, 0, keepdims=False)
            if step:
                both = chip_send(jnp.concatenate([tokens, rows]), step)
                token_blocks.append(both[:count])
                rows = both[count:]
            out_got.append(rows)
        elif step:
            token_blocks.append(chip_send(tokens, step))
    start = segment_starts(seq_lengths[0], length)
    cosine, sine = rope_tables(jnp.arange(length, dtype=jnp.int32) - start)
    gu_got, qkv_got, token_blocks, out_got, cosine, sine, w_down = together(
        gu_got, qkv_got, token_blocks, out_got, cosine, sine, w_down
    )

    tokens_mine = jnp.stack(token_blocks)
    tokens_other = core_swap(tokens_mine)
    gu_rows = gather_rows(plane, core, gu_got)
    qkv_rows = gather_rows(chip, core, qkv_got)
    steps = [step for step in range(chips) if ones(step) <= 1]
    w_gate_up = [gu_rows] + [chip_send(gu_rows, step) for step in steps[1:]]
    w_qkv = {0: qkv_rows}
    for stage in range(1, stages + 1):
        w_qkv = gather_stage(w_qkv, plane_send, planes, stage)
    w_qkv = [w_qkv[far] for far in everyone]
    w_gate_up, w_qkv, out_grad, tokens_mine, tokens_other, out_rows = together(
        w_gate_up, w_qkv, out_grad, tokens_mine, tokens_other, out_rows
    )

    gate_up = {step: (block[0], block[1]) for step, block in zip(steps, w_gate_up)}
    for stage in range(2, chip_stages + 1):
        for step in range(1, chips):
            if ones(step) == stage:
                top = 1 << (step.bit_length() - 1)
                gate_up[step] = (
                    chip_send(gate_up[step & (step - 1)][0], step & -step),
                    chip_send(gate_up[step ^ top][1], top),
                )
    more = [step for step in range(chips) if ones(step) > 1]
    layout = [(step, None) for step in steps] + [(step, side) for step in more for side in range(2)]
    w_gate_up = w_gate_up + [gate_up[step][side] for step in more for side in range(2)]
    normed, queries, keys_values, attended = attend(
        spot, tokens_mine, tokens_other, w_qkv, start[:, None], cosine, sine
    )
    out_grad_blocks = gather_stage({0: out_grad}, plane_send, planes, 1)
    hop = members // planes
    own_plane = index // hop

    def out_route(turn_no):
        return [(i, ((turn_no + i) % planes) * hop + i // planes) for i in range(members)]

    if head_rows:
        w_output = jnp.concatenate(out_got)
    else:
        w_output = jnp.zeros((planes, slice_rows, width), BF16)
        for turn_no in range(planes):
            sent = lax.dynamic_index_in_dim(
                out_rows, ((turn_no + index) % planes) ^ plane, 0, keepdims=False
            )
            got = lax.ppermute(sent, "fsdp", out_route(turn_no))
            spare = (own_plane + planes - turn_no) % planes
            w_output = lax.dynamic_update_index_in_dim(w_output, got, spare, 0)
        w_output = w_output.reshape(planes * slice_rows, width)
    w_gate_up, attended, out_grad_blocks, w_output = together(
        w_gate_up, attended, out_grad_blocks, w_output
    )

    w_gate_up = list(zip(layout, w_gate_up))
    for stage in range(2, stages + 1):
        out_grad_blocks = gather_stage(out_grad_blocks, plane_send, planes, stage)
    own_tokens = tokens.astype(F32)
    mixed = [over_cores(terms) for terms in zip(*project(attended, w_output, chips))]
    mixed = mixed[:1] + [
        chip_send(mixed[step].astype(BF16), step).astype(F32) for step in range(1, chips)
    ]
    resid = own_tokens + sum(mixed[1:], mixed[0])
    resid, out_grad_blocks = together(resid, out_grad_blocks)

    scale_two = rms_scale(resid)
    own_normed_two = (resid * scale_two).astype(BF16)
    normed_blocks = gather_stage({0: own_normed_two}, plane_send, planes, 1)
    out_grad_all = both_cores([out_grad_blocks[far] for far in everyone])
    normed_blocks, out_grad_all = together(normed_blocks, out_grad_all)

    for stage in range(2, stages + 1):
        normed_blocks = gather_stage(normed_blocks, plane_send, planes, stage)
    normed_two = both_cores([normed_blocks[far] for far in everyone])
    normed_two, out_grad_all = together(normed_two, out_grad_all)

    order = sorted(everyone, key=lambda j: (-ones(j), -j))
    x = {far: normed_two[2 * far : 2 * far + 2] for far in everyone}
    fed = {}
    sums = ({}, {})
    last = []
    moved_here = {}
    for turn_no, far in enumerate(order):
        span = slice(2 * far, 2 * far + 2)
        fed[far] = feed(place, planes, x[far], out_grad_all[span], w_gate_up, w_down)
        pair, moved = None, None
        if turn_no >= 1:
            pair = tuple(over_cores(fed[order[turn_no - 1]][side]) for side in (2, 1))
        if turn_no >= 2:
            near = order[turn_no - 2]
            if ones(near) > 1:
                moved = plane_send(sums[0][near].astype(BF16), near & -near)
            else:
                last.append(plane_send(sums[0][near].astype(BF16), near))
        later = {j: x[j] for j in order[turn_no + 1 :]}
        fed[far], later, pair, moved = together(fed[far], later, pair, moved)
        x.update(later)
        for side in (0, 1):
            if pair is not None:
                sums[side][order[turn_no - 1]] = pair[side]
        if moved is not None:
            moved_here.setdefault(near & (near - 1), []).append(moved)
        for target in list(moved_here):
            if target in sums[0]:
                for part in moved_here.pop(target):
                    sums[0][target] = sums[0][target] + part.astype(F32)
    last.append(plane_send(sums[0][order[-2]].astype(BF16), order[-2]))
    sums[1][0] = over_cores(fed[0][1])
    grad_normed_two = over_cores(fed[0][2])
    hidden, grad_gate, grad_up = zip(*[fed[far][0] for far in everyone])
    lanes = w_gate_up[0][1].shape[-1]
    grads = feed_grad(place, planes, chips, normed_two, grad_gate, grad_up, lanes)
    grad_normed_two, last, grads, result = together(grad_normed_two, last, grads, sums[1])
    grad_normed_two = sum([part.astype(F32) for part in last], grad_normed_two)

    grad_resid = (
        out_grad.astype(F32)
        + scale_two * grad_normed_two
        - resid
        * (scale_two * scale_two * scale_two)
        * jnp.mean(grad_normed_two * resid, -1, keepdims=True)
    )
    own_grad = grad_resid.astype(BF16)
    own_grad, result, hidden = together(own_grad, result, hidden)

    grad_blocks = gather(own_grad, chip_send, chips)
    for stage in range(stages, 1, -1):
        result = scatter_stage(result, plane_send, stage)
    grad_down = rows_grad(jnp.concatenate(hidden), out_grad_all)
    grad_blocks, result, grad_down = together(grad_blocks, result, grad_down)

    grad_attn_out = both_cores(grad_blocks)
    grad_output = rows_grad(attended, grad_attn_out).reshape(planes, slice_rows, width)
    grad_output, grad_attn_out, grads, result = together(
        grad_output, grad_attn_out, grads, result
    )

    result = scatter_stage(result, plane_send, 1)[0]
    grad_gate_up = {step: grads[2 * step - 1 : 2 * step + 1] for step in range(1, chips)}

    def plus(one, two):
        return (one.astype(F32) + two.astype(F32)).astype(BF16)

    for stage in range(chip_stages, 1, -1):
        for step in range(chips - 1, 0, -1):
            if ones(step) == stage:
                top = 1 << (step.bit_length() - 1)
                low = step & (step - 1)
                gate, up = grad_gate_up.pop(step)
                gate, up = chip_send(gate, step & -step), chip_send(up, top)
                grad_gate_up[low] = (plus(grad_gate_up[low][0], gate), grad_gate_up[low][1])
                low = step ^ top
                grad_gate_up[low] = (grad_gate_up[low][0], plus(grad_gate_up[low][1], up))
    grad_gate_up = {step: jnp.stack(pair) for step, pair in grad_gate_up.items()}
    grad_qkv = attend_back(
        spot, queries, keys_values, w_output, grad_attn_out, start[None, :], cosine, sine
    )
    grad_qkv, result, grad_gate_up = together(grad_qkv, result, grad_gate_up)
    result = (resid + result).astype(BF16)

    grad_w_qkv = qkv_grad(spot, normed, grad_qkv, planes)
    grad_qkv, grad_w_qkv, grad_gate_up = together(grad_qkv, grad_w_qkv, grad_gate_up)

    grad_gate_up = [grads[0]] + [chip_send(part, step) for step, part in grad_gate_up.items()]
    grad_w_qkv = dict(enumerate(grad_w_qkv))
    for stage in range(stages, 0, -1):
        grad_w_qkv = scatter_stage(grad_w_qkv, plane_send, stage)
    mixed = [over_cores(terms) for terms in zip(*project_back(spot, grad_qkv, w_qkv, chips))]
    mixed, grad_w_qkv, grad_gate_up, grad_down, grad_output = together(
        mixed, grad_w_qkv[0], grad_gate_up, grad_down, grad_output
    )

    grad_down_weight = lax.psum_scatter(
        grad_down, "fsdp", scatter_dimension=0, tiled=True, axis_index_groups=same_core
    ).astype(F32)
    gu_pairs = swap_pairs(*spread_rows(plane, core, grad_gate_up, planes))
    qkv_pairs = swap_pairs(*spread_rows(chip, core, [grad_w_qkv], chips))
    mixed = dict(enumerate(mixed))
    for stage in range(chip_stages, 1, -1):
        mixed = scatter_stage(mixed, chip_send, stage)
    if head_rows:
        parts = [grad_output[0]] + [chip_send(grad_output[step], step) for step in range(1, chips)]
        parts = jnp.stack(parts)
        out_parts = [
            lax.dynamic_index_in_dim(parts, (plane ^ far) ^ chip, 0, keepdims=False)
            for far in everyone
        ]
    else:
        parts = jnp.zeros((planes, slice_rows, width), BF16)
        for turn_no in range(planes):
            spare = (own_plane + planes - turn_no) % planes
            sent = lax.dynamic_index_in_dim(grad_output, spare, 0, keepdims=False)
            part = lax.ppermute(sent, "fsdp", [(b, a) for a, b in out_route(turn_no)])
            parts = lax.dynamic_update_index_in_dim(
                parts, part, ((turn_no + index) % planes) ^ plane, 0
            )
        out_parts = [parts[far] for far in everyone]
    gu_pairs, qkv_pairs, mixed, out_parts = together(gu_pairs, qkv_pairs, mixed, out_parts)

    grad_gate_up = exchange(gu_pairs, plane_send)
    got = exchange(qkv_pairs, chip_send)
    got = by_offset(jnp.concatenate(got), index).astype(F32)
    got = jnp.transpose(got, (1, 0, 2))
    grad_query = got[:, :, :own_q].reshape(slice_rows, HEADS, HEAD_DIM)
    kept = [head for device_heads in heads for head in device_heads]
    grad_query = jnp.stack([grad_query[:, kept.index(head)] for head in range(HEADS)], 1)
    grad_query = grad_query.reshape(slice_rows, -1)
    grad_kv = got[:, :, own_q:].reshape(slice_rows, KV_HEADS, sharing, PAIR).sum(2)
    grad_key = grad_kv[:, :, :HEAD_DIM].reshape(slice_rows, -1)
    grad_value = grad_kv[:, :, HEAD_DIM:].reshape(slice_rows, -1)

    gain_one = gain_columns[:, :1]
    grad_gain_one = sum(
        jnp.sum(weight.astype(BF16).astype(F32) * gradient, 1)
        for weight, gradient in (
            (query_weight, grad_query),
            (key_weight, grad_key),
            (value_weight, grad_value),
        )
    )
    attention_new = (
        adam_step(query_weight, query_first, query_second, grad_query * gain_one, 0.02)
        + adam_step(key_weight, key_first, key_second, grad_key * gain_one, 0.02)
        + adam_step(value_weight, value_first, value_second, grad_value * gain_one, 0.02)
    )
    grad_gate_up, attention_new, grad_gain_one, out_parts, mixed, grad_down_weight = together(
        grad_gate_up, attention_new, grad_gain_one, out_parts, mixed, grad_down_weight
    )

    grad_normed = scatter_stage(mixed, chip_send, 1)[0]
    grad_output_weight = scatter_sum(out_parts, plane_send)
    scale_one = rms_scale(own_tokens)
    grad_tokens = (
        grad_resid
        + scale_one * grad_normed
        - own_tokens
        * (scale_one * scale_one * scale_one)
        * jnp.mean(grad_normed * own_tokens, -1, keepdims=True)
    )
    fed_weights, grad_gain_two = feed_adam(
        place,
        planes,
        chips,
        gain_columns,
        grad_gate_up,
        (gate_weight, gate_first, gate_second, up_weight, up_first, up_second),
    )
    gain_grads = jnp.stack([grad_gain_one, grad_gain_two])
    updated = (
        attention_new
        + adam_step(output_weight, output_first, output_second, grad_output_weight, 0.1)
        + fed_weights
        + adam_step(down_weight, down_first, down_second, grad_down_weight, 0.02)
        + adam_step(norm_gains, gains_first, gains_second, gain_grads, 0.2)
    )
    return (result, grad_tokens) + updated


def solution(mesh):
    rows = P(("dp", "fsdp"), None)
    columns = P(None, ("dp", "fsdp"))
    in_specs = (rows, rows, P("dp", None)) + (rows,) * 21 + (columns,) * 3
    out_specs = (rows, rows) + (rows,) * 21 + (columns,) * 3
    return jax.shard_map(local, mesh=mesh, in_specs=in_specs, out_specs=out_specs, check_vma=False)
```

```python
import functools
import math

import jax
import jax.numpy as jnp
from jax import lax
from jax.experimental import pallas as pl
from jax.experimental.pallas import tpu as pltpu
from jax.sharding import PartitionSpec as P

HEADS = 32
KV_HEADS = 4
HEAD_DIM = 64
STEP = 3

NORM_EPS = 1e-05
ROPE_BASE = 10000.0
BETA = 0.5
ADAM_EPS = 1e-08
DECAY = 0.1
MASKED = -1e30
PAIR = 2 * HEAD_DIM
BF16 = jnp.bfloat16
F32 = jnp.float32


def matmul(left, right):
    return jnp.dot(left, right, preferred_element_type=F32)


def matmul_tn(left, right):
    return lax.dot_general(left, right, (((0,), (0,)), ((), ())), preferred_element_type=F32)


def matmul_nt(left, right):
    return lax.dot_general(left, right, (((1,), (1,)), ((), ())), preferred_element_type=F32)


def rms_scale(values):
    return lax.rsqrt(jnp.mean(values * values, -1, keepdims=True) + NORM_EPS)


def adam_step(master, first_moment, second_moment, gradient, rate):
    first_new = BETA * first_moment + (1.0 - BETA) * gradient
    second_new = BETA * second_moment + (1.0 - BETA) * gradient * gradient
    correction = 1.0 - BETA**STEP
    master_new = master - rate * (
        first_new / correction / (jnp.sqrt(second_new / correction) + ADAM_EPS) + DECAY * master
    )
    return (master_new, first_new, second_new)


def core_swap(value):
    members = lax.axis_size("fsdp")
    return lax.ppermute(value, "fsdp", [(i, i ^ 1) for i in range(members)])


def chip_send(value, step):
    members = lax.axis_size("fsdp")
    return lax.ppermute(value, "fsdp", [(i, i ^ (2 * step)) for i in range(members)])


def plane_send(value, step):
    planes = lax.axis_size("dp")
    return lax.ppermute(value, "dp", [(i, i ^ step) for i in range(planes)])


def gather(own, send, count):
    return [own] + [send(own, step) for step in range(1, count)]


def ones(step):
    return step.bit_count()


def gather_stage(got, send, count, stage):
    more = {j: send(got[j & (j - 1)], j & -j) for j in range(count) if ones(j) == stage}
    return {**got, **more}


def scatter_stage(parts, send, stage):
    parts = dict(parts)
    for j in sorted(parts, reverse=True):
        if ones(j) == stage:
            got = send(parts.pop(j).astype(BF16), j & -j)
            parts[j & (j - 1)] = parts[j & (j - 1)].astype(F32) + got.astype(F32)
    return parts


def gather_terms(parts, send):
    return [parts[0]] + [send(parts[step], step) for step in range(1, len(parts))]


def scatter_sum(parts, send):
    return sum(part.astype(F32) for part in gather_terms(parts, send))


def together(*values):
    return lax.optimization_barrier(values)


def swap_pairs(mine, other):
    got = core_swap(other)
    return [jnp.stack([mine[step], got[step]]) for step in range(mine.shape[0])]


def exchange(pairs, send):
    return pairs[:1] + [send(pairs[step], step) for step in range(1, len(pairs))]


def by_offset(blocks, index):
    count = blocks.shape[0]
    return jnp.stack(
        [lax.dynamic_index_in_dim(blocks, j ^ index, 0, keepdims=False) for j in range(count)]
    )


def lane_ids(shape):
    return lax.broadcasted_iota(jnp.int32, shape, len(shape) - 1)


def turn(values, cosine, sine):
    low_half = lane_ids(values.shape) % HEAD_DIM < HEAD_DIM // 2
    shifted = jnp.where(
        low_half,
        pltpu.roll(values, PAIR - HEAD_DIM // 2, 1),
        pltpu.roll(values, HEAD_DIM // 2, 1),
    )
    return values * cosine + shifted * sine


VMEM = pl.BlockSpec(memory_space=pltpu.VMEM)
SMEM = pl.BlockSpec(memory_space=pltpu.SMEM)
ANY = pl.BlockSpec(memory_space=pl.ANY)


def params(mib=56):
    return pltpu.CompilerParams(vmem_limit_bytes=mib * 2**20)


def shape_of(shape, dtype=BF16):
    return jax.ShapeDtypeStruct(shape, dtype)


def cost(flops, moved, exps=0):
    return pl.CostEstimate(flops=int(flops), bytes_accessed=int(moved), transcendentals=int(exps))


def whole_lanes(width):
    return -(-width // 128) * 128


def head_order(planes, members):
    chips = members // 2
    if HEADS == planes * members and planes == chips:
        return [
            [f // 2 * members + 2 * ((f // 2) ^ step) + f % 2 for step in range(chips)]
            for f in range(members)
        ]
    share = HEADS // members
    return [list(range(f * share, (f + 1) * share)) for f in range(members)]


def pack_kernel(planes, chips, piece, place, gains, gate, up, query, key, value, *outs):
    gu_mine, gu_other, qkv_mine, qkv_other = outs
    plane, chip, core = place[0], place[1], place[2]
    sharing = 2 * chips // KV_HEADS
    heads = head_order(planes, 2 * chips)

    def put(mine, other, core_to, index, block):
        @pl.when(core == core_to)
        def _():
            mine[index] = block

        @pl.when(core != core_to)
        def _():
            other[index] = block

    def rounded(block, row):
        return (block.astype(BF16).astype(F32) * gains[:, row : row + 1]).astype(BF16)

    for to in range(2 * chips):
        head = slice(to // sharing * HEAD_DIM, (to // sharing + 1) * HEAD_DIM)
        columns = [query[:, h * HEAD_DIM : (h + 1) * HEAD_DIM] for h in heads[to]]
        block = jnp.concatenate(columns + [key[:, head], value[:, head]], 1)
        put(qkv_mine, qkv_other, to % 2, (to // 2) ^ chip, rounded(block, 0))
    for side, weight in enumerate((gate, up)):
        for to in range(2 * planes):
            starts = [((to // 2 * chips + c) * 2 + to % 2) * piece for c in range(chips)]
            columns = [weight[:, s : s + piece] for s in starts]
            spare = gu_mine.shape[-1] - chips * piece
            if spare:
                columns.append(jnp.zeros((weight.shape[0], spare), F32))
            block = rounded(jnp.concatenate(columns, 1), 1)
            put(gu_mine.at[:, side], gu_other.at[:, side], to % 2, (to // 2) ^ plane, block)


def whole_lanes(width):
    return -(-width // 128) * 128


def pack(place, planes, chips, gains, gate, up, query, key, value):
    rows, hidden = gate.shape
    gu = shape_of((planes, 2, rows, whole_lanes(hidden // (2 * planes))))
    qkv = shape_of((chips, rows, query.shape[1] // (2 * chips) + PAIR))
    return pl.pallas_call(
        functools.partial(pack_kernel, planes, chips, hidden // (2 * planes * chips)),
        out_shape=(gu, gu, qkv, qkv),
        in_specs=[SMEM] + [VMEM] * 6,
        out_specs=(VMEM,) * 4,
        compiler_params=params(),
        cost_estimate=cost(0, rows * hidden * 12),
        name="pack",
    )(place, gains, gate, up, query, key, value)


def gather_rows_kernel(members, place, *refs):
    blocks, out = refs[:-1], refs[-1]
    first, core = place[0], place[1]
    rows = blocks[0].shape[-2]
    for step, block in enumerate(blocks):
        for side in range(2):
            at = ((first ^ step) * 2 + (core ^ side)) * rows
            if len(block.shape) == 3:
                out[pl.ds(pl.multiple_of(at, 16), rows), :] = block[side]
            else:
                for part in range(2):
                    out[part, pl.ds(pl.multiple_of(at, 16), rows), :] = block[side, part]


def gather_rows(first, core, pairs):
    lead, (rows, width) = pairs[0].shape[1:-2], pairs[0].shape[-2:]
    return pl.pallas_call(
        functools.partial(gather_rows_kernel, 2 * len(pairs)),
        out_shape=shape_of(lead + (2 * len(pairs) * rows, width)),
        in_specs=[SMEM] + [VMEM] * len(pairs),
        out_specs=VMEM,
        compiler_params=params(),
        cost_estimate=cost(0, pairs[0].size * len(pairs) * 4),
        name="gather_rows",
    )(jnp.stack([first, core]), *pairs)


def spread_rows_kernel(place, *refs):
    terms, (mine, other) = refs[:-2], refs[-2:]
    first, core = place[0], place[1]
    count = mine.shape[0]
    rows = mine.shape[-2]
    for step in range(count):
        for side, out in enumerate((mine, other)):
            at = pl.ds(pl.multiple_of(((first ^ step) * 2 + (core ^ side)) * rows, 16), rows)
            if len(mine.shape) == 3:
                out[step] = sum(t[at, :].astype(F32) for t in terms).astype(BF16)
            else:
                for part in range(2):
                    out[step, part] = sum(t[part, at, :].astype(F32) for t in terms).astype(BF16)


def spread_rows(first, core, terms, count):
    whole = terms[0]
    rows = whole.shape[-2] // (2 * count)
    out = shape_of((count,) + whole.shape[:-2] + (rows, whole.shape[-1]))
    return pl.pallas_call(
        spread_rows_kernel,
        out_shape=(out, out),
        in_specs=[SMEM] + [VMEM] * len(terms),
        out_specs=(VMEM, VMEM),
        compiler_params=params(),
        cost_estimate=cost(0, whole.size * 6),
        name="spread_rows",
    )(jnp.stack([first, core]), *terms)


def attend_kernel(members, pairs, planes, place, start_ref, cos_ref, sin_ref, *refs):
    tokens, refs = refs[:2], refs[2:]
    weights, refs = refs[:planes], refs[planes:]
    normed_ref, q_ref, kv_ref, o_ref = refs
    plane, index = place[0], place[1]
    rows = tokens[0].shape[1]
    length = rows * members
    even = lane_ids((rows, PAIR)) < HEAD_DIM
    depth = weights[0].shape[0]
    for j in range(members):
        values = tokens[j % 2][j // 2].astype(F32)
        normed_ref[j * rows : (j + 1) * rows, :] = (values * rms_scale(values)).astype(BF16)
    block = min(2 * rows, 256)
    per = block // rows
    for first in range(0, length, block):
        qkv = None
        for step in range(planes):
            columns = pl.ds(pl.multiple_of((plane ^ step) * depth, 128), depth)
            term = matmul(normed_ref[first : first + block, columns], weights[step][...])
            qkv = term if qkv is None else qkv + term
        for part in range(per):
            j = first // rows + part
            here = pl.ds(pl.multiple_of((j ^ index) * rows, rows), rows)
            cosine = cos_ref[here, :]
            sine = sin_ref[here, :]
            piece = qkv[part * rows : (part + 1) * rows, :]
            for pair in range(pairs):
                lanes = slice(pair * PAIR, (pair + 1) * PAIR)
                turned = turn(piece[:, lanes], cosine, sine).astype(BF16).astype(F32)
                q_ref[here, lanes] = (turned * HEAD_DIM**-0.5).astype(BF16)
            both = piece[:, pairs * PAIR :]
            kv_ref[here, :] = jnp.where(even, turn(both, cosine, sine), both).astype(BF16)
    for first in range(0, length, block):
        reach = first + block
        both = kv_ref[:reach, :].astype(F32)
        left = lane_ids(both.shape) < HEAD_DIM
        keys_even = jnp.where(left, both, 0.0)
        values_odd = jnp.where(left, 0.0, both)
        keys = (keys_even.astype(BF16), pltpu.roll(keys_even, HEAD_DIM, 1).astype(BF16))
        values = (pltpu.roll(values_odd, HEAD_DIM, 1).astype(BF16), values_odd.astype(BF16))
        query_at = first + lax.broadcasted_iota(jnp.int32, (block, reach), 0)
        key_at = lax.broadcasted_iota(jnp.int32, (block, reach), 1)
        allowed = (key_at <= query_at) & (key_at >= start_ref[first:reach, :])
        for pair in range(pairs):
            lanes = slice(pair * PAIR, (pair + 1) * PAIR)
            query = q_ref[first:reach, lanes]
            mixed = jnp.zeros((block, PAIR), F32)
            for side in range(2):
                scores = jnp.where(allowed, matmul_nt(query, keys[side]), MASKED)
                raised = jnp.exp(scores - jnp.max(scores, -1, keepdims=True))
                probs = raised * (1.0 / jnp.sum(raised, -1, keepdims=True))
                mixed = mixed + matmul(probs.astype(BF16), values[side])
            mixed = mixed.astype(BF16)
            for part in range(per):
                j = first // rows + part
                there = pl.ds(pl.multiple_of((j ^ index) * rows, rows), rows)
                o_ref[there, lanes] = mixed[part * rows : (part + 1) * rows, :]


def attend(place, mine, other, weights, start, cosine, sine):
    members, planes = 2 * mine.shape[0], len(weights)
    rows, width = mine.shape[1:]
    length = members * rows
    pairs = weights[0].shape[1] // PAIR - 1
    return pl.pallas_call(
        functools.partial(attend_kernel, members, pairs, planes),
        out_shape=(
            shape_of((length, width)),
            shape_of((length, pairs * PAIR)),
            shape_of((length, PAIR)),
            shape_of((length, pairs * PAIR)),
        ),
        in_specs=[SMEM] + [VMEM] * (5 + planes),
        out_specs=(VMEM,) * 4,
        compiler_params=params(),
        cost_estimate=cost(
            2 * length * width * (pairs + 1) * PAIR + 3 * length * length * pairs * PAIR,
            length * width * 4,
            length * length * pairs,
        ),
        name="attend",
    )(place, start, cosine, sine, mine, other, *weights)


def attend_back_kernel(members, pairs, place, start_ref, cos_ref, sin_ref, q_ref, kv_ref, w_ref, *refs):
    grads, refs = refs[:members], refs[members:]
    out_ref, do_ref, dk_ref, dv_ref = refs
    length = q_ref.shape[0]
    rows = length // members
    index = place[1]
    block = min(2 * rows, 256)
    per = block // rows
    for j in range(0, members, 2):
        grad = jnp.concatenate([grads[j][...], grads[j + 1][...]], 0)
        do_ref[j * rows : (j + 2) * rows, :] = matmul_nt(grad, w_ref[...]).astype(BF16)
    dk_ref[...] = jnp.zeros_like(dk_ref)
    dv_ref[...] = jnp.zeros_like(dv_ref)
    for first in range(0, length, block):
        reach = first + block
        both = kv_ref[:reach, :].astype(F32)
        left = lane_ids(both.shape) < HEAD_DIM
        keys_even = jnp.where(left, both, 0.0)
        values_odd = jnp.where(left, 0.0, both)
        keys = (keys_even.astype(BF16), pltpu.roll(keys_even, HEAD_DIM, 1).astype(BF16))
        values = (pltpu.roll(values_odd, HEAD_DIM, 1).astype(BF16), values_odd.astype(BF16))
        key_at = lax.broadcasted_iota(jnp.int32, (reach, block), 0)
        query_at = first + lax.broadcasted_iota(jnp.int32, (reach, block), 1)
        allowed = (key_at <= query_at) & (key_at >= start_ref[:, first:reach])
        half = lane_ids((block, PAIR)) < HEAD_DIM
        theres = [
            pl.ds(pl.multiple_of(((first // rows + part) ^ index) * rows, rows), rows)
            for part in range(per)
        ]
        for pair in range(pairs):
            lanes = slice(pair * PAIR, (pair + 1) * PAIR)
            query = q_ref[first:reach, lanes]
            grad = jnp.concatenate([do_ref[there, lanes] for there in theres], 0)
            dq = jnp.zeros((block, PAIR), F32)
            for side in range(2):
                keep = half if side == 0 else ~half
                query_side = jnp.where(keep, query.astype(F32), 0.0).astype(BF16)
                grad_side = jnp.where(keep, grad.astype(F32), 0.0).astype(BF16)
                scores = jnp.where(allowed, matmul_nt(keys[side], query), MASKED)
                raised = jnp.exp(scores - jnp.max(scores, 0, keepdims=True))
                probs = raised * (1.0 / jnp.sum(raised, 0, keepdims=True))
                dp = matmul_nt(values[side], grad)
                centre = jnp.sum(probs * dp, 0, keepdims=True)
                ds = (probs * (dp - centre)).astype(BF16)
                dv_ref[:reach, :] += matmul(probs.astype(BF16), grad_side)
                dk_ref[:reach, :] += matmul(ds, query_side)
                dq = dq + matmul_tn(ds, keys[side])
            dq = dq * HEAD_DIM**-0.5
            for part in range(per):
                piece = dq[part * rows : (part + 1) * rows, :]
                here = slice(first + part * rows, first + (part + 1) * rows)
                out_ref[theres[part], lanes] = turn(
                    piece, cos_ref[here, :], -sin_ref[here, :]
                ).astype(BF16)
    left = lane_ids((rows, PAIR)) < HEAD_DIM
    for j in range(members):
        here = slice(j * rows, (j + 1) * rows)
        there = pl.ds(pl.multiple_of((j ^ index) * rows, rows), rows)
        dk = dk_ref[here, :]
        dv = dv_ref[here, :]
        dk = turn(dk + pltpu.roll(dk, HEAD_DIM, 1), cos_ref[here, :], -sin_ref[here, :])
        dv = dv + pltpu.roll(dv, HEAD_DIM, 1)
        out_ref[there, pairs * PAIR :] = jnp.where(left, dk, dv).astype(BF16)


def attend_back(place, queries, keys_values, w_output, grads, start, cosine, sine):
    length, width = queries.shape
    pairs = width // PAIR
    members = len(grads)
    model = grads[0].shape[1]
    return pl.pallas_call(
        functools.partial(attend_back_kernel, members, pairs),
        out_shape=shape_of((length, width + PAIR)),
        in_specs=[SMEM] + [VMEM] * (6 + members),
        out_specs=VMEM,
        scratch_shapes=[
            pltpu.VMEM((length, width), BF16),
            pltpu.VMEM((length, PAIR), F32),
            pltpu.VMEM((length, PAIR), F32),
        ],
        compiler_params=params(),
        cost_estimate=cost(
            2 * length * width * model + 7 * length * length * width,
            length * model * 2,
            length * length * pairs,
        ),
        name="attend_back",
    )(place, start, cosine, sine, queries, keys_values, w_output, *grads)


def project_kernel(count, left_ref, weight_ref, *outs):
    rows = left_ref.shape[0] // (2 * count)
    for step in range(count):
        whole = matmul(left_ref[2 * step * rows : 2 * (step + 1) * rows, :], weight_ref[...])
        outs[step][...] = whole[:rows, :]
        outs[count + step][...] = whole[rows:, :].astype(BF16)


def project(left, weight, count):
    rows, width = left.shape[0] // (2 * count), weight.shape[1]
    outs = pl.pallas_call(
        functools.partial(project_kernel, count),
        out_shape=(shape_of((rows, width), F32),) * count + (shape_of((rows, width)),) * count,
        in_specs=[VMEM, VMEM],
        out_specs=(VMEM,) * (2 * count),
        compiler_params=params(),
        cost_estimate=cost(2 * left.size * width, left.shape[0] * width * 3),
        name="project",
    )(left, weight)
    return outs[:count], outs[count:]


def project_back_kernel(planes, count, place, left_ref, *refs):
    weights, outs = refs[:planes], refs[planes:]
    rows = left_ref.shape[0] // (2 * count)
    depth = weights[0].shape[0]
    for step in range(count):
        left = left_ref[2 * step * rows : 2 * (step + 1) * rows, :]
        for far in range(planes):
            columns = pl.ds(pl.multiple_of((place[0] ^ far) * depth, 128), depth)
            whole = matmul_nt(left, weights[far][...])
            outs[step][:, columns] = whole[:rows, :]
            outs[count + step][:, columns] = whole[rows:, :].astype(BF16)


def project_back(place, left, weights, count):
    rows, planes = left.shape[0] // (2 * count), len(weights)
    width = weights[0].shape[0] * planes
    outs = pl.pallas_call(
        functools.partial(project_back_kernel, planes, count),
        out_shape=(shape_of((rows, width), F32),) * count + (shape_of((rows, width)),) * count,
        in_specs=[SMEM] + [VMEM] * (1 + planes),
        out_specs=(VMEM,) * (2 * count),
        compiler_params=params(),
        cost_estimate=cost(2 * left.size * width, left.shape[0] * width * 3),
        name="project_back",
    )(place, left, *weights)
    return outs[:count], outs[count:]


def qkv_grad_kernel(place, normed_ref, grad_ref, *outs):
    depth = outs[0].shape[0]
    for far, out in enumerate(outs):
        columns = pl.ds(pl.multiple_of((place[0] ^ far) * depth, 128), depth)
        out[...] = matmul_tn(normed_ref[:, columns], grad_ref[...]).astype(BF16)


def qkv_grad(place, normed, grad, planes):
    depth, width = normed.shape[1] // planes, grad.shape[1]
    return pl.pallas_call(
        qkv_grad_kernel,
        out_shape=(shape_of((depth, width)),) * planes,
        in_specs=[SMEM, VMEM, VMEM],
        out_specs=(VMEM,) * planes,
        compiler_params=params(),
        cost_estimate=cost(2 * normed.size * width, normed.size * 2),
        name="qkv_grad",
    )(place, normed, grad)


def rows_grad_kernel(count, left_ref, *refs):
    grads, out = refs[:-1], refs[-1]
    left = left_ref[...]
    width = out.shape[1]
    block = 512
    for first in range(0, width, block):
        columns = slice(first, first + block)
        right = jnp.concatenate([grad[:, columns] for grad in grads], 0)
        out[:, columns] = matmul_tn(left, right).astype(BF16)


def rows_grad(left, grads):
    return pl.pallas_call(
        functools.partial(rows_grad_kernel, len(grads)),
        out_shape=shape_of((left.shape[1], grads[0].shape[1])),
        in_specs=[VMEM] * (1 + len(grads)),
        out_specs=VMEM,
        compiler_params=params(),
        cost_estimate=cost(2 * left.size * grads[0].shape[1], left.size * 2),
        name="rows_grad",
    )(left, *grads)


def weight_copies(place, planes, sides, gu, sem):
    chips = len(sides)
    rows = gu.shape[1] // (planes * chips)
    copies = []
    for side in range(2):
        for step, pair in enumerate(sides):
            for plane in range(planes):
                to = (plane * chips + (place[1] ^ step)) * rows
                copies.append(
                    pltpu.make_async_copy(
                        pair[side].at[pl.ds(plane * rows, rows), :],
                        gu.at[side, pl.ds(pl.multiple_of(to, 16), rows), :],
                        sem.at[side],
                    )
                )
    return copies


def feed_kernel(planes, layout, count, place, *refs):
    x, refs = refs[:count], refs[count:]
    grads, refs = refs[:count], refs[count:]
    blocks, refs = refs[: len(layout)], refs[len(layout) :]
    chips = 1 + max(step for step, _ in layout)
    sides = [[None, None] for _ in range(chips)]
    for (step, side), ref in zip(layout, blocks):
        for part in (0, 1) if side is None else (side,):
            sides[step][part] = ref.at[part] if side is None else ref
    down_ref, hidden_ref, gate_ref, up_ref = refs[:4]
    outs, refs = refs[4 : 4 + count], refs[4 + count :]
    dxs, refs = refs[:count], refs[count:]
    gu, down, sem = refs
    rows = x[0].shape[0]
    units = down.shape[0]
    copies = weight_copies(place, planes, sides, gu, sem)
    down_copy = pltpu.make_async_copy(down_ref, down, sem.at[2])
    half = len(copies) // 2
    for copy in copies:
        copy.start()
    down_copy.start()
    x = jnp.concatenate([part[...] for part in x], 0)
    grad = jnp.concatenate([part[...] for part in grads], 0)
    for copy in copies[:half]:
        copy.wait()
    gate = matmul(x, gu[0, :, :units])
    for copy in copies[half:]:
        copy.wait()
    up = matmul(x, gu[1, :, :units])
    down_copy.wait()
    dhidden = matmul_nt(grad, down[...])
    sigmoid = 1.0 / (1.0 + jnp.exp(-gate))
    hidden = (gate * sigmoid * up).astype(BF16)
    dgate = (dhidden * up * sigmoid * (1.0 + gate * (1.0 - sigmoid))).astype(BF16)
    dup = (dhidden * gate * sigmoid).astype(BF16)
    hidden_ref[...] = hidden
    gate_ref[...] = dgate
    up_ref[...] = dup
    block = 512
    for first in range(0, x.shape[1], block):
        columns = slice(first, first + block)
        dx = matmul_nt(dgate, gu[0, columns, :units]) + matmul_nt(dup, gu[1, columns, :units])
        for j in range(count):
            dxs[j][:, columns] = dx[j * rows : (j + 1) * rows, :].astype(dxs[j].dtype)
    for first in range(0, x.shape[1], block):
        columns = slice(first, first + block)
        out = matmul(hidden, down[:, columns])
        for j in range(count):
            outs[j][:, columns] = out[j * rows : (j + 1) * rows, :].astype(outs[j].dtype)


def feed(place, planes, x, grad, w_gate_up, w_down):
    layout, blocks = zip(*w_gate_up)
    rows, width = x[0].shape
    units = w_down.shape[0]
    count = len(x)
    part = shape_of((count * rows, units))
    terms = (shape_of((rows, width), F32), shape_of((rows, width))) * (count // 2)
    got = pl.pallas_call(
        functools.partial(feed_kernel, planes, layout, count),
        out_shape=(part,) * 3 + terms * 2,
        in_specs=[SMEM] + [VMEM] * (2 * count) + [ANY] * (len(blocks) + 1),
        out_specs=(VMEM,) * (3 + 2 * count),
        scratch_shapes=[
            pltpu.VMEM((2, width, blocks[0].shape[-1]), BF16),
            pltpu.VMEM((units, width), BF16),
            pltpu.SemaphoreType.DMA((3,)),
        ],
        compiler_params=params(),
        cost_estimate=cost(12 * count * rows * width * units, 6 * width * units, rows * units),
        name="feed",
    )(place, *x, *grad, *blocks, w_down)
    return got[:3], got[3 : 3 + count], got[3 + count :]


def feed_grad_kernel(planes, chips, count, batches, place, *refs):
    x, refs = refs[:count], refs[count:]
    gates, refs = refs[:batches], refs[batches:]
    ups, refs = refs[:batches], refs[batches:]
    outs, (held, sem) = refs[:-2], refs[-2:]
    width = held.shape[1]
    units = gates[0].shape[1]
    block = 256
    rows = width // (planes * chips)
    copies = []
    dgate = jnp.concatenate([gate[...] for gate in gates], 0)
    dup = jnp.concatenate([up[...] for up in ups], 0)
    if held.shape[2] > units:
        held[:, :, units:] = jnp.zeros((2, width, held.shape[2] - units), BF16)
    for plane in range(planes):
        for first in range(plane * chips * rows, (plane + 1) * chips * rows, block):
            columns = slice(first, first + block)
            left = jnp.concatenate([part[:, columns] for part in x], 0)
            held[0, columns, :units] = matmul_tn(left, dgate).astype(BF16)
            held[1, columns, :units] = matmul_tn(left, dup).astype(BF16)
        for step in range(chips):
            at = (plane * chips + (place[1] ^ step)) * rows
            for side in range(2):
                to = outs[0].at[side] if step == 0 else outs[2 * step - 1 + side]
                copy = pltpu.make_async_copy(
                    held.at[side, pl.ds(pl.multiple_of(at, 16), rows), :],
                    to.at[pl.ds(plane * rows, rows), :],
                    sem,
                )
                copy.start()
                copies.append(copy)
    for copy in copies:
        copy.wait()


def feed_grad(place, planes, chips, x, gates, ups, lanes):
    width, units = x[0].shape[1], gates[0].shape[1]
    tokens = x[0].shape[0] * len(x)
    own = shape_of((2, width // chips, lanes))
    part = shape_of((width // chips, lanes))
    outs = (own,) + (part,) * (2 * chips - 2)
    return pl.pallas_call(
        functools.partial(feed_grad_kernel, planes, chips, len(x), len(gates)),
        out_shape=outs,
        in_specs=[SMEM] + [VMEM] * (len(x) + len(gates) + len(ups)),
        out_specs=(ANY,) * len(outs),
        scratch_shapes=[pltpu.VMEM((2, width, lanes), BF16), pltpu.SemaphoreType.DMA],
        compiler_params=params(),
        cost_estimate=cost(4 * tokens * width * units, 4 * width * units),
        name="feed_grad",
    )(place, *x, *gates, *ups)


def feed_adam_kernel(planes, chips, piece, place, gains, *refs):
    blocks, refs = refs[:planes], refs[planes:]
    ins, outs = refs[:6], refs[6:12]
    gain_grad, held = refs[12], refs[13]
    plane, core = place[0], place[2]
    for step in range(planes):
        for side in range(2):
            held[plane ^ step, core ^ side] = blocks[step][side].astype(F32)
    gain = gains[:, 1:2]
    total = jnp.zeros(gain.shape, F32)
    for part in range(2):
        w, m, u = ins[3 * part : 3 * part + 3]
        grad = jnp.concatenate(
            [
                held[far, c, part, :, at * piece : (at + 1) * piece]
                for far in range(planes)
                for at in range(chips)
                for c in range(2)
            ],
            1,
        )
        weight = w[...]
        total = total + jnp.sum(weight.astype(BF16).astype(F32) * grad, -1, keepdims=True)
        updated = adam_step(weight, m[...], u[...], grad * gain, 0.02)
        for out, value in zip(outs[3 * part : 3 * part + 3], updated):
            out[...] = value
    gain_grad[...] = jnp.broadcast_to(total, gain_grad.shape)


def feed_adam(place, planes, chips, gains, blocks, arrays):
    rows, hidden = arrays[0].shape
    piece = hidden // (2 * planes * chips)
    tile = min(rows, 16)
    whole = pl.BlockSpec((tile, hidden), lambda i: (i, 0))
    lanes = blocks[0].shape[-1]
    block = pl.BlockSpec((2, 2, tile, lanes), lambda i: (0, 0, i, 0))
    two = pl.BlockSpec((tile, 2), lambda i: (i, 0))
    *new, gain_grad = pl.pallas_call(
        functools.partial(feed_adam_kernel, planes, chips, piece),
        grid=(rows // tile,),
        out_shape=(shape_of((rows, hidden), F32),) * 6 + (shape_of((rows, 128), F32),),
        in_specs=[SMEM, two] + [block] * planes + [whole] * 6,
        out_specs=(whole,) * 6 + (pl.BlockSpec((tile, 128), lambda i: (i, 0)),),
        scratch_shapes=[pltpu.VMEM((planes, 2, 2, tile, lanes), F32)],
        compiler_params=params(),
        cost_estimate=cost(40 * rows * hidden, 52 * rows * hidden),
        name="feed_adam",
    )(place, gains, *blocks, *arrays)
    return tuple(new), gain_grad[:, 0]


def attention_adam_kernel(heads, place, gains, *refs):
    members = len(heads)
    blocks, refs = refs[: members // 2], refs[members // 2 :]
    ins, refs = refs[:9], refs[9:]
    outs, gain_grad, held = refs[:9], refs[9], refs[10]
    chip, core = place[1], place[2]
    own_q = len(heads[0]) * HEAD_DIM
    sharing = members // KV_HEADS
    for step in range(members // 2):
        for side in range(2):
            held[(chip ^ step) * 2 + (core ^ side)] = blocks[step][side].astype(F32)
    kept = {head: (f, at) for f, own in enumerate(heads) for at, head in enumerate(own)}

    def shared(first):
        return jnp.concatenate(
            [
                sum(
                    held[group * sharing + one, :, first : first + HEAD_DIM]
                    for one in range(sharing)
                )
                for group in range(KV_HEADS)
            ],
            1,
        )

    query = jnp.concatenate(
        [
            held[kept[head][0], :, kept[head][1] * HEAD_DIM : (kept[head][1] + 1) * HEAD_DIM]
            for head in range(HEADS)
        ],
        1,
    )
    gain = gains[:, 0:1]
    total = jnp.zeros(gain.shape, F32)
    for part, grad in enumerate((query, shared(own_q), shared(own_q + HEAD_DIM))):
        w, m, u = ins[3 * part : 3 * part + 3]
        weight = w[...]
        total = total + jnp.sum(weight.astype(BF16).astype(F32) * grad, -1, keepdims=True)
        updated = adam_step(weight, m[...], u[...], grad * gain, 0.02)
        for out, value in zip(outs[3 * part : 3 * part + 3], updated):
            out[...] = value
    gain_grad[...] = jnp.broadcast_to(total, gain_grad.shape)


def attention_adam(place, heads, gains, blocks, arrays):
    rows = arrays[0].shape[0]
    tile = min(rows, 16)
    lanes = blocks[0].shape[-1]
    wholes = [pl.BlockSpec((tile, array.shape[1]), lambda i: (i, 0)) for array in arrays]
    block = pl.BlockSpec((2, tile, lanes), lambda i: (0, i, 0))
    two = pl.BlockSpec((tile, 2), lambda i: (i, 0))
    *new, gain_grad = pl.pallas_call(
        functools.partial(attention_adam_kernel, heads),
        grid=(rows // tile,),
        out_shape=tuple(shape_of(array.shape, F32) for array in arrays)
        + (shape_of((rows, 128), F32),),
        in_specs=[SMEM, two] + [block] * len(blocks) + wholes,
        out_specs=tuple(wholes) + (pl.BlockSpec((tile, 128), lambda i: (i, 0)),),
        scratch_shapes=[pltpu.VMEM((len(heads), tile, lanes), F32)],
        compiler_params=params(),
        cost_estimate=cost(40 * arrays[0].size, 28 * arrays[0].size),
        name="attention_adam",
    )(place, gains, *blocks, *arrays)
    return tuple(new), gain_grad[:, 0]


def segment_starts(lengths_row, length):
    count = lengths_row.shape[0]
    ahead = jnp.arange(count)[:, None] < jnp.arange(count)[None, :]
    starts = jnp.sum(jnp.where(ahead, lengths_row[:, None], 0), 0, dtype=jnp.int32)
    ends = starts + lengths_row
    places = jnp.arange(length, dtype=jnp.int32)
    within = (places[:, None] >= starts[None, :]) & (places[:, None] < ends[None, :])
    return jnp.sum(jnp.where(within, starts[None, :], 0), 1, dtype=jnp.int32)


def rope_tables(positions):
    half = HEAD_DIM // 2
    freqs = jnp.exp(jnp.arange(half, dtype=F32) * (-2.0 * math.log(ROPE_BASE) / HEAD_DIM))
    angles = positions.astype(F32)[:, None] * freqs[None, :]
    cosine = jnp.cos(angles)
    sine = jnp.sin(angles)
    return (
        jnp.concatenate([cosine] * 4, 1),
        jnp.concatenate([-sine, sine, -sine, sine], 1),
    )


def local(
    tokens,
    out_grad,
    seq_lengths,
    query_weight,
    query_first,
    query_second,
    key_weight,
    key_first,
    key_second,
    value_weight,
    value_first,
    value_second,
    output_weight,
    output_first,
    output_second,
    gate_weight,
    gate_first,
    gate_second,
    up_weight,
    up_first,
    up_second,
    down_weight,
    down_first,
    down_second,
    norm_gains,
    gains_first,
    gains_second,
):
    planes = lax.axis_size("dp")
    members = lax.axis_size("fsdp")
    chips = members // 2
    plane = lax.axis_index("dp")
    index = lax.axis_index("fsdp")
    chip = index // 2
    core = index % 2
    place = jnp.stack([plane, chip, core]).astype(jnp.int32)
    spot = jnp.stack([plane, index]).astype(jnp.int32)
    count, width = tokens.shape
    length = count * members
    slice_rows = query_weight.shape[0]
    own_q = query_weight.shape[1] // members
    sharing = members // KV_HEADS
    same_core = [list(range(c, members, 2)) for c in range(2)]

    stages = planes.bit_length() - 1
    chip_stages = chips.bit_length() - 1
    everyone = range(planes)
    heads = head_order(planes, members)
    head_rows = HEADS == planes * members and planes == chips

    def both_cores(blocks):
        return [b for block in blocks for b in (block, core_swap(block))]

    def over_cores(terms):
        return terms[0] + core_swap(terms[1]).astype(F32)

    gains = norm_gains.astype(BF16).astype(F32)
    gain_columns = gains.T
    gu_mine, gu_other, qkv_mine, qkv_other = pack(
        place,
        planes,
        chips,
        gain_columns,
        gate_weight,
        up_weight,
        query_weight,
        key_weight,
        value_weight,
    )
    w_down = lax.all_gather(
        down_weight.astype(BF16), "fsdp", axis=0, tiled=True, axis_index_groups=same_core
    )
    start = segment_starts(seq_lengths[0], length)
    starts = (start[:, None], start[None, :])
    gu_mine, gu_other, qkv_mine, qkv_other, starts, place, spot, output_rows = together(
        gu_mine, gu_other, qkv_mine, qkv_other, starts, place, spot, output_weight.astype(BF16)
    )

    qkv_pairs = swap_pairs(qkv_mine, qkv_other)
    gu_pairs = swap_pairs(gu_mine, gu_other)
    qkv_got = exchange(qkv_pairs, chip_send)
    gu_near = plane_send(gu_pairs[1], 1)
    out_rows = gather_stage({0: output_rows}, plane_send, planes, 1)
    qkv_got, gu_pairs, gu_near, tokens, out_rows = together(
        qkv_got, gu_pairs, gu_near, tokens, out_rows
    )

    gu_got = [gu_pairs[0], gu_near] + [
        plane_send(gu_pairs[step], step) for step in range(2, planes)
    ]
    token_blocks = gather(tokens, chip_send, chips)
    cosine, sine = rope_tables(jnp.arange(length, dtype=jnp.int32) - start)
    gu_got, qkv_got, token_blocks, cosine, sine, w_down, out_rows = together(
        gu_got, qkv_got, token_blocks, cosine, sine, w_down, out_rows
    )

    tokens_mine = jnp.stack(token_blocks)
    tokens_other = core_swap(tokens_mine)
    gu_rows = gather_rows(plane, core, gu_got)
    qkv_rows = gather_rows(chip, core, qkv_got)
    steps = [step for step in range(chips) if ones(step) <= 1]
    w_gate_up = [gu_rows] + [chip_send(gu_rows, step) for step in steps[1:]]
    w_qkv = gather_stage({0: qkv_rows}, plane_send, planes, 1)
    w_qkv, out_rows = together(w_qkv, out_rows)
    for stage in range(2, stages + 1):
        w_qkv = gather_stage(w_qkv, plane_send, planes, stage)
    w_qkv = [w_qkv[far] for far in everyone]
    for stage in range(2, stages + 1):
        out_rows = gather_stage(out_rows, plane_send, planes, stage)
    out_rows = jnp.stack([out_rows[far] for far in everyone])
    w_gate_up, w_qkv, out_grad, tokens_mine, tokens_other, out_rows = together(
        w_gate_up, w_qkv, out_grad, tokens_mine, tokens_other, out_rows
    )

    gate_up = {step: (block[0], block[1]) for step, block in zip(steps, w_gate_up)}
    for stage in range(2, chip_stages + 1):
        for step in range(1, chips):
            if ones(step) == stage:
                top = 1 << (step.bit_length() - 1)
                gate_up[step] = (
                    chip_send(gate_up[step & (step - 1)][0], step & -step),
                    chip_send(gate_up[step ^ top][1], top),
                )
    more = [step for step in range(chips) if ones(step) > 1]
    layout = [(step, None) for step in steps] + [(step, side) for step in more for side in range(2)]
    w_gate_up = w_gate_up + [gate_up[step][side] for step in more for side in range(2)]
    normed, queries, keys_values, attended = attend(
        spot, tokens_mine, tokens_other, w_qkv, starts[0], cosine, sine
    )
    hop = members // planes
    own_plane = index // hop

    def out_route(turn_no):
        return [(i, ((turn_no + i) % planes) * hop + i // planes) for i in range(members)]

    if head_rows:
        out_got = [
            lax.dynamic_index_in_dim(out_rows, (chip ^ step) ^ plane, 0, keepdims=False)
            for step in range(chips)
        ]
        w_output = [out_got[0]] + [chip_send(out_got[step], step) for step in range(1, chips)]
    else:
        w_output = jnp.zeros((planes, slice_rows, width), BF16)
        for turn_no in range(planes):
            sent = lax.dynamic_index_in_dim(
                out_rows, ((turn_no + index) % planes) ^ plane, 0, keepdims=False
            )
            got = lax.ppermute(sent, "fsdp", out_route(turn_no))
            spare = (own_plane + planes - turn_no) % planes
            w_output = lax.dynamic_update_index_in_dim(w_output, got, spare, 0)
        w_output = [w_output.reshape(planes * slice_rows, width)]
    w_gate_up, attended, w_output, out_grad = together(w_gate_up, attended, w_output, out_grad)

    w_gate_up = list(zip(layout, w_gate_up))
    w_output = jnp.concatenate(w_output)
    out_grad_blocks = gather_stage({0: out_grad}, plane_send, planes, 1)
    own_tokens = tokens.astype(F32)
    mixed = [over_cores(terms) for terms in zip(*project(attended, w_output, chips))]
    mixed = mixed[:1] + [
        chip_send(mixed[step].astype(BF16), step).astype(F32) for step in range(1, chips)
    ]
    resid = own_tokens + sum(mixed[1:], mixed[0])
    resid, out_grad_blocks = together(resid, out_grad_blocks)

    scale_two = rms_scale(resid)
    own_normed_two = (resid * scale_two).astype(BF16)
    normed_blocks = gather_stage({0: own_normed_two}, plane_send, planes, 1)
    out_grad_pairs = {far: [block, core_swap(block)] for far, block in out_grad_blocks.items()}
    normed_blocks, out_grad_pairs, out_grad_blocks = together(
        normed_blocks, out_grad_pairs, out_grad_blocks
    )

    x = {far: [block, core_swap(block)] for far, block in normed_blocks.items()}
    x, out_grad_pairs = together(x, out_grad_pairs)
    fed = []
    fed_order = []
    sums = {}
    result = {}
    last = []
    sent = []
    for stage in range(1, stages + 1):
        batch = [far for far in reversed(everyone) if ones(far) == stage]
        if stage == stages:
            batch.append(0)
        fed_order += batch
        parts, outs, dxs = feed(
            place,
            planes,
            [part for far in batch for part in x[far]],
            [part for far in batch for part in out_grad_pairs[far]],
            w_gate_up,
            w_down,
        )
        last += [plane_send(sums[far].astype(BF16), far) for far in sent]
        more = gather_stage(normed_blocks, plane_send, planes, stage + 1)
        more_grad = gather_stage(out_grad_blocks, plane_send, planes, stage + 1)
        parts, outs, dxs, last, normed_blocks, out_grad_blocks = together(
            parts, outs, dxs, last, more, more_grad
        )
        fed.append(parts)
        for blocks, pairs in ((normed_blocks, x), (out_grad_blocks, out_grad_pairs)):
            for far, block in blocks.items():
                if far not in pairs:
                    pairs[far] = [block, core_swap(block)]
        for at, far in enumerate(batch):
            sums[far] = over_cores(dxs[2 * at : 2 * at + 2])
            result[far] = over_cores(outs[2 * at : 2 * at + 2])
        x, sums, out_grad_pairs = together(x, sums, out_grad_pairs)
        sent = [far for far in batch if far]
    last += [plane_send(sums[far].astype(BF16), far) for far in sent]
    hidden, grad_gate, grad_up = zip(*fed)
    lanes = w_gate_up[0][1].shape[-1]
    fed_x = [part for far in fed_order for part in x[far]]
    fed_grad = [part for far in fed_order for part in out_grad_pairs[far]]
    grads = feed_grad(place, planes, chips, fed_x, grad_gate, grad_up, lanes)
    grad_normed_two, last, grads, result = together(sums[0], last, grads, result)
    grad_normed_two = sum([part.astype(F32) for part in last], grad_normed_two)

    grad_resid = (
        out_grad.astype(F32)
        + scale_two * grad_normed_two
        - resid
        * (scale_two * scale_two * scale_two)
        * jnp.mean(grad_normed_two * resid, -1, keepdims=True)
    )
    own_grad = grad_resid.astype(BF16)
    own_grad, result, hidden = together(own_grad, result, hidden)

    grad_blocks = gather(own_grad, chip_send, chips)
    for stage in range(stages, 1, -1):
        result = scatter_stage(result, plane_send, stage)
    grad_down = rows_grad(jnp.concatenate(hidden), fed_grad)
    grad_blocks, result, grad_down = together(grad_blocks, result, grad_down)

    grad_attn_out = both_cores(grad_blocks)
    grad_attn_out, grads, result = together(grad_attn_out, grads, result)

    result = scatter_stage(result, plane_send, 1)[0]
    grad_gate_up = {step: grads[2 * step - 1 : 2 * step + 1] for step in range(1, chips)}

    def plus(one, two):
        return (one.astype(F32) + two.astype(F32)).astype(BF16)

    for stage in range(chip_stages, 1, -1):
        for step in range(chips - 1, 0, -1):
            if ones(step) == stage:
                top = 1 << (step.bit_length() - 1)
                low = step & (step - 1)
                gate, up = grad_gate_up.pop(step)
                gate, up = chip_send(gate, step & -step), chip_send(up, top)
                grad_gate_up[low] = (plus(grad_gate_up[low][0], gate), grad_gate_up[low][1])
                low = step ^ top
                grad_gate_up[low] = (grad_gate_up[low][0], plus(grad_gate_up[low][1], up))
    grad_gate_up = {step: jnp.stack(pair) for step, pair in grad_gate_up.items()}
    grad_qkv = attend_back(
        spot, queries, keys_values, w_output, grad_attn_out, starts[1], cosine, sine
    )
    grad_qkv, result, grad_gate_up, grad_attn_out = together(
        grad_qkv, result, grad_gate_up, grad_attn_out
    )
    result = (resid + result).astype(BF16)

    grad_gate_up = [grads[0]] + [chip_send(part, step) for step, part in grad_gate_up.items()]
    grad_w_qkv = dict(enumerate(qkv_grad(spot, normed, grad_qkv, planes)))
    for stage in range(stages, 0, -1):
        grad_w_qkv = scatter_stage(grad_w_qkv, plane_send, stage)
    mixed = project_back(spot, grad_qkv, w_qkv, chips)
    grad_output = rows_grad(attended, grad_attn_out).reshape(planes, slice_rows, width)
    grad_gate_up, grad_w_qkv, mixed, grad_output = together(
        grad_gate_up, grad_w_qkv[0], mixed, grad_output
    )

    gu_pairs = swap_pairs(*spread_rows(plane, core, grad_gate_up, planes))
    qkv_pairs = swap_pairs(*spread_rows(chip, core, [grad_w_qkv], chips))
    mixed = [(mine, core_swap(other)) for mine, other in zip(*mixed)]
    gu_pairs, qkv_pairs, mixed, grad_output, grad_down = together(
        gu_pairs, qkv_pairs, mixed, grad_output, grad_down
    )

    grad_down_weight = lax.psum_scatter(
        grad_down, "fsdp", scatter_dimension=0, tiled=True, axis_index_groups=same_core
    ).astype(F32)
    got = exchange(qkv_pairs, chip_send)
    mixed = [mine + other.astype(F32) for mine, other in mixed]
    far_pairs = gu_pairs[planes // 2 + 1 :]
    near_got = exchange(gu_pairs[: planes // 2 + 1], plane_send)
    far_pairs, near_got, got, mixed, grad_output = together(
        far_pairs, near_got, got, mixed, grad_output
    )

    far_got = [
        plane_send(pair, planes // 2 + 1 + step) for step, pair in enumerate(far_pairs)
    ]
    grad_gate_up = near_got + far_got
    mixed = dict(enumerate(mixed))
    for stage in range(chip_stages, 1, -1):
        mixed = scatter_stage(mixed, chip_send, stage)
    if head_rows:
        parts = [grad_output[0]] + [chip_send(grad_output[step], step) for step in range(1, chips)]
        parts = jnp.stack(parts)
        out_parts = [
            lax.dynamic_index_in_dim(parts, (plane ^ far) ^ chip, 0, keepdims=False)
            for far in everyone
        ]
    else:
        parts = jnp.zeros((planes, slice_rows, width), BF16)
        for turn_no in range(planes):
            spare = (own_plane + planes - turn_no) % planes
            sent = lax.dynamic_index_in_dim(grad_output, spare, 0, keepdims=False)
            part = lax.ppermute(sent, "fsdp", [(b, a) for a, b in out_route(turn_no)])
            parts = lax.dynamic_update_index_in_dim(
                parts, part, ((turn_no + index) % planes) ^ plane, 0
            )
        out_parts = [parts[far] for far in everyone]
    attention_new, grad_gain_one = attention_adam(
        place,
        heads,
        gain_columns,
        got,
        (
            query_weight,
            query_first,
            query_second,
            key_weight,
            key_first,
            key_second,
            value_weight,
            value_first,
            value_second,
        ),
    )
    grad_gate_up, grad_gain_one, out_parts, mixed, grad_down_weight = together(
        grad_gate_up, grad_gain_one, out_parts, mixed, grad_down_weight
    )

    grad_normed = scatter_stage(mixed, chip_send, 1)[0]
    grad_output_weight = scatter_sum(out_parts, plane_send)
    scale_one = rms_scale(own_tokens)
    grad_tokens = (
        grad_resid
        + scale_one * grad_normed
        - own_tokens
        * (scale_one * scale_one * scale_one)
        * jnp.mean(grad_normed * own_tokens, -1, keepdims=True)
    )
    fed_weights, grad_gain_two = feed_adam(
        place,
        planes,
        chips,
        gain_columns,
        grad_gate_up,
        (gate_weight, gate_first, gate_second, up_weight, up_first, up_second),
    )
    gain_grads = jnp.stack([grad_gain_one, grad_gain_two])
    updated = (
        attention_new
        + adam_step(output_weight, output_first, output_second, grad_output_weight, 0.1)
        + fed_weights
        + adam_step(down_weight, down_first, down_second, grad_down_weight, 0.02)
        + adam_step(norm_gains, gains_first, gains_second, gain_grads, 0.2)
    )
    return (result, grad_tokens) + updated


def solution(mesh):
    rows = P(("dp", "fsdp"), None)
    columns = P(None, ("dp", "fsdp"))
    in_specs = (rows, rows, P("dp", None)) + (rows,) * 21 + (columns,) * 3
    out_specs = (rows, rows) + (rows,) * 21 + (columns,) * 3
    return jax.shard_map(local, mesh=mesh, in_specs=in_specs, out_specs=out_specs, check_vma=False)
```

```python
import functools
import math

import jax
import jax.numpy as jnp
from jax import lax
from jax.experimental import pallas as pl
from jax.experimental.pallas import tpu as pltpu
from jax.sharding import PartitionSpec as P

HEADS = 32
KV_HEADS = 4
HEAD_DIM = 64
STEP = 3

NORM_EPS = 1e-05
ROPE_BASE = 10000.0
BETA = 0.5
ADAM_EPS = 1e-08
DECAY = 0.1
MASKED = -1e30
PAIR = 2 * HEAD_DIM
BF16 = jnp.bfloat16
F32 = jnp.float32


def matmul(left, right):
    return jnp.dot(left, right, preferred_element_type=F32)


def matmul_tn(left, right):
    return lax.dot_general(left, right, (((0,), (0,)), ((), ())), preferred_element_type=F32)


def matmul_nt(left, right):
    return lax.dot_general(left, right, (((1,), (1,)), ((), ())), preferred_element_type=F32)


def rms_scale(values):
    return lax.rsqrt(jnp.mean(values * values, -1, keepdims=True) + NORM_EPS)


def adam_step(master, first_moment, second_moment, gradient, rate):
    first_new = BETA * first_moment + (1.0 - BETA) * gradient
    second_new = BETA * second_moment + (1.0 - BETA) * gradient * gradient
    correction = 1.0 - BETA**STEP
    master_new = master - rate * (
        first_new / correction / (jnp.sqrt(second_new / correction) + ADAM_EPS) + DECAY * master
    )
    return (master_new, first_new, second_new)


def core_swap(value):
    members = lax.axis_size("fsdp")
    return lax.ppermute(value, "fsdp", [(i, i ^ 1) for i in range(members)])


def chip_send(value, step):
    members = lax.axis_size("fsdp")
    return lax.ppermute(value, "fsdp", [(i, i ^ (2 * step)) for i in range(members)])


def plane_send(value, step):
    planes = lax.axis_size("dp")
    return lax.ppermute(value, "dp", [(i, i ^ step) for i in range(planes)])


def gather(own, send, count):
    return [own] + [send(own, step) for step in range(1, count)]


def ones(step):
    return step.bit_count()


def gather_stage(got, send, count, stage):
    more = {j: send(got[j & (j - 1)], j & -j) for j in range(count) if ones(j) == stage}
    return {**got, **more}


def scatter_stage(parts, send, stage):
    parts = dict(parts)
    for j in sorted(parts, reverse=True):
        if ones(j) == stage:
            got = send(parts.pop(j).astype(BF16), j & -j)
            parts[j & (j - 1)] = parts[j & (j - 1)].astype(F32) + got.astype(F32)
    return parts


def gather_terms(parts, send):
    return [parts[0]] + [send(parts[step], step) for step in range(1, len(parts))]


def scatter_sum(parts, send):
    return sum(part.astype(F32) for part in gather_terms(parts, send))


def together(*values):
    return lax.optimization_barrier(values)


def swap_pairs(mine, other):
    got = core_swap(other)
    return [jnp.stack([mine[step], got[step]]) for step in range(mine.shape[0])]


def exchange(pairs, send):
    return pairs[:1] + [send(pairs[step], step) for step in range(1, len(pairs))]


def by_offset(blocks, index):
    count = blocks.shape[0]
    return jnp.stack(
        [lax.dynamic_index_in_dim(blocks, j ^ index, 0, keepdims=False) for j in range(count)]
    )


def lane_ids(shape):
    return lax.broadcasted_iota(jnp.int32, shape, len(shape) - 1)


def turn(values, cosine, sine):
    low_half = lane_ids(values.shape) % HEAD_DIM < HEAD_DIM // 2
    shifted = jnp.where(
        low_half,
        pltpu.roll(values, PAIR - HEAD_DIM // 2, 1),
        pltpu.roll(values, HEAD_DIM // 2, 1),
    )
    return values * cosine + shifted * sine


VMEM = pl.BlockSpec(memory_space=pltpu.VMEM)
SMEM = pl.BlockSpec(memory_space=pltpu.SMEM)
ANY = pl.BlockSpec(memory_space=pl.ANY)


def params(mib=56):
    return pltpu.CompilerParams(vmem_limit_bytes=mib * 2**20)


def shape_of(shape, dtype=BF16):
    return jax.ShapeDtypeStruct(shape, dtype)


def cost(flops, moved, exps=0):
    return pl.CostEstimate(
        flops=3 * int(flops), bytes_accessed=3 * int(moved), transcendentals=3 * int(exps)
    )


def whole_lanes(width):
    return -(-width // 128) * 128


def head_order(planes, members):
    chips = members // 2
    if HEADS == planes * members and planes == chips:
        return [
            [f // 2 * members + 2 * ((f // 2) ^ step) + f % 2 for step in range(chips)]
            for f in range(members)
        ]
    share = HEADS // members
    return [list(range(f * share, (f + 1) * share)) for f in range(members)]


def pack_kernel(planes, chips, piece, place, gains, gate, up, query, key, value, *outs):
    gu_mine, gu_other, qkv_mine, qkv_other = outs
    plane, chip, core = place[0], place[1], place[2]
    sharing = 2 * chips // KV_HEADS
    heads = head_order(planes, 2 * chips)

    def put(mine, other, core_to, index, block):
        @pl.when(core == core_to)
        def _():
            mine[index] = block

        @pl.when(core != core_to)
        def _():
            other[index] = block

    def rounded(block, row):
        return (block.astype(BF16).astype(F32) * gains[:, row : row + 1]).astype(BF16)

    for to in range(2 * chips):
        head = slice(to // sharing * HEAD_DIM, (to // sharing + 1) * HEAD_DIM)
        columns = [query[:, h * HEAD_DIM : (h + 1) * HEAD_DIM] for h in heads[to]]
        block = jnp.concatenate(columns + [key[:, head], value[:, head]], 1)
        put(qkv_mine, qkv_other, to % 2, (to // 2) ^ chip, rounded(block, 0))
    for side, weight in enumerate((gate, up)):
        for to in range(2 * planes):
            starts = [((to // 2 * chips + c) * 2 + to % 2) * piece for c in range(chips)]
            columns = [weight[:, s : s + piece] for s in starts]
            spare = gu_mine.shape[-1] - chips * piece
            if spare:
                columns.append(jnp.zeros((weight.shape[0], spare), F32))
            block = rounded(jnp.concatenate(columns, 1), 1)
            put(gu_mine.at[:, side], gu_other.at[:, side], to % 2, (to // 2) ^ plane, block)


def whole_lanes(width):
    return -(-width // 128) * 128


def pack(place, planes, chips, gains, gate, up, query, key, value):
    rows, hidden = gate.shape
    gu = shape_of((planes, 2, rows, whole_lanes(hidden // (2 * planes))))
    qkv = shape_of((chips, rows, query.shape[1] // (2 * chips) + PAIR))
    return pl.pallas_call(
        functools.partial(pack_kernel, planes, chips, hidden // (2 * planes * chips)),
        out_shape=(gu, gu, qkv, qkv),
        in_specs=[SMEM] + [VMEM] * 6,
        out_specs=(VMEM,) * 4,
        compiler_params=params(),
        cost_estimate=cost(0, rows * hidden * 12),
        name="pack",
    )(place, gains, gate, up, query, key, value)


def gather_rows_kernel(members, place, *refs):
    blocks, out = refs[:-1], refs[-1]
    first, core = place[0], place[1]
    rows = blocks[0].shape[-2]
    for step, block in enumerate(blocks):
        for side in range(2):
            at = ((first ^ step) * 2 + (core ^ side)) * rows
            if len(block.shape) == 3:
                out[pl.ds(pl.multiple_of(at, 16), rows), :] = block[side]
            else:
                for part in range(2):
                    out[part, pl.ds(pl.multiple_of(at, 16), rows), :] = block[side, part]


def gather_rows(first, core, pairs):
    lead, (rows, width) = pairs[0].shape[1:-2], pairs[0].shape[-2:]
    return pl.pallas_call(
        functools.partial(gather_rows_kernel, 2 * len(pairs)),
        out_shape=shape_of(lead + (2 * len(pairs) * rows, width)),
        in_specs=[SMEM] + [VMEM] * len(pairs),
        out_specs=VMEM,
        compiler_params=params(),
        cost_estimate=cost(0, pairs[0].size * len(pairs) * 4),
        name="gather_rows",
    )(jnp.stack([first, core]), *pairs)


def spread_rows_kernel(place, *refs):
    terms, (mine, other) = refs[:-2], refs[-2:]
    first, core = place[0], place[1]
    count = mine.shape[0]
    rows = mine.shape[-2]
    for step in range(count):
        for side, out in enumerate((mine, other)):
            at = pl.ds(pl.multiple_of(((first ^ step) * 2 + (core ^ side)) * rows, 16), rows)
            if len(mine.shape) == 3:
                out[step] = sum(t[at, :].astype(F32) for t in terms).astype(BF16)
            else:
                for part in range(2):
                    out[step, part] = sum(t[part, at, :].astype(F32) for t in terms).astype(BF16)


def spread_rows(first, core, terms, count):
    whole = terms[0]
    rows = whole.shape[-2] // (2 * count)
    out = shape_of((count,) + whole.shape[:-2] + (rows, whole.shape[-1]))
    return pl.pallas_call(
        spread_rows_kernel,
        out_shape=(out, out),
        in_specs=[SMEM] + [VMEM] * len(terms),
        out_specs=(VMEM, VMEM),
        compiler_params=params(),
        cost_estimate=cost(0, whole.size * 6),
        name="spread_rows",
    )(jnp.stack([first, core]), *terms)


def attend_kernel(members, pairs, planes, place, start_ref, cos_ref, sin_ref, *refs):
    tokens, refs = refs[:2], refs[2:]
    weights, refs = refs[:planes], refs[planes:]
    normed_ref, q_ref, kv_ref, o_ref = refs
    plane, index = place[0], place[1]
    rows = tokens[0].shape[1]
    length = rows * members
    even = lane_ids((rows, PAIR)) < HEAD_DIM
    depth = weights[0].shape[0]
    for j in range(members):
        values = tokens[j % 2][j // 2].astype(F32)
        normed_ref[j * rows : (j + 1) * rows, :] = (values * rms_scale(values)).astype(BF16)
    block = min(2 * rows, 256)
    per = block // rows
    for first in range(0, length, block):
        qkv = None
        for step in range(planes):
            columns = pl.ds(pl.multiple_of((plane ^ step) * depth, 128), depth)
            term = matmul(normed_ref[first : first + block, columns], weights[step][...])
            qkv = term if qkv is None else qkv + term
        for part in range(per):
            j = first // rows + part
            here = pl.ds(pl.multiple_of((j ^ index) * rows, rows), rows)
            cosine = cos_ref[here, :]
            sine = sin_ref[here, :]
            piece = qkv[part * rows : (part + 1) * rows, :]
            for pair in range(pairs):
                lanes = slice(pair * PAIR, (pair + 1) * PAIR)
                turned = turn(piece[:, lanes], cosine, sine).astype(BF16).astype(F32)
                q_ref[here, lanes] = (turned * HEAD_DIM**-0.5).astype(BF16)
            both = piece[:, pairs * PAIR :]
            kv_ref[here, :] = jnp.where(even, turn(both, cosine, sine), both).astype(BF16)
    for first in range(0, length, block):
        reach = first + block
        both = kv_ref[:reach, :].astype(F32)
        left = lane_ids(both.shape) < HEAD_DIM
        keys_even = jnp.where(left, both, 0.0)
        values_odd = jnp.where(left, 0.0, both)
        keys = (keys_even.astype(BF16), pltpu.roll(keys_even, HEAD_DIM, 1).astype(BF16))
        values = (pltpu.roll(values_odd, HEAD_DIM, 1).astype(BF16), values_odd.astype(BF16))
        query_at = first + lax.broadcasted_iota(jnp.int32, (block, reach), 0)
        key_at = lax.broadcasted_iota(jnp.int32, (block, reach), 1)
        allowed = (key_at <= query_at) & (key_at >= start_ref[first:reach, :])
        for pair in range(pairs):
            lanes = slice(pair * PAIR, (pair + 1) * PAIR)
            query = q_ref[first:reach, lanes]
            mixed = jnp.zeros((block, PAIR), F32)
            for side in range(2):
                scores = jnp.where(allowed, matmul_nt(query, keys[side]), MASKED)
                raised = jnp.exp(scores - jnp.max(scores, -1, keepdims=True))
                probs = raised * (1.0 / jnp.sum(raised, -1, keepdims=True))
                mixed = mixed + matmul(probs.astype(BF16), values[side])
            mixed = mixed.astype(BF16)
            for part in range(per):
                j = first // rows + part
                there = pl.ds(pl.multiple_of((j ^ index) * rows, rows), rows)
                o_ref[there, lanes] = mixed[part * rows : (part + 1) * rows, :]


def attend(place, mine, other, weights, start, cosine, sine):
    members, planes = 2 * mine.shape[0], len(weights)
    rows, width = mine.shape[1:]
    length = members * rows
    pairs = weights[0].shape[1] // PAIR - 1
    return pl.pallas_call(
        functools.partial(attend_kernel, members, pairs, planes),
        out_shape=(
            shape_of((length, width)),
            shape_of((length, pairs * PAIR)),
            shape_of((length, PAIR)),
            shape_of((length, pairs * PAIR)),
        ),
        in_specs=[SMEM] + [VMEM] * (5 + planes),
        out_specs=(VMEM,) * 4,
        compiler_params=params(),
        cost_estimate=cost(
            2 * length * width * (pairs + 1) * PAIR + 3 * length * length * pairs * PAIR,
            length * width * 4,
            length * length * pairs,
        ),
        name="attend",
    )(place, start, cosine, sine, mine, other, *weights)


def attend_back_kernel(members, pairs, place, start_ref, cos_ref, sin_ref, q_ref, kv_ref, w_ref, *refs):
    grads, refs = refs[:members], refs[members:]
    out_ref, do_ref, dk_ref, dv_ref = refs
    length = q_ref.shape[0]
    rows = length // members
    index = place[1]
    block = min(2 * rows, 256)
    per = block // rows
    for j in range(0, members, 2):
        grad = jnp.concatenate([grads[j][...], grads[j + 1][...]], 0)
        do_ref[j * rows : (j + 2) * rows, :] = matmul_nt(grad, w_ref[...]).astype(BF16)
    dk_ref[...] = jnp.zeros_like(dk_ref)
    dv_ref[...] = jnp.zeros_like(dv_ref)
    for first in range(0, length, block):
        reach = first + block
        both = kv_ref[:reach, :].astype(F32)
        left = lane_ids(both.shape) < HEAD_DIM
        keys_even = jnp.where(left, both, 0.0)
        values_odd = jnp.where(left, 0.0, both)
        keys = (keys_even.astype(BF16), pltpu.roll(keys_even, HEAD_DIM, 1).astype(BF16))
        values = (pltpu.roll(values_odd, HEAD_DIM, 1).astype(BF16), values_odd.astype(BF16))
        key_at = lax.broadcasted_iota(jnp.int32, (reach, block), 0)
        query_at = first + lax.broadcasted_iota(jnp.int32, (reach, block), 1)
        allowed = (key_at <= query_at) & (key_at >= start_ref[:, first:reach])
        half = lane_ids((block, PAIR)) < HEAD_DIM
        theres = [
            pl.ds(pl.multiple_of(((first // rows + part) ^ index) * rows, rows), rows)
            for part in range(per)
        ]
        for pair in range(pairs):
            lanes = slice(pair * PAIR, (pair + 1) * PAIR)
            query = q_ref[first:reach, lanes]
            grad = jnp.concatenate([do_ref[there, lanes] for there in theres], 0)
            dq = jnp.zeros((block, PAIR), F32)
            for side in range(2):
                keep = half if side == 0 else ~half
                query_side = jnp.where(keep, query.astype(F32), 0.0).astype(BF16)
                grad_side = jnp.where(keep, grad.astype(F32), 0.0).astype(BF16)
                scores = jnp.where(allowed, matmul_nt(keys[side], query), MASKED)
                raised = jnp.exp(scores - jnp.max(scores, 0, keepdims=True))
                probs = raised * (1.0 / jnp.sum(raised, 0, keepdims=True))
                dp = matmul_nt(values[side], grad)
                centre = jnp.sum(probs * dp, 0, keepdims=True)
                ds = (probs * (dp - centre)).astype(BF16)
                dv_ref[:reach, :] += matmul(probs.astype(BF16), grad_side)
                dk_ref[:reach, :] += matmul(ds, query_side)
                dq = dq + matmul_tn(ds, keys[side])
            dq = dq * HEAD_DIM**-0.5
            for part in range(per):
                piece = dq[part * rows : (part + 1) * rows, :]
                here = slice(first + part * rows, first + (part + 1) * rows)
                out_ref[theres[part], lanes] = turn(
                    piece, cos_ref[here, :], -sin_ref[here, :]
                ).astype(BF16)
    left = lane_ids((rows, PAIR)) < HEAD_DIM
    for j in range(members):
        here = slice(j * rows, (j + 1) * rows)
        there = pl.ds(pl.multiple_of((j ^ index) * rows, rows), rows)
        dk = dk_ref[here, :]
        dv = dv_ref[here, :]
        dk = turn(dk + pltpu.roll(dk, HEAD_DIM, 1), cos_ref[here, :], -sin_ref[here, :])
        dv = dv + pltpu.roll(dv, HEAD_DIM, 1)
        out_ref[there, pairs * PAIR :] = jnp.where(left, dk, dv).astype(BF16)


def attend_back(place, queries, keys_values, w_output, grads, start, cosine, sine):
    length, width = queries.shape
    pairs = width // PAIR
    members = len(grads)
    model = grads[0].shape[1]
    return pl.pallas_call(
        functools.partial(attend_back_kernel, members, pairs),
        out_shape=shape_of((length, width + PAIR)),
        in_specs=[SMEM] + [VMEM] * (6 + members),
        out_specs=VMEM,
        scratch_shapes=[
            pltpu.VMEM((length, width), BF16),
            pltpu.VMEM((length, PAIR), F32),
            pltpu.VMEM((length, PAIR), F32),
        ],
        compiler_params=params(),
        cost_estimate=cost(
            2 * length * width * model + 7 * length * length * width,
            length * model * 2,
            length * length * pairs,
        ),
        name="attend_back",
    )(place, start, cosine, sine, queries, keys_values, w_output, *grads)


def project_kernel(count, left_ref, weight_ref, *outs):
    rows = left_ref.shape[0] // (2 * count)
    for step in range(count):
        whole = matmul(left_ref[2 * step * rows : 2 * (step + 1) * rows, :], weight_ref[...])
        outs[step][...] = whole[:rows, :]
        outs[count + step][...] = whole[rows:, :].astype(BF16)


def project(left, weight, count):
    rows, width = left.shape[0] // (2 * count), weight.shape[1]
    outs = pl.pallas_call(
        functools.partial(project_kernel, count),
        out_shape=(shape_of((rows, width), F32),) * count + (shape_of((rows, width)),) * count,
        in_specs=[VMEM, VMEM],
        out_specs=(VMEM,) * (2 * count),
        compiler_params=params(),
        cost_estimate=cost(2 * left.size * width, left.shape[0] * width * 3),
        name="project",
    )(left, weight)
    return outs[:count], outs[count:]


def project_back_kernel(planes, count, place, left_ref, *refs):
    weights, outs = refs[:planes], refs[planes:]
    rows = left_ref.shape[0] // (2 * count)
    depth = weights[0].shape[0]
    for step in range(count):
        left = left_ref[2 * step * rows : 2 * (step + 1) * rows, :]
        for far in range(planes):
            columns = pl.ds(pl.multiple_of((place[0] ^ far) * depth, 128), depth)
            whole = matmul_nt(left, weights[far][...])
            outs[step][:, columns] = whole[:rows, :]
            outs[count + step][:, columns] = whole[rows:, :].astype(BF16)


def project_back(place, left, weights, count):
    rows, planes = left.shape[0] // (2 * count), len(weights)
    width = weights[0].shape[0] * planes
    outs = pl.pallas_call(
        functools.partial(project_back_kernel, planes, count),
        out_shape=(shape_of((rows, width), F32),) * count + (shape_of((rows, width)),) * count,
        in_specs=[SMEM] + [VMEM] * (1 + planes),
        out_specs=(VMEM,) * (2 * count),
        compiler_params=params(),
        cost_estimate=cost(2 * left.size * width, left.shape[0] * width * 3),
        name="project_back",
    )(place, left, *weights)
    return outs[:count], outs[count:]


def qkv_grad_kernel(place, normed_ref, grad_ref, *outs):
    depth = outs[0].shape[0]
    for far, out in enumerate(outs):
        columns = pl.ds(pl.multiple_of((place[0] ^ far) * depth, 128), depth)
        out[...] = matmul_tn(normed_ref[:, columns], grad_ref[...]).astype(BF16)


def qkv_grad(place, normed, grad, planes):
    depth, width = normed.shape[1] // planes, grad.shape[1]
    return pl.pallas_call(
        qkv_grad_kernel,
        out_shape=(shape_of((depth, width)),) * planes,
        in_specs=[SMEM, VMEM, VMEM],
        out_specs=(VMEM,) * planes,
        compiler_params=params(),
        cost_estimate=cost(2 * normed.size * width, normed.size * 2),
        name="qkv_grad",
    )(place, normed, grad)


def rows_grad_kernel(count, left_ref, *refs):
    grads, out = refs[:-1], refs[-1]
    left = left_ref[...]
    width = out.shape[1]
    block = 512
    for first in range(0, width, block):
        columns = slice(first, first + block)
        right = jnp.concatenate([grad[:, columns] for grad in grads], 0)
        out[:, columns] = matmul_tn(left, right).astype(BF16)


def rows_grad(left, grads):
    return pl.pallas_call(
        functools.partial(rows_grad_kernel, len(grads)),
        out_shape=shape_of((left.shape[1], grads[0].shape[1])),
        in_specs=[VMEM] * (1 + len(grads)),
        out_specs=VMEM,
        compiler_params=params(),
        cost_estimate=cost(2 * left.size * grads[0].shape[1], left.size * 2),
        name="rows_grad",
    )(left, *grads)


def weight_copies(place, planes, sides, gu, sem):
    chips = len(sides)
    rows = gu.shape[1] // (planes * chips)
    copies = []
    for side in range(2):
        for step, pair in enumerate(sides):
            for plane in range(planes):
                to = (plane * chips + (place[1] ^ step)) * rows
                copies.append(
                    pltpu.make_async_copy(
                        pair[side].at[pl.ds(plane * rows, rows), :],
                        gu.at[side, pl.ds(pl.multiple_of(to, 16), rows), :],
                        sem.at[side],
                    )
                )
    return copies


def feed_kernel(planes, layout, count, place, *refs):
    x, refs = refs[:count], refs[count:]
    grads, refs = refs[:count], refs[count:]
    blocks, refs = refs[: len(layout)], refs[len(layout) :]
    chips = 1 + max(step for step, _ in layout)
    sides = [[None, None] for _ in range(chips)]
    for (step, side), ref in zip(layout, blocks):
        for part in (0, 1) if side is None else (side,):
            sides[step][part] = ref.at[part] if side is None else ref
    down_ref, hidden_ref, gate_ref, up_ref = refs[:4]
    outs, refs = refs[4 : 4 + count], refs[4 + count :]
    dxs, refs = refs[:count], refs[count:]
    gu, down, sem = refs
    rows = x[0].shape[0]
    units = down.shape[0]
    copies = weight_copies(place, planes, sides, gu, sem)
    down_copy = pltpu.make_async_copy(down_ref, down, sem.at[2])
    half = len(copies) // 2
    for copy in copies:
        copy.start()
    down_copy.start()
    x = jnp.concatenate([part[...] for part in x], 0)
    grad = jnp.concatenate([part[...] for part in grads], 0)
    for copy in copies[:half]:
        copy.wait()
    gate = matmul(x, gu[0, :, :units])
    for copy in copies[half:]:
        copy.wait()
    up = matmul(x, gu[1, :, :units])
    down_copy.wait()
    dhidden = matmul_nt(grad, down[...])
    sigmoid = 1.0 / (1.0 + jnp.exp(-gate))
    hidden = (gate * sigmoid * up).astype(BF16)
    dgate = (dhidden * up * sigmoid * (1.0 + gate * (1.0 - sigmoid))).astype(BF16)
    dup = (dhidden * gate * sigmoid).astype(BF16)
    hidden_ref[...] = hidden
    gate_ref[...] = dgate
    up_ref[...] = dup
    block = 512
    for first in range(0, x.shape[1], block):
        columns = slice(first, first + block)
        dx = matmul_nt(dgate, gu[0, columns, :units]) + matmul_nt(dup, gu[1, columns, :units])
        for j in range(count):
            dxs[j][:, columns] = dx[j * rows : (j + 1) * rows, :].astype(dxs[j].dtype)
    for first in range(0, x.shape[1], block):
        columns = slice(first, first + block)
        out = matmul(hidden, down[:, columns])
        for j in range(count):
            outs[j][:, columns] = out[j * rows : (j + 1) * rows, :].astype(outs[j].dtype)


def feed(place, planes, x, grad, w_gate_up, w_down):
    layout, blocks = zip(*w_gate_up)
    rows, width = x[0].shape
    units = w_down.shape[0]
    count = len(x)
    part = shape_of((count * rows, units))
    terms = (shape_of((rows, width), F32), shape_of((rows, width))) * (count // 2)
    got = pl.pallas_call(
        functools.partial(feed_kernel, planes, layout, count),
        out_shape=(part,) * 3 + terms * 2,
        in_specs=[SMEM] + [VMEM] * (2 * count) + [ANY] * (len(blocks) + 1),
        out_specs=(VMEM,) * (3 + 2 * count),
        scratch_shapes=[
            pltpu.VMEM((2, width, blocks[0].shape[-1]), BF16),
            pltpu.VMEM((units, width), BF16),
            pltpu.SemaphoreType.DMA((3,)),
        ],
        compiler_params=params(),
        cost_estimate=cost(12 * count * rows * width * units, 6 * width * units, rows * units),
        name="feed",
    )(place, *x, *grad, *blocks, w_down)
    return got[:3], got[3 : 3 + count], got[3 + count :]


def feed_grad_kernel(planes, chips, count, batches, place, *refs):
    x, refs = refs[:count], refs[count:]
    gates, refs = refs[:batches], refs[batches:]
    ups, refs = refs[:batches], refs[batches:]
    outs, (held, sem) = refs[:-2], refs[-2:]
    width = held.shape[1]
    units = gates[0].shape[1]
    block = 256
    rows = width // (planes * chips)
    copies = []
    dgate = jnp.concatenate([gate[...] for gate in gates], 0)
    dup = jnp.concatenate([up[...] for up in ups], 0)
    if held.shape[2] > units:
        held[:, :, units:] = jnp.zeros((2, width, held.shape[2] - units), BF16)
    for plane in range(planes):
        for first in range(plane * chips * rows, (plane + 1) * chips * rows, block):
            columns = slice(first, first + block)
            left = jnp.concatenate([part[:, columns] for part in x], 0)
            held[0, columns, :units] = matmul_tn(left, dgate).astype(BF16)
            held[1, columns, :units] = matmul_tn(left, dup).astype(BF16)
        for step in range(chips):
            at = (plane * chips + (place[1] ^ step)) * rows
            for side in range(2):
                to = outs[0].at[side] if step == 0 else outs[2 * step - 1 + side]
                copy = pltpu.make_async_copy(
                    held.at[side, pl.ds(pl.multiple_of(at, 16), rows), :],
                    to.at[pl.ds(plane * rows, rows), :],
                    sem,
                )
                copy.start()
                copies.append(copy)
    for copy in copies:
        copy.wait()


def feed_grad(place, planes, chips, x, gates, ups, lanes):
    width, units = x[0].shape[1], gates[0].shape[1]
    tokens = x[0].shape[0] * len(x)
    own = shape_of((2, width // chips, lanes))
    part = shape_of((width // chips, lanes))
    outs = (own,) + (part,) * (2 * chips - 2)
    return pl.pallas_call(
        functools.partial(feed_grad_kernel, planes, chips, len(x), len(gates)),
        out_shape=outs,
        in_specs=[SMEM] + [VMEM] * (len(x) + len(gates) + len(ups)),
        out_specs=(ANY,) * len(outs),
        scratch_shapes=[pltpu.VMEM((2, width, lanes), BF16), pltpu.SemaphoreType.DMA],
        compiler_params=params(),
        cost_estimate=cost(4 * tokens * width * units, 4 * width * units),
        name="feed_grad",
    )(place, *x, *gates, *ups)


def feed_adam_kernel(planes, chips, piece, place, gains, *refs):
    blocks, refs = refs[:planes], refs[planes:]
    ins, outs = refs[:6], refs[6:12]
    gain_grad, held = refs[12], refs[13]
    plane, core = place[0], place[2]
    for step in range(planes):
        for side in range(2):
            held[plane ^ step, core ^ side] = blocks[step][side].astype(F32)
    gain = gains[:, 1:2]
    total = jnp.zeros(gain.shape, F32)
    for part in range(2):
        w, m, u = ins[3 * part : 3 * part + 3]
        grad = jnp.concatenate(
            [
                held[far, c, part, :, at * piece : (at + 1) * piece]
                for far in range(planes)
                for at in range(chips)
                for c in range(2)
            ],
            1,
        )
        weight = w[...]
        total = total + jnp.sum(weight.astype(BF16).astype(F32) * grad, -1, keepdims=True)
        updated = adam_step(weight, m[...], u[...], grad * gain, 0.02)
        for out, value in zip(outs[3 * part : 3 * part + 3], updated):
            out[...] = value
    gain_grad[...] = jnp.broadcast_to(total, gain_grad.shape)


def feed_adam(place, planes, chips, gains, blocks, arrays):
    rows, hidden = arrays[0].shape
    piece = hidden // (2 * planes * chips)
    tile = min(rows, 16)
    whole = pl.BlockSpec((tile, hidden), lambda i: (i, 0))
    lanes = blocks[0].shape[-1]
    block = pl.BlockSpec((2, 2, tile, lanes), lambda i: (0, 0, i, 0))
    two = pl.BlockSpec((tile, 2), lambda i: (i, 0))
    *new, gain_grad = pl.pallas_call(
        functools.partial(feed_adam_kernel, planes, chips, piece),
        grid=(rows // tile,),
        out_shape=(shape_of((rows, hidden), F32),) * 6 + (shape_of((rows, 128), F32),),
        in_specs=[SMEM, two] + [block] * planes + [whole] * 6,
        out_specs=(whole,) * 6 + (pl.BlockSpec((tile, 128), lambda i: (i, 0)),),
        scratch_shapes=[pltpu.VMEM((planes, 2, 2, tile, lanes), F32)],
        compiler_params=params(),
        cost_estimate=cost(40 * rows * hidden, 52 * rows * hidden),
        name="feed_adam",
    )(place, gains, *blocks, *arrays)
    return tuple(new), gain_grad[:, 0]


def attention_adam_kernel(heads, place, gains, *refs):
    members = len(heads)
    blocks, refs = refs[: members // 2], refs[members // 2 :]
    ins, refs = refs[:9], refs[9:]
    outs, gain_grad, held = refs[:9], refs[9], refs[10]
    chip, core = place[1], place[2]
    own_q = len(heads[0]) * HEAD_DIM
    sharing = members // KV_HEADS
    for step in range(members // 2):
        for side in range(2):
            held[(chip ^ step) * 2 + (core ^ side)] = blocks[step][side].astype(F32)
    kept = {head: (f, at) for f, own in enumerate(heads) for at, head in enumerate(own)}

    def shared(first):
        return jnp.concatenate(
            [
                sum(
                    held[group * sharing + one, :, first : first + HEAD_DIM]
                    for one in range(sharing)
                )
                for group in range(KV_HEADS)
            ],
            1,
        )

    query = jnp.concatenate(
        [
            held[kept[head][0], :, kept[head][1] * HEAD_DIM : (kept[head][1] + 1) * HEAD_DIM]
            for head in range(HEADS)
        ],
        1,
    )
    gain = gains[:, 0:1]
    total = jnp.zeros(gain.shape, F32)
    for part, grad in enumerate((query, shared(own_q), shared(own_q + HEAD_DIM))):
        w, m, u = ins[3 * part : 3 * part + 3]
        weight = w[...]
        total = total + jnp.sum(weight.astype(BF16).astype(F32) * grad, -1, keepdims=True)
        updated = adam_step(weight, m[...], u[...], grad * gain, 0.02)
        for out, value in zip(outs[3 * part : 3 * part + 3], updated):
            out[...] = value
    gain_grad[...] = jnp.broadcast_to(total, gain_grad.shape)


def attention_adam(place, heads, gains, blocks, arrays):
    rows = arrays[0].shape[0]
    tile = min(rows, 16)
    lanes = blocks[0].shape[-1]
    wholes = [pl.BlockSpec((tile, array.shape[1]), lambda i: (i, 0)) for array in arrays]
    block = pl.BlockSpec((2, tile, lanes), lambda i: (0, i, 0))
    two = pl.BlockSpec((tile, 2), lambda i: (i, 0))
    *new, gain_grad = pl.pallas_call(
        functools.partial(attention_adam_kernel, heads),
        grid=(rows // tile,),
        out_shape=tuple(shape_of(array.shape, F32) for array in arrays)
        + (shape_of((rows, 128), F32),),
        in_specs=[SMEM, two] + [block] * len(blocks) + wholes,
        out_specs=tuple(wholes) + (pl.BlockSpec((tile, 128), lambda i: (i, 0)),),
        scratch_shapes=[pltpu.VMEM((len(heads), tile, lanes), F32)],
        compiler_params=params(),
        cost_estimate=cost(40 * arrays[0].size, 28 * arrays[0].size),
        name="attention_adam",
    )(place, gains, *blocks, *arrays)
    return tuple(new), gain_grad[:, 0]


def segment_starts(lengths_row, length):
    count = lengths_row.shape[0]
    ahead = jnp.arange(count)[:, None] < jnp.arange(count)[None, :]
    starts = jnp.sum(jnp.where(ahead, lengths_row[:, None], 0), 0, dtype=jnp.int32)
    ends = starts + lengths_row
    places = jnp.arange(length, dtype=jnp.int32)
    within = (places[:, None] >= starts[None, :]) & (places[:, None] < ends[None, :])
    return jnp.sum(jnp.where(within, starts[None, :], 0), 1, dtype=jnp.int32)


def rope_tables(positions):
    half = HEAD_DIM // 2
    freqs = jnp.exp(jnp.arange(half, dtype=F32) * (-2.0 * math.log(ROPE_BASE) / HEAD_DIM))
    angles = positions.astype(F32)[:, None] * freqs[None, :]
    cosine = jnp.cos(angles)
    sine = jnp.sin(angles)
    return (
        jnp.concatenate([cosine] * 4, 1),
        jnp.concatenate([-sine, sine, -sine, sine], 1),
    )


def local(
    tokens,
    out_grad,
    seq_lengths,
    query_weight,
    query_first,
    query_second,
    key_weight,
    key_first,
    key_second,
    value_weight,
    value_first,
    value_second,
    output_weight,
    output_first,
    output_second,
    gate_weight,
    gate_first,
    gate_second,
    up_weight,
    up_first,
    up_second,
    down_weight,
    down_first,
    down_second,
    norm_gains,
    gains_first,
    gains_second,
):
    planes = lax.axis_size("dp")
    members = lax.axis_size("fsdp")
    chips = members // 2
    plane = lax.axis_index("dp")
    index = lax.axis_index("fsdp")
    chip = index // 2
    core = index % 2
    place = jnp.stack([plane, chip, core]).astype(jnp.int32)
    spot = jnp.stack([plane, index]).astype(jnp.int32)
    count, width = tokens.shape
    length = count * members
    slice_rows = query_weight.shape[0]
    own_q = query_weight.shape[1] // members
    sharing = members // KV_HEADS
    same_core = [list(range(c, members, 2)) for c in range(2)]

    stages = planes.bit_length() - 1
    chip_stages = chips.bit_length() - 1
    everyone = range(planes)
    heads = head_order(planes, members)
    head_rows = HEADS == planes * members and planes == chips

    def both_cores(blocks):
        return [b for block in blocks for b in (block, core_swap(block))]

    def over_cores(terms):
        return terms[0] + core_swap(terms[1]).astype(F32)

    gains = norm_gains.astype(BF16).astype(F32)
    gain_columns = gains.T
    gu_mine, gu_other, qkv_mine, qkv_other = pack(
        place,
        planes,
        chips,
        gain_columns,
        gate_weight,
        up_weight,
        query_weight,
        key_weight,
        value_weight,
    )
    w_down = lax.all_gather(
        down_weight.astype(BF16), "fsdp", axis=0, tiled=True, axis_index_groups=same_core
    )
    start = segment_starts(seq_lengths[0], length)
    starts = (start[:, None], start[None, :])
    gu_mine, gu_other, qkv_mine, qkv_other, starts, place, spot, output_rows = together(
        gu_mine, gu_other, qkv_mine, qkv_other, starts, place, spot, output_weight.astype(BF16)
    )

    qkv_pairs = swap_pairs(qkv_mine, qkv_other)
    gu_pairs = swap_pairs(gu_mine, gu_other)
    qkv_got = exchange(qkv_pairs, chip_send)
    gu_near = plane_send(gu_pairs[1], 1)
    out_rows = gather_stage({0: output_rows}, plane_send, planes, 1)
    qkv_got, gu_pairs, gu_near, tokens, out_rows = together(
        qkv_got, gu_pairs, gu_near, tokens, out_rows
    )

    gu_got = [gu_pairs[0], gu_near] + [
        plane_send(gu_pairs[step], step) for step in range(2, planes)
    ]
    token_blocks = gather(tokens, chip_send, chips)
    cosine, sine = rope_tables(jnp.arange(length, dtype=jnp.int32) - start)
    gu_got, qkv_got, token_blocks, cosine, sine, w_down, out_rows = together(
        gu_got, qkv_got, token_blocks, cosine, sine, w_down, out_rows
    )

    tokens_mine = jnp.stack(token_blocks)
    tokens_other = core_swap(tokens_mine)
    gu_rows = gather_rows(plane, core, gu_got)
    qkv_rows = gather_rows(chip, core, qkv_got)
    steps = [step for step in range(chips) if ones(step) <= 1]
    w_gate_up = [gu_rows] + [chip_send(gu_rows, step) for step in steps[1:]]
    w_qkv = gather_stage({0: qkv_rows}, plane_send, planes, 1)
    w_qkv, out_rows = together(w_qkv, out_rows)
    for stage in range(2, stages + 1):
        w_qkv = gather_stage(w_qkv, plane_send, planes, stage)
    w_qkv = [w_qkv[far] for far in everyone]
    for stage in range(2, stages + 1):
        out_rows = gather_stage(out_rows, plane_send, planes, stage)
    out_rows = jnp.stack([out_rows[far] for far in everyone])
    w_gate_up, w_qkv, out_grad, tokens_mine, tokens_other, out_rows = together(
        w_gate_up, w_qkv, out_grad, tokens_mine, tokens_other, out_rows
    )

    gate_up = {step: (block[0], block[1]) for step, block in zip(steps, w_gate_up)}
    for stage in range(2, chip_stages + 1):
        for step in range(1, chips):
            if ones(step) == stage:
                top = 1 << (step.bit_length() - 1)
                gate_up[step] = (
                    chip_send(gate_up[step & (step - 1)][0], step & -step),
                    chip_send(gate_up[step ^ top][1], top),
                )
    more = [step for step in range(chips) if ones(step) > 1]
    layout = [(step, None) for step in steps] + [(step, side) for step in more for side in range(2)]
    w_gate_up = w_gate_up + [gate_up[step][side] for step in more for side in range(2)]
    normed, queries, keys_values, attended = attend(
        spot, tokens_mine, tokens_other, w_qkv, starts[0], cosine, sine
    )
    hop = members // planes
    own_plane = index // hop

    def out_route(turn_no):
        return [(i, ((turn_no + i) % planes) * hop + i // planes) for i in range(members)]

    if head_rows:
        out_got = [
            lax.dynamic_index_in_dim(out_rows, (chip ^ step) ^ plane, 0, keepdims=False)
            for step in range(chips)
        ]
        w_output = [out_got[0]] + [chip_send(out_got[step], step) for step in range(1, chips)]
    else:
        w_output = jnp.zeros((planes, slice_rows, width), BF16)
        for turn_no in range(planes):
            sent = lax.dynamic_index_in_dim(
                out_rows, ((turn_no + index) % planes) ^ plane, 0, keepdims=False
            )
            got = lax.ppermute(sent, "fsdp", out_route(turn_no))
            spare = (own_plane + planes - turn_no) % planes
            w_output = lax.dynamic_update_index_in_dim(w_output, got, spare, 0)
        w_output = [w_output.reshape(planes * slice_rows, width)]
    w_gate_up, attended, w_output, out_grad = together(w_gate_up, attended, w_output, out_grad)

    w_gate_up = list(zip(layout, w_gate_up))
    w_output = jnp.concatenate(w_output)
    out_grad_blocks = gather_stage({0: out_grad}, plane_send, planes, 1)
    own_tokens = tokens.astype(F32)
    mixed = [over_cores(terms) for terms in zip(*project(attended, w_output, chips))]
    mixed = mixed[:1] + [
        chip_send(mixed[step].astype(BF16), step).astype(F32) for step in range(1, chips)
    ]
    resid = own_tokens + sum(mixed[1:], mixed[0])
    resid, out_grad_blocks = together(resid, out_grad_blocks)

    scale_two = rms_scale(resid)
    own_normed_two = (resid * scale_two).astype(BF16)
    normed_blocks = gather_stage({0: own_normed_two}, plane_send, planes, 1)
    out_grad_pairs = {far: [block, core_swap(block)] for far, block in out_grad_blocks.items()}
    normed_blocks, out_grad_pairs, out_grad_blocks = together(
        normed_blocks, out_grad_pairs, out_grad_blocks
    )

    x = {far: [block, core_swap(block)] for far, block in normed_blocks.items()}
    x, out_grad_pairs = together(x, out_grad_pairs)
    fed = []
    fed_order = []
    sums = {}
    result = {}
    last = []
    sent = []
    for stage in range(1, stages + 1):
        batch = [far for far in reversed(everyone) if ones(far) == stage]
        if stage == stages:
            batch.append(0)
        fed_order += batch
        parts, outs, dxs = feed(
            place,
            planes,
            [part for far in batch for part in x[far]],
            [part for far in batch for part in out_grad_pairs[far]],
            w_gate_up,
            w_down,
        )
        last += [plane_send(sums[far].astype(BF16), far) for far in sent]
        more = gather_stage(normed_blocks, plane_send, planes, stage + 1)
        more_grad = gather_stage(out_grad_blocks, plane_send, planes, stage + 1)
        parts, outs, dxs, last, normed_blocks, out_grad_blocks = together(
            parts, outs, dxs, last, more, more_grad
        )
        fed.append(parts)
        for blocks, pairs in ((normed_blocks, x), (out_grad_blocks, out_grad_pairs)):
            for far, block in blocks.items():
                if far not in pairs:
                    pairs[far] = [block, core_swap(block)]
        for at, far in enumerate(batch):
            sums[far] = over_cores(dxs[2 * at : 2 * at + 2])
            result[far] = over_cores(outs[2 * at : 2 * at + 2])
        x, sums, out_grad_pairs = together(x, sums, out_grad_pairs)
        sent = [far for far in batch if far]
    last += [plane_send(sums[far].astype(BF16), far) for far in sent]
    hidden, grad_gate, grad_up = zip(*fed)
    lanes = w_gate_up[0][1].shape[-1]
    fed_x = [part for far in fed_order for part in x[far]]
    fed_grad = [part for far in fed_order for part in out_grad_pairs[far]]
    grads = feed_grad(place, planes, chips, fed_x, grad_gate, grad_up, lanes)
    grad_normed_two, last, grads, result = together(sums[0], last, grads, result)
    grad_normed_two = sum([part.astype(F32) for part in last], grad_normed_two)

    grad_resid = (
        out_grad.astype(F32)
        + scale_two * grad_normed_two
        - resid
        * (scale_two * scale_two * scale_two)
        * jnp.mean(grad_normed_two * resid, -1, keepdims=True)
    )
    own_grad = grad_resid.astype(BF16)
    own_grad, result, hidden = together(own_grad, result, hidden)

    grad_blocks = gather(own_grad, chip_send, chips)
    for stage in range(stages, 1, -1):
        result = scatter_stage(result, plane_send, stage)
    grad_down = rows_grad(jnp.concatenate(hidden), fed_grad)
    grad_blocks, result, grad_down = together(grad_blocks, result, grad_down)

    grad_attn_out = both_cores(grad_blocks)
    grad_attn_out, grads, result = together(grad_attn_out, grads, result)

    result = scatter_stage(result, plane_send, 1)[0]
    grad_gate_up = {step: grads[2 * step - 1 : 2 * step + 1] for step in range(1, chips)}

    def plus(one, two):
        return (one.astype(F32) + two.astype(F32)).astype(BF16)

    for stage in range(chip_stages, 1, -1):
        for step in range(chips - 1, 0, -1):
            if ones(step) == stage:
                top = 1 << (step.bit_length() - 1)
                low = step & (step - 1)
                gate, up = grad_gate_up.pop(step)
                gate, up = chip_send(gate, step & -step), chip_send(up, top)
                grad_gate_up[low] = (plus(grad_gate_up[low][0], gate), grad_gate_up[low][1])
                low = step ^ top
                grad_gate_up[low] = (grad_gate_up[low][0], plus(grad_gate_up[low][1], up))
    grad_gate_up = {step: jnp.stack(pair) for step, pair in grad_gate_up.items()}
    grad_qkv = attend_back(
        spot, queries, keys_values, w_output, grad_attn_out, starts[1], cosine, sine
    )
    grad_qkv, result, grad_gate_up, grad_attn_out = together(
        grad_qkv, result, grad_gate_up, grad_attn_out
    )
    result = (resid + result).astype(BF16)

    grad_gate_up = [grads[0]] + [chip_send(part, step) for step, part in grad_gate_up.items()]
    grad_w_qkv = dict(enumerate(qkv_grad(spot, normed, grad_qkv, planes)))
    for stage in range(stages, 0, -1):
        grad_w_qkv = scatter_stage(grad_w_qkv, plane_send, stage)
    mixed = project_back(spot, grad_qkv, w_qkv, chips)
    grad_output = rows_grad(attended, grad_attn_out).reshape(planes, slice_rows, width)
    grad_gate_up, grad_w_qkv, mixed, grad_output, grad_down = together(
        grad_gate_up, grad_w_qkv[0], mixed, grad_output, grad_down
    )

    grad_down_weight = lax.psum_scatter(
        grad_down, "fsdp", scatter_dimension=0, tiled=True, axis_index_groups=same_core
    ).astype(F32)

    qkv_pairs = swap_pairs(*spread_rows(chip, core, [grad_w_qkv], chips))
    gu_mine, gu_other = spread_rows(plane, core, grad_gate_up, planes)
    gu_other = core_swap(gu_other)
    got = exchange(qkv_pairs, chip_send)
    gu_mine, gu_other, got, mixed, grad_output = together(
        gu_mine, gu_other, got, mixed, grad_output
    )

    gu_pairs = [jnp.stack([gu_mine[step], gu_other[step]]) for step in everyone]
    far_pairs = gu_pairs[planes // 2 + 1 :]
    near_got = exchange(gu_pairs[: planes // 2 + 1], plane_send)
    if head_rows:
        parts = [grad_output[0]] + [chip_send(grad_output[step], step) for step in range(1, chips)]
        parts = jnp.stack(parts)
        out_parts = [
            lax.dynamic_index_in_dim(parts, (plane ^ far) ^ chip, 0, keepdims=False)
            for far in everyone
        ]
    else:
        parts = jnp.zeros((planes, slice_rows, width), BF16)
        for turn_no in range(planes):
            spare = (own_plane + planes - turn_no) % planes
            sent = lax.dynamic_index_in_dim(grad_output, spare, 0, keepdims=False)
            part = lax.ppermute(sent, "fsdp", [(b, a) for a, b in out_route(turn_no)])
            parts = lax.dynamic_update_index_in_dim(
                parts, part, ((turn_no + index) % planes) ^ plane, 0
            )
        out_parts = [parts[far] for far in everyone]
    attention_new, grad_gain_one = attention_adam(
        place,
        heads,
        gain_columns,
        got,
        (
            query_weight,
            query_first,
            query_second,
            key_weight,
            key_first,
            key_second,
            value_weight,
            value_first,
            value_second,
        ),
    )
    far_pairs, near_got, out_parts, mixed, grad_gain_one = together(
        far_pairs, near_got, out_parts, mixed, grad_gain_one
    )

    far_got = [
        plane_send(pair, planes // 2 + 1 + step) for step, pair in enumerate(far_pairs)
    ]
    grad_gate_up = near_got + far_got
    out_parts = dict(enumerate(out_parts))
    for stage in range(stages, 1, -1):
        out_parts = scatter_stage(out_parts, plane_send, stage)
    mixed = {step: over_cores(terms) for step, terms in enumerate(zip(*mixed))}
    for stage in range(chip_stages, 1, -1):
        mixed = scatter_stage(mixed, chip_send, stage)
    down_new = adam_step(down_weight, down_first, down_second, grad_down_weight, 0.02)
    grad_gate_up, out_parts, mixed, down_new = together(grad_gate_up, out_parts, mixed, down_new)

    grad_normed = scatter_stage(mixed, chip_send, 1)[0]
    grad_output_weight = scatter_stage(out_parts, plane_send, 1)[0]
    scale_one = rms_scale(own_tokens)
    grad_tokens = (
        grad_resid
        + scale_one * grad_normed
        - own_tokens
        * (scale_one * scale_one * scale_one)
        * jnp.mean(grad_normed * own_tokens, -1, keepdims=True)
    )
    fed_weights, grad_gain_two = feed_adam(
        place,
        planes,
        chips,
        gain_columns,
        grad_gate_up,
        (gate_weight, gate_first, gate_second, up_weight, up_first, up_second),
    )
    gain_grads = jnp.stack([grad_gain_one, grad_gain_two])
    updated = (
        attention_new
        + adam_step(output_weight, output_first, output_second, grad_output_weight, 0.1)
        + fed_weights
        + tuple(down_new)
        + adam_step(norm_gains, gains_first, gains_second, gain_grads, 0.2)
    )
    return (result, grad_tokens) + updated


def solution(mesh):
    rows = P(("dp", "fsdp"), None)
    columns = P(None, ("dp", "fsdp"))
    in_specs = (rows, rows, P("dp", None)) + (rows,) * 21 + (columns,) * 3
    out_specs = (rows, rows) + (rows,) * 21 + (columns,) * 3
    return jax.shard_map(local, mesh=mesh, in_specs=in_specs, out_specs=out_specs, check_vma=False)
```
